512 devices in a mesh: leaf: 64 (over x, z), blk: 8 (over y, core).
Axes of the slice: x: 4, y: 4, z: 16, core: 2. Of those that a mesh axis runs over, the one named last changes fastest.
Arguments:
- leaf_inverse: bfloat16 [64, 1024, 1024], P('leaf', 'blk'), as said below
- leaf_coupling: bfloat16 [64, 6, 1024, 1024], P('leaf', None, None, 'blk'), as said below
- sep_inverse: bfloat16 [64, 1024, 1024], P('leaf', 'blk'), as said below
- sep_coupling: bfloat16 [64, 6, 1024, 1024], P('leaf', None, None, 'blk'), as said below
- leaf_right: bfloat16 [64, 64, 1024], P('leaf', None, 'blk'), may hold values from -6 to 6
- sep_right: bfloat16 [64, 64, 1024], P('leaf', None, 'blk'), may hold values from -6 to 6
- pattern: int32 [64, 6], P('leaf'), may hold values 0 or 1
Outputs:
- leaf_sol: float32 [64, 64, 1024], P('leaf', None, 'blk')
- sep_sol: float32 [64, 64, 1024], P('leaf', None, 'blk')
The draws below stay inside these ranges and needn't reach their ends.
Inputs may be any that keep to these rules, and one draw needn't show every extreme that they name: `leaf_inverse`: inverses of the leaves' diagonal blocks. `leaf_coupling`: off-diagonal factor blocks of the leaves. `sep_inverse`: inverses of the separators' diagonal blocks. `sep_coupling`: off-diagonal factor blocks of the separators.
All inputs are finite; a program needn't handle non-finite values. No bound on the sum of `pattern` on one device may be relied on, other than what follows from the above.
Results may differ from the reference program's by a relative error of at most 0.02.
Values may be sent and summed in bfloat16 or wider, within the bound.
A program may use at most 64 MiB of HBM per device.

```python
import math
import jax
import jax.numpy as jnp
from jax import lax

S = 1024
P_SIZE = 1024
R = 64
LEAVES = 64
LEV = 6


def inverse_block(key, count, order):
    first_key = jax.random.fold_in(key, 0)
    noise_part = jax.random.truncated_normal(first_key, -4.0, 4.0, (count, order, order), jnp.float32)
    return (jnp.eye(order, dtype=jnp.float32) + 0.3 * noise_part / math.sqrt(order)).astype(jnp.bfloat16)


def coupling_block(key, count, rows_out, cols_in):
    first_key = jax.random.fold_in(key, 0)
    noise_part = jax.random.truncated_normal(first_key, -4.0, 4.0, (count, LEV, rows_out, cols_in), jnp.float32)
    level_scale = jnp.exp2(-0.5 * (jnp.arange(LEV).astype(jnp.float32) + 1.0)) / math.sqrt(cols_in)
    return (noise_part * level_scale[None, :, None, None]).astype(jnp.bfloat16)


def draw_leaf_inverse(key, part):
    return inverse_block(jax.random.fold_in(key, 11), LEAVES, S)


def draw_sep_inverse(key, part):
    return inverse_block(jax.random.fold_in(key, 12), LEAVES, P_SIZE)


def draw_leaf_coupling(key, part):
    return coupling_block(jax.random.fold_in(key, 13), LEAVES, P_SIZE, S)


def draw_sep_coupling(key, part):
    return coupling_block(jax.random.fold_in(key, 14), LEAVES, P_SIZE, P_SIZE)


def place_ends(array, stream_key, smallest, top_value):
    shape = array.shape
    index_at = [jax.random.randint(jax.random.fold_in(stream_key, axis), (), 0, shape[axis]) for axis in range(len(shape))]
    array = array.at[tuple(index_at)].set(smallest)
    longest = shape.index(max(shape))
    index_at[longest] = (index_at[longest] + 1) % shape[longest]
    return array.at[tuple(index_at)].set(top_value)


def block_scale(stream_key, extent, shards, low, high):
    gain = 1.0
    for position, blocks in shards:
        steps = jax.random.uniform(jax.random.fold_in(jax.random.fold_in(stream_key, 6), position), (blocks,), jnp.float32, low / len(shards), high / len(shards))
        gain = gain * jnp.repeat(jnp.exp(steps), extent[position] // blocks).reshape((-1,) + (1,) * (len(extent) - 1 - position))
    return gain


def scatter_about(rng, extent, scale, most, cuts=(), held_as=jnp.bfloat16):
    array = scale * jax.random.normal(rng, extent, jnp.float32)
    if cuts:
        array = array * block_scale(rng, extent, cuts, -0.22, 0.18)
    return jnp.clip(array, -most, most).astype(held_as)


def setup_inputs(seed: int = 0) -> dict:
    key_of = jax.random.split(jax.random.key(seed), 8)
    leaf_inverse = draw_leaf_inverse(jax.random.fold_in(key_of[7], 71), 0)
    leaf_coupling = draw_leaf_coupling(jax.random.fold_in(key_of[7], 71), 0)
    sep_inverse = draw_sep_inverse(jax.random.fold_in(key_of[7], 71), 0)
    sep_coupling = draw_sep_coupling(jax.random.fold_in(key_of[7], 71), 0)
    leaf_right = scatter_about(key_of[4], (LEAVES, R, S), 1.0, 6.0, ((0, 64), (2, 8)))
    sep_right = scatter_about(key_of[5], (LEAVES, R, P_SIZE), 1.0, 6.0, ((0, 64), (2, 8)))
    pattern = place_ends((jax.random.randint(key_of[6], (LEAVES, LEV), 0, 4) < 3).astype(jnp.int32), jax.random.fold_in(key_of[6], 1), 0, 1)
    return {"leaf_inverse": leaf_inverse, "leaf_coupling": leaf_coupling, "sep_inverse": sep_inverse, "sep_coupling": sep_coupling, "leaf_right": leaf_right, "sep_right": sep_right, "pattern": pattern}


def rounded(values):
    return lax.optimization_barrier(values.astype(jnp.bfloat16)).astype(jnp.float32)


def reference(leaf_inverse, leaf_coupling, sep_inverse, sep_coupling, leaf_right, sep_right, pattern):
    mask_f = pattern.astype(jnp.float32)

    def leaf_forward(inputs):
        inverse_blk, coupling_blk, right_blk, mask_row = inputs
        solved = jnp.dot(right_blk, inverse_blk.T, preferred_element_type=jnp.float32)
        terms = jnp.einsum("rs,lps->lrp", rounded(solved), coupling_blk.astype(jnp.float32))
        return solved, terms * mask_row[:, None, None]

    leaf_y, leaf_terms = lax.map(leaf_forward, (leaf_inverse, leaf_coupling, leaf_right, mask_f))
    sep_y = jnp.zeros((LEAVES, R, P_SIZE), jnp.float32)
    sep_terms = jnp.zeros((LEAVES, LEV, R, P_SIZE), jnp.float32)
    for height in range(1, LEV + 1):
        span_size = 2 ** height
        groups = LEAVES // span_size
        owners = (jnp.arange(groups) * span_size + span_size // 2 - 1).astype(jnp.int32)
        grand = (leaf_terms[:, height - 1] + sep_terms[:, height - 1]).reshape(groups, span_size, R, P_SIZE).sum(axis=1)
        residue = sep_right[owners].astype(jnp.float32) - grand
        later = (jnp.arange(LEV) >= height).astype(jnp.float32)

        def sep_forward(inputs, later=later):
            owner_id, residue_blk = inputs
            solved = jnp.dot(residue_blk.astype(jnp.bfloat16), sep_inverse[owner_id].T, preferred_element_type=jnp.float32)
            spread = jnp.einsum("rq,lpq->lrp", rounded(solved), sep_coupling[owner_id].astype(jnp.float32))
            return solved, spread * later[:, None, None]

        solved_all, spread_all = lax.map(sep_forward, (owners, residue))
        sep_y = sep_y.at[owners].set(solved_all)
        sep_terms = sep_terms.at[owners].add(spread_all)
    ancestor = {}
    sep_sol = jnp.zeros((LEAVES, R, P_SIZE), jnp.float32)
    for height in range(LEV, 0, -1):
        span_size = 2 ** height
        groups = LEAVES // span_size
        owners = (jnp.arange(groups) * span_size + span_size // 2 - 1).astype(jnp.int32)

        def sep_backward(owner_id, height=height):
            rows_in = sep_y[owner_id]
            for upper in range(height + 1, LEV + 1):
                rows_in = rows_in - jnp.dot(ancestor[upper][owner_id], sep_coupling[owner_id, upper - 1], preferred_element_type=jnp.float32)
            return jnp.dot(rows_in.astype(jnp.bfloat16), sep_inverse[owner_id], preferred_element_type=jnp.float32)

        solved_all = lax.map(sep_backward, owners)
        sep_sol = sep_sol.at[owners].set(solved_all)
        ancestor[height] = jnp.repeat(solved_all.astype(jnp.bfloat16), span_size, axis=0)

    def leaf_backward(leaf_id):
        rows_in = leaf_y[leaf_id]
        for upper in range(1, LEV + 1):
            rows_in = rows_in - mask_f[leaf_id, upper - 1] * jnp.dot(ancestor[upper][leaf_id], leaf_coupling[leaf_id, upper - 1], preferred_element_type=jnp.float32)
        return jnp.dot(rows_in.astype(jnp.bfloat16), leaf_inverse[leaf_id], preferred_element_type=jnp.float32)

    leaf_sol = lax.map(leaf_backward, jnp.arange(LEAVES).astype(jnp.int32))
    return leaf_sol, sep_sol
```

```python
import jax
import jax.numpy as jnp
from jax import lax
from jax.experimental import pallas as pl
from jax.experimental.pallas import tpu as pltpu
from jax.sharding import PartitionSpec as P

MESH = pl.DeviceIdType.MESH
F32 = jnp.float32
BF16 = jnp.bfloat16
NB = 8
LEV = 6


def tree_place(i):
    lev, half, run = 1, 1, 1
    for n in range(LEV):
        run = run * ((i // 2**n) % 2)
        lev = lev + run
        half = half + run * 2**n
    return lev, half


def dot_t(a, b):
    return lax.dot_general(a, b, (((1,), (1,)), ((), ())), preferred_element_type=F32)


def kernel(li, lc, si, sc, lr_in, sr_in, pat, lsol, ssol,
           LR, LY, T1, TL, RSL, U, UO1, UO2, UX, RX, SR, SY, TC, TN, RSS, XF, PB, RSB, LB, RLB, SA, LA,
           s_lr, r_lr, s_t1, s_tl, r_tl, s_u1, s_u2, r_ux, r_rx, s_sr, r_sr, s_tc, s_tn, r_tn,
           s_xf, s_xo, r_xf, s_pb, r_pb, s_lb, r_lb):
    i = lax.axis_index("leaf")
    b = lax.axis_index("blk")
    lev, half = tree_place(i)
    odd = i % 2
    even_slot = i - odd
    pair_slot = i + 1 - 2 * odd
    pb = (i // (2 * half)) % 2
    parent = i + half - 2 * half * pb
    kid0 = i - half // 2
    kid1 = i + half // 2
    lev_next, _ = tree_place(i + 1)
    owner = lev <= LEV

    def send(src, dst, ssem, rsem, leaf, blk):
        pltpu.make_async_remote_copy(src_ref=src, dst_ref=dst, send_sem=ssem, recv_sem=rsem,
                                     device_id=(leaf, blk), device_id_type=MESH).start()

    def drain(ref, sem):
        pltpu.make_async_copy(ref, ref, sem).wait()

    def others(fn):
        def step(d, c):
            fn(d, (b + d) % NB)
            return c
        lax.fori_loop(1, NB, step, 0)

    def all_blk(fn):
        def step(d, c):
            fn((b + d) % NB)
            return c
        lax.fori_loop(0, NB, step, 0)

    def full(ref):
        return jnp.concatenate([ref[c] for c in range(NB)], axis=1)

    def spread(ref, value):
        for c in range(NB):
            ref[c] = value[:, c * 128:(c + 1) * 128].astype(BF16)

    def sum7(ref):
        total = ref[0].astype(F32)
        for d in range(1, NB - 1):
            total = total + ref[d].astype(F32)
        return total

    barrier = pltpu.get_barrier_semaphore()

    def greet(leaf, blk):
        pl.semaphore_signal(barrier, inc=1, device_id=(leaf, blk), device_id_type=MESH)

    pair_is_kin = (lev == 2) | ((lev == 1) & (pb == 0))
    others(lambda d, t: greet(i, t))

    @pl.when(~pair_is_kin)
    def _():
        all_blk(lambda t: greet(pair_slot, t))

    @pl.when(lev < LEV)
    def _():
        all_blk(lambda t: greet(parent, t))

    @pl.when((lev >= 2) & owner)
    def _():
        all_blk(lambda t: greet(kid0, t))
        all_blk(lambda t: greet(kid1, t))

    peers = (7 + jnp.where(pair_is_kin, 0, 8) + jnp.where(lev < LEV, 8, 0)
             + jnp.where((lev >= 2) & owner, 16, 0))
    pl.semaphore_wait(barrier, peers)

    LR[b] = lr_in[0]
    others(lambda d, t: send(LR.at[b], LR.at[b], s_lr, r_lr, i, t))
    drain(LR.at[pl.ds(0, 7)], r_lr)
    ly = dot_t(full(LR), li[0])
    LY[...] = ly
    LA[...] = ly
    lyb = ly.astype(BF16)

    spread(T1, dot_t(lyb, lc[0, 0]) * pat[0, 0].astype(F32))

    @pl.when(odd == 1)
    def _():
        all_blk(lambda t: send(T1.at[t], RX.at[NB + b], s_t1, r_rx, even_slot, t))

    @pl.when(odd == 0)
    def _():
        RX[b] = T1[b]
        others(lambda d, t: send(T1.at[t], RX.at[b], s_t1, r_rx, i, t))

    for a in range(2, LEV + 1):
        n = a - 2
        spread(TL.at[n], dot_t(lyb, lc[0, a - 1]) * pat[0, a - 1].astype(F32))
        others(lambda d, t, n=n: send(TL.at[n, t], RSL.at[n, d - 1], s_tl.at[n], r_tl.at[n], i, t))

    for a in range(2, LEV + 1):
        n = a - 2
        drain(RSL.at[n], r_tl.at[n])
        total = TL[n, b].astype(F32) + sum7(RSL.at[n])

        @pl.when(odd == 1)
        def _(n=n, total=total):
            UO1[n] = total.astype(BF16)
            send(UO1.at[n], UX.at[n, 1], s_u1.at[n], r_ux.at[n], even_slot, b)
            U[n] = jnp.zeros((64, 128), F32)

        @pl.when(odd == 0)
        def _(n=n, total=total):
            U[n] = total
            UX[n, 0] = jnp.zeros((64, 128), BF16)

    def upward(n):
        @pl.when(lev == 1)
        def _():
            drain(UX.at[n, 1], r_ux.at[n])

        @pl.when(lev != 1)
        def _():
            drain(UX.at[n], r_ux.at[n])

        return U[n] + UX[n, 0].astype(F32) + UX[n, 1].astype(F32)

    @pl.when(owner)
    def _():
        @pl.when(lev == 1)
        def _():
            drain(RX.at[pl.ds(0, 15)], r_rx)

        @pl.when(lev != 1)
        def _():
            drain(RX, r_rx)

        rs = sr_in[0].astype(F32)
        for c in range(2 * NB):
            rs = rs - RX[c].astype(F32)
        SR[b] = rs.astype(BF16)
        others(lambda d, t: send(SR.at[b], SR.at[b], s_sr, r_sr, i, t))
        drain(SR.at[pl.ds(0, 7)], r_sr)
        sy = dot_t(full(SR), si[0])
        SA[...] = sy
        syb = sy.astype(BF16)

        for a in range(2, LEV + 1):
            n = a - 2

            @pl.when(lev == a - 1)
            def _(a=a, n=n):
                spread(TC, dot_t(syb, sc[0, a - 1]))
                others(lambda d, t: send(TC.at[t], RX.at[pb * NB + b], s_tc, r_rx, parent, t))
                TC[b] = (TC[b].astype(F32) + upward(n)).astype(BF16)
                send(TC.at[b], RX.at[pb * NB + b], s_tc, r_rx, parent, b)

            if a > 2:
                @pl.when(lev < a - 1)
                def _(a=a, n=n):
                    spread(TN.at[a - 3], dot_t(syb, sc[0, a - 1]))
                    others(lambda d, t: send(TN.at[a - 3, t], RSS.at[a - 3, d - 1], s_tn.at[a - 3], r_tn.at[a - 3], i, t))

        for a in range(3, LEV + 1):
            n = a - 2

            @pl.when(lev < a - 1)
            def _(a=a, n=n):
                drain(RSS.at[a - 3], r_tn.at[a - 3])
                UO2[n] = (TN[a - 3, b].astype(F32) + sum7(RSS.at[a - 3]) + upward(n)).astype(BF16)
                send(UO2.at[n], UX.at[n, pb], s_u2.at[n], r_ux.at[n], parent, b)

    def leaf_part(a):
        LA[...] = LA[...] - pat[0, a - 1].astype(F32) * jnp.dot(full(XF.at[a - 1]), lc[0, a - 1], preferred_element_type=F32)

    for a in range(LEV, 1, -1):
        @pl.when(lev < a)
        def _(a=a):
            drain(XF.at[a - 1], r_xf.at[a - 1])

            @pl.when(lev >= 2)
            def _():
                all_blk(lambda t: send(XF.at[a - 1, b], XF.at[a - 1, b], s_xf.at[a - 1], r_xf.at[a - 1], kid0, t))
                all_blk(lambda t: send(XF.at[a - 1, b], XF.at[a - 1, b], s_xf.at[a - 1], r_xf.at[a - 1], kid1, t))

            @pl.when((lev == 1) & (a < lev_next))
            def _():
                all_blk(lambda t: send(XF.at[a - 1, b], XF.at[a - 1, b], s_xf.at[a - 1], r_xf.at[a - 1], pair_slot, t))

            SA[...] = SA[...] - jnp.dot(full(XF.at[a - 1]), sc[0, a - 1], preferred_element_type=F32)
            leaf_part(a)

    @pl.when(owner)
    def _():
        spread(PB, jnp.dot(SA[...].astype(BF16), si[0], preferred_element_type=F32))
        others(lambda d, t: send(PB.at[t], RSB.at[d - 1], s_pb, r_pb, i, t))
        drain(RSB, r_pb)
        x = PB[b].astype(F32) + sum7(RSB)
        ssol[0] = x
        own = lev - 1
        XF[own, b] = x.astype(BF16)

        @pl.when(lev >= 2)
        def _():
            all_blk(lambda t: send(XF.at[own, b], XF.at[own, b], s_xo, r_xf.at[own], kid0, t))
            all_blk(lambda t: send(XF.at[own, b], XF.at[own, b], s_xo, r_xf.at[own], kid1, t))

        @pl.when(lev == 1)
        def _():
            all_blk(lambda t: send(XF.at[own, b], XF.at[own, b], s_xo, r_xf.at[own], pair_slot, t))

        others(lambda d, t: send(XF.at[own, b], XF.at[own, b], s_pb, r_xf.at[own], i, t))
        drain(XF.at[own, pl.ds(0, 7)], r_xf.at[own])
        leaf_part(lev)

    @pl.when(lev > LEV)
    def _():
        ssol[0] = jnp.zeros((64, 128), F32)

    for a in range(LEV, 0, -1):
        @pl.when(a < lev)
        def _(a=a):
            drain(XF.at[a - 1], r_xf.at[a - 1])
            leaf_part(a)

    spread(LB, jnp.dot(LA[...].astype(BF16), li[0], preferred_element_type=F32))
    others(lambda d, t: send(LB.at[t], RLB.at[d - 1], s_lb, r_lb, i, t))
    drain(RLB, r_lb)
    lsol[0] = LB[b].astype(F32) + sum7(RLB)

    drain(LR.at[pl.ds(0, 7)], s_lr)

    @pl.when(odd == 1)
    def _():
        drain(T1, s_t1)
        for n in range(LEV - 1):
            drain(UO1.at[n], s_u1.at[n])

    @pl.when(odd == 0)
    def _():
        drain(T1.at[pl.ds(0, 7)], s_t1)

    for n in range(LEV - 1):
        drain(TL.at[n, pl.ds(0, 7)], s_tl.at[n])
    drain(LB.at[pl.ds(0, 7)], s_lb)

    @pl.when(owner)
    def _():
        drain(SR.at[pl.ds(0, 7)], s_sr)
        drain(RX.at[pl.ds(0, 14)], s_pb)

        @pl.when(lev >= 2)
        def _():
            drain(RX, s_xo)

        @pl.when(lev == 1)
        def _():
            drain(PB, s_xo)

        @pl.when(lev < LEV)
        def _():
            drain(TC, s_tc)

    for a in range(3, LEV + 1):
        @pl.when(lev < a - 1)
        def _(a=a):
            drain(TN.at[a - 3, pl.ds(0, 7)], s_tn.at[a - 3])
            drain(UO2.at[a - 2], s_u2.at[a - 2])

    for a in range(LEV, 1, -1):
        @pl.when((lev < a) & (lev >= 2))
        def _(a=a):
            drain(RX, s_xf.at[a - 1])

        @pl.when((lev == 1) & (a < lev_next))
        def _(a=a):
            drain(PB, s_xf.at[a - 1])


def body(*args):
    chunk = (64, 128)
    vmem = pl.BlockSpec(memory_space=pltpu.VMEM)
    dma = pltpu.SemaphoreType.DMA

    def chunks(*lead, dtype=BF16):
        return pltpu.VMEM(lead + chunk, dtype)

    scratch = [
        chunks(8), chunks(dtype=F32), chunks(8), chunks(5, 8), chunks(5, 7), chunks(5, dtype=F32),
        chunks(5), chunks(5), chunks(5, 2), chunks(16), chunks(8), chunks(dtype=F32), chunks(8),
        chunks(4, 8), chunks(4, 7), chunks(6, 8), chunks(8), chunks(7), chunks(8), chunks(7),
        chunks(dtype=F32), chunks(dtype=F32),
        dma, dma, dma, dma((5,)), dma((5,)), dma((5,)), dma((5,)), dma((5,)), dma, dma, dma, dma,
        dma((4,)), dma((4,)), dma((6,)), dma, dma((6,)), dma, dma, dma, dma,
    ]
    out = jax.ShapeDtypeStruct((1,) + chunk, F32)
    return pl.pallas_call(
        kernel,
        out_shape=(out, out),
        in_specs=[vmem] * 6 + [pl.BlockSpec(memory_space=pltpu.SMEM)],
        out_specs=(vmem, vmem),
        scratch_shapes=scratch,
        compiler_params=pltpu.CompilerParams(collective_id=0, has_side_effects=True, vmem_limit_bytes=40 * 2**20),
        name="solve",
    )(*args)


def solution(mesh):
    in_specs = (
        P("leaf", "blk", None),
        P("leaf", None, None, "blk"),
        P("leaf", "blk", None),
        P("leaf", None, None, "blk"),
        P("leaf", None, "blk"),
        P("leaf", None, "blk"),
        P("leaf", None),
    )
    out_specs = (P("leaf", None, "blk"), P("leaf", None, "blk"))
    return jax.shard_map(body, mesh=mesh, in_specs=in_specs, out_specs=out_specs, check_vma=False)
```

```python
import jax
import jax.numpy as jnp
from jax import lax
from jax.experimental import pallas as pl
from jax.experimental.pallas import tpu as pltpu
from jax.sharding import PartitionSpec as P

MESH = pl.DeviceIdType.MESH
F32 = jnp.float32
BF16 = jnp.bfloat16
NB = 8
LEV = 6


def tree_place(i):
    lev, half, run = 1, 1, 1
    for n in range(LEV):
        run = run * ((i // 2**n) % 2)
        lev = lev + run
        half = half + run * 2**n
    return lev, half


def dot_t(a, b):
    return lax.dot_general(a, b, (((1,), (1,)), ((), ())), preferred_element_type=F32)


def kernel(li_in, lc_in, si_in, sc_in, lr_in, sr_in, pat, lsol, ssol,
           li, lc, si, sc, SRI, ld, LR, LY, T1, TL, RSL, U, UO1, UO2, UX, RX, SR, SY, TC, TN, RSS, XF, PB, RSB, LB, RLB, SA, LA,
           s_lr, r_lr, s_t1, s_tl, r_tl, s_u1, s_u2, r_ux, r_rx, s_sr, r_sr, s_tc, s_tn, r_tn,
           s_xf, s_xo, r_xf, s_pb, r_pb, s_lb, r_lb):
    i = lax.axis_index("leaf")
    b = lax.axis_index("blk")
    lev, half = tree_place(i)
    odd = i % 2
    even_slot = i - odd
    pair_slot = i + 1 - 2 * odd
    pb = (i // (2 * half)) % 2
    parent = i + half - 2 * half * pb
    kid0 = i - half // 2
    kid1 = i + half // 2
    lev_next, _ = tree_place(i + 1)
    owner = lev <= LEV

    def send(src, dst, ssem, rsem, leaf, blk):
        pltpu.make_async_remote_copy(src_ref=src, dst_ref=dst, send_sem=ssem, recv_sem=rsem,
                                     device_id=(leaf, blk), device_id_type=MESH).start()

    def drain(ref, sem):
        pltpu.make_async_copy(ref, ref, sem).wait()

    def others(fn):
        def step(d, c):
            fn(d, (b + d) % NB)
            return c
        lax.fori_loop(1, NB, step, 0)

    def all_blk(fn):
        def step(d, c):
            fn((b + d) % NB)
            return c
        lax.fori_loop(0, NB, step, 0)

    def full(ref):
        return jnp.concatenate([ref[c] for c in range(NB)], axis=1)

    def spread(ref, value):
        for c in range(NB):
            ref[c] = value[:, c * 128:(c + 1) * 128].astype(BF16)

    def sum7(ref):
        total = ref[0].astype(F32)
        for d in range(1, NB - 1):
            total = total + ref[d].astype(F32)
        return total

    loads = [
        pltpu.make_async_copy(lr_in.at[0], LR.at[b], ld.at[0]),
        pltpu.make_async_copy(li_in, li, ld.at[1]),
        pltpu.make_async_copy(lc_in, lc, ld.at[2]),
        pltpu.make_async_copy(sr_in, SRI, ld.at[3]),
        pltpu.make_async_copy(si_in, si, ld.at[4]),
        pltpu.make_async_copy(sc_in, sc, ld.at[5]),
    ]
    for load in loads:
        load.start()

    barrier = pltpu.get_barrier_semaphore()

    def greet(leaf, blk):
        pl.semaphore_signal(barrier, inc=1, device_id=(leaf, blk), device_id_type=MESH)

    pair_is_kin = (lev == 2) | ((lev == 1) & (pb == 0))
    others(lambda d, t: greet(i, t))

    @pl.when(~pair_is_kin)
    def _():
        all_blk(lambda t: greet(pair_slot, t))

    @pl.when(lev < LEV)
    def _():
        all_blk(lambda t: greet(parent, t))

    @pl.when((lev >= 2) & owner)
    def _():
        all_blk(lambda t: greet(kid0, t))
        all_blk(lambda t: greet(kid1, t))

    peers = (7 + jnp.where(pair_is_kin, 0, 8) + jnp.where(lev < LEV, 8, 0)
             + jnp.where((lev >= 2) & owner, 16, 0))
    pl.semaphore_wait(barrier, peers)

    loads[0].wait()
    others(lambda d, t: send(LR.at[b], LR.at[b], s_lr, r_lr, i, t))
    drain(LR.at[pl.ds(0, 7)], r_lr)
    loads[1].wait()
    ly = dot_t(full(LR), li[0])
    LY[...] = ly
    LA[...] = ly
    lyb = ly.astype(BF16)

    loads[2].wait()
    spread(T1, dot_t(lyb, lc[0, 0]) * pat[0, 0].astype(F32))

    @pl.when(odd == 1)
    def _():
        all_blk(lambda t: send(T1.at[t], RX.at[NB + b], s_t1, r_rx, even_slot, t))

    @pl.when(odd == 0)
    def _():
        RX[b] = T1[b]
        others(lambda d, t: send(T1.at[t], RX.at[b], s_t1, r_rx, i, t))

    for a in range(2, LEV + 1):
        n = a - 2
        spread(TL.at[n], dot_t(lyb, lc[0, a - 1]) * pat[0, a - 1].astype(F32))
        others(lambda d, t, n=n: send(TL.at[n, t], RSL.at[n, d - 1], s_tl.at[n], r_tl.at[n], i, t))

    for a in range(2, LEV + 1):
        n = a - 2
        drain(RSL.at[n], r_tl.at[n])
        total = TL[n, b].astype(F32) + sum7(RSL.at[n])

        @pl.when(odd == 1)
        def _(n=n, total=total):
            UO1[n] = total.astype(BF16)
            send(UO1.at[n], UX.at[n, 1], s_u1.at[n], r_ux.at[n], even_slot, b)
            U[n] = jnp.zeros((64, 128), F32)

        @pl.when(odd == 0)
        def _(n=n, total=total):
            U[n] = total
            UX[n, 0] = jnp.zeros((64, 128), BF16)

    def upward(n):
        @pl.when(lev == 1)
        def _():
            drain(UX.at[n, 1], r_ux.at[n])

        @pl.when(lev != 1)
        def _():
            drain(UX.at[n], r_ux.at[n])

        return U[n] + UX[n, 0].astype(F32) + UX[n, 1].astype(F32)

    for load in loads[3:]:
        load.wait()

    @pl.when(owner)
    def _():
        @pl.when(lev == 1)
        def _():
            drain(RX.at[pl.ds(0, 15)], r_rx)

        @pl.when(lev != 1)
        def _():
            drain(RX, r_rx)

        rs = SRI[0].astype(F32)
        for c in range(2 * NB):
            rs = rs - RX[c].astype(F32)
        SR[b] = rs.astype(BF16)
        others(lambda d, t: send(SR.at[b], SR.at[b], s_sr, r_sr, i, t))
        drain(SR.at[pl.ds(0, 7)], r_sr)
        sy = dot_t(full(SR), si[0])
        SA[...] = sy
        syb = sy.astype(BF16)

        for a in range(2, LEV + 1):
            n = a - 2

            @pl.when(lev == a - 1)
            def _(a=a, n=n):
                spread(TC, dot_t(syb, sc[0, a - 1]))
                others(lambda d, t: send(TC.at[t], RX.at[pb * NB + b], s_tc, r_rx, parent, t))
                TC[b] = (TC[b].astype(F32) + upward(n)).astype(BF16)
                send(TC.at[b], RX.at[pb * NB + b], s_tc, r_rx, parent, b)

            if a > 2:
                @pl.when(lev < a - 1)
                def _(a=a, n=n):
                    spread(TN.at[a - 3], dot_t(syb, sc[0, a - 1]))
                    others(lambda d, t: send(TN.at[a - 3, t], RSS.at[a - 3, d - 1], s_tn.at[a - 3], r_tn.at[a - 3], i, t))

        for a in range(3, LEV + 1):
            n = a - 2

            @pl.when(lev < a - 1)
            def _(a=a, n=n):
                drain(RSS.at[a - 3], r_tn.at[a - 3])
                UO2[n] = (TN[a - 3, b].astype(F32) + sum7(RSS.at[a - 3]) + upward(n)).astype(BF16)
                send(UO2.at[n], UX.at[n, pb], s_u2.at[n], r_ux.at[n], parent, b)

    def leaf_part(a):
        LA[...] = LA[...] - pat[0, a - 1].astype(F32) * jnp.dot(full(XF.at[a - 1]), lc[0, a - 1], preferred_element_type=F32)

    for a in range(LEV, 1, -1):
        @pl.when(lev < a)
        def _(a=a):
            drain(XF.at[a - 1], r_xf.at[a - 1])

            @pl.when(lev >= 2)
            def _():
                all_blk(lambda t: send(XF.at[a - 1, b], XF.at[a - 1, b], s_xf.at[a - 1], r_xf.at[a - 1], kid0, t))
                all_blk(lambda t: send(XF.at[a - 1, b], XF.at[a - 1, b], s_xf.at[a - 1], r_xf.at[a - 1], kid1, t))

            @pl.when((lev == 1) & (a < lev_next))
            def _():
                all_blk(lambda t: send(XF.at[a - 1, b], XF.at[a - 1, b], s_xf.at[a - 1], r_xf.at[a - 1], pair_slot, t))

            SA[...] = SA[...] - jnp.dot(full(XF.at[a - 1]), sc[0, a - 1], preferred_element_type=F32)
            leaf_part(a)

    @pl.when(owner)
    def _():
        spread(PB, jnp.dot(SA[...].astype(BF16), si[0], preferred_element_type=F32))
        others(lambda d, t: send(PB.at[t], RSB.at[d - 1], s_pb, r_pb, i, t))
        drain(RSB, r_pb)
        x = PB[b].astype(F32) + sum7(RSB)
        ssol[0] = x
        own = lev - 1
        XF[own, b] = x.astype(BF16)

        @pl.when(lev >= 2)
        def _():
            all_blk(lambda t: send(XF.at[own, b], XF.at[own, b], s_xo, r_xf.at[own], kid0, t))
            all_blk(lambda t: send(XF.at[own, b], XF.at[own, b], s_xo, r_xf.at[own], kid1, t))

        @pl.when(lev == 1)
        def _():
            all_blk(lambda t: send(XF.at[own, b], XF.at[own, b], s_xo, r_xf.at[own], pair_slot, t))

        others(lambda d, t: send(XF.at[own, b], XF.at[own, b], s_pb, r_xf.at[own], i, t))
        drain(XF.at[own, pl.ds(0, 7)], r_xf.at[own])
        leaf_part(lev)

    @pl.when(lev > LEV)
    def _():
        ssol[0] = jnp.zeros((64, 128), F32)

    for a in range(LEV, 0, -1):
        @pl.when(a < lev)
        def _(a=a):
            drain(XF.at[a - 1], r_xf.at[a - 1])
            leaf_part(a)

    spread(LB, jnp.dot(LA[...].astype(BF16), li[0], preferred_element_type=F32))
    others(lambda d, t: send(LB.at[t], RLB.at[d - 1], s_lb, r_lb, i, t))
    drain(RLB, r_lb)
    lsol[0] = LB[b].astype(F32) + sum7(RLB)

    drain(LR.at[pl.ds(0, 7)], s_lr)

    @pl.when(odd == 1)
    def _():
        drain(T1, s_t1)
        for n in range(LEV - 1):
            drain(UO1.at[n], s_u1.at[n])

    @pl.when(odd == 0)
    def _():
        drain(T1.at[pl.ds(0, 7)], s_t1)

    for n in range(LEV - 1):
        drain(TL.at[n, pl.ds(0, 7)], s_tl.at[n])
    drain(LB.at[pl.ds(0, 7)], s_lb)

    @pl.when(owner)
    def _():
        drain(SR.at[pl.ds(0, 7)], s_sr)
        drain(RX.at[pl.ds(0, 14)], s_pb)

        @pl.when(lev >= 2)
        def _():
            drain(RX, s_xo)

        @pl.when(lev == 1)
        def _():
            drain(PB, s_xo)

        @pl.when(lev < LEV)
        def _():
            drain(TC, s_tc)

    for a in range(3, LEV + 1):
        @pl.when(lev < a - 1)
        def _(a=a):
            drain(TN.at[a - 3, pl.ds(0, 7)], s_tn.at[a - 3])
            drain(UO2.at[a - 2], s_u2.at[a - 2])

    for a in range(LEV, 1, -1):
        @pl.when((lev < a) & (lev >= 2))
        def _(a=a):
            drain(RX, s_xf.at[a - 1])

        @pl.when((lev == 1) & (a < lev_next))
        def _(a=a):
            drain(PB, s_xf.at[a - 1])


def body(*args):
    chunk = (64, 128)
    vmem = pl.BlockSpec(memory_space=pltpu.VMEM)
    dma = pltpu.SemaphoreType.DMA

    def chunks(*lead, dtype=BF16):
        return pltpu.VMEM(lead + chunk, dtype)

    scratch = [
        pltpu.VMEM((1, 128, 1024), BF16), pltpu.VMEM((1, 6, 1024, 128), BF16),
        pltpu.VMEM((1, 128, 1024), BF16), pltpu.VMEM((1, 6, 1024, 128), BF16), chunks(1), dma((6,)),
        chunks(8), chunks(dtype=F32), chunks(8), chunks(5, 8), chunks(5, 7), chunks(5, dtype=F32),
        chunks(5), chunks(5), chunks(5, 2), chunks(16), chunks(8), chunks(dtype=F32), chunks(8),
        chunks(4, 8), chunks(4, 7), chunks(6, 8), chunks(8), chunks(7), chunks(8), chunks(7),
        chunks(dtype=F32), chunks(dtype=F32),
        dma, dma, dma, dma((5,)), dma((5,)), dma((5,)), dma((5,)), dma((5,)), dma, dma, dma, dma,
        dma((4,)), dma((4,)), dma((6,)), dma, dma((6,)), dma, dma, dma, dma,
    ]
    out = jax.ShapeDtypeStruct((1,) + chunk, F32)
    return pl.pallas_call(
        kernel,
        out_shape=(out, out),
        in_specs=[pl.BlockSpec(memory_space=pl.ANY)] * 6 + [pl.BlockSpec(memory_space=pltpu.SMEM)],
        out_specs=(vmem, vmem),
        scratch_shapes=scratch,
        compiler_params=pltpu.CompilerParams(collective_id=0, has_side_effects=True, vmem_limit_bytes=56 * 2**20),
        name="solve",
    )(*args)


def solution(mesh):
    in_specs = (
        P("leaf", "blk", None),
        P("leaf", None, None, "blk"),
        P("leaf", "blk", None),
        P("leaf", None, None, "blk"),
        P("leaf", None, "blk"),
        P("leaf", None, "blk"),
        P("leaf", None),
    )
    out_specs = (P("leaf", None, "blk"), P("leaf", None, "blk"))
    return jax.shard_map(body, mesh=mesh, in_specs=in_specs, out_specs=out_specs, check_vma=False)
```

```python
import jax
import jax.numpy as jnp
from jax import lax
from jax.experimental import pallas as pl
from jax.experimental.pallas import tpu as pltpu
from jax.sharding import PartitionSpec as P

MESH = pl.DeviceIdType.MESH
F32 = jnp.float32
BF16 = jnp.bfloat16
NB = 8
LEV = 6


def tree_place(i):
    lev, half, run = 1, 1, 1
    for n in range(3):
        run = run * ((i // 2**n) % 2)
        lev = lev + run
        half = half + run * 2**n
    run = run * ((i // 8) % 2)
    return lev + 3 * run, half


def dot(a, b):
    return jnp.dot(a, b, preferred_element_type=F32)


def dot_t(a, b):
    return lax.dot_general(a, b, (((1,), (1,)), ((), ())), preferred_element_type=F32)


class Names:
    def __init__(self, names, refs):
        for name, ref in zip(names, refs, strict=True):
            setattr(self, name, ref)


def chunks(*lead, dtype=BF16):
    return pltpu.VMEM(lead + (64, 128), dtype)


def sems(*shape):
    return pltpu.SemaphoreType.DMA(shape) if shape else pltpu.SemaphoreType.DMA


def blocks(*shape):
    return pltpu.VMEM(shape, BF16)


SCRATCH = dict(
    li=blocks(1, 128, 1024), lc=blocks(1, 6, 1024, 128), si=blocks(1, 128, 1024), sc=blocks(1, 6, 1024, 128),
    SRI=chunks(1), ld=sems(6),
    LR=chunks(8), LY=chunks(dtype=F32), T1=chunks(8), TL=chunks(5, 8), RSL=chunks(5, 7), U=chunks(5, dtype=F32),
    UO1=chunks(5), UO2=chunks(5), UX=chunks(5, 2),
    s_lr=sems(), r_lr=sems(), s_t1=sems(), s_tl=sems(5), r_tl=sems(5), s_u1=sems(5), s_u2=sems(5), r_ux=sems(5),
    RX=chunks(16), SR=chunks(8), TC=chunks(8), TN=chunks(4, 8), RSS=chunks(4, 7), XF=chunks(6, 8),
    PB=chunks(8), RSB=chunks(7), SA=chunks(dtype=F32), SZ=chunks(dtype=F32), LA=chunks(dtype=F32),
    r_rx=sems(), s_sr=sems(), r_sr=sems(), s_tc=sems(), s_tn=sems(4), r_tn=sems(4),
    s_xf=sems(6), s_xb=sems(2), s_xo=sems(), r_xf=sems(6), s_pb=sems(), r_pb=sems(),
    IG=blocks(8, 128, 128), CG=blocks(2, 8, 1024, 128), VG=blocks(8, 128, 1024), M=blocks(2, 1024, 128), G=blocks(128, 1024),
    s_ig=sems(), r_ig=sems(), l_ig=sems(), s_g=sems(3), ra_g=sems(3), rb_g=sems(3), l_g=sems(3),
    HM=blocks(1024, 128), HG5=blocks(128, 1024), HG6=blocks(128, 1024), H5=chunks(1), H6=chunks(1),
    s_hm=sems(), s_hs=sems(), r_hm=sems(), r_hg5=sems(), r_hg6=sems(), r_h5=sems(), r_h6=sems(),
    RX5=chunks(16), RX6=chunks(16), SR5=chunks(8), SR6=chunks(8), TD=chunks(8), HU=chunks(2), Z5=chunks(dtype=F32),
    r_rx5=sems(), r_rx6=sems(), s_r5=sems(), r_r5=sems(), s_r6=sems(), r_r6=sems(), s_td=sems(), r_hu=sems(),
    HX=chunks(dtype=F32), HY=chunks(dtype=F32), s_hx=sems(), r_hx=sems(),
    LB=chunks(8), RLB=chunks(7), s_lb=sems(), r_lb=sems(),
)


def kernel(li_in, lc_in, si_in, sc_in, lr_in, sr_in, pat, lsol, ssol, *scratch):
    v = Names(SCRATCH, scratch)
    i = lax.axis_index("leaf")
    b = lax.axis_index("blk")
    x, z = i // 16, i % 16
    core = b % 2
    mate = b + 1 - 2 * core
    lev, half = tree_place(i)
    lev_next, _ = tree_place(i + 1)
    odd = i % 2
    even_slot = i - odd
    pair_slot = i + 1 - 2 * odd
    side = (i // (2 * half)) % 2
    parent = i + half - 2 * half * side
    kid0 = i - half // 2
    kid1 = i + half // 2
    normal = lev <= 4
    host = lev == 4
    own5 = (z == 15) & (x % 2 == 0)
    own6 = (z == 15) & (x == 1)
    x_near = x + 1 - 2 * (x % 2)
    x_far = (x + 2) % 4
    near = x_near * 16 + 7
    far = x_far * 16 + 7
    host_a = (x - x % 2) * 16 + 7
    host_b = host_a + 16
    owner5 = (x - x % 2) * 16 + 15

    def send(src, dst, ssem, rsem, leaf, blk):
        pltpu.make_async_remote_copy(src_ref=src, dst_ref=dst, send_sem=ssem, recv_sem=rsem,
                                     device_id=(leaf, blk), device_id_type=MESH).start()

    def drain(ref, sem):
        pltpu.make_async_copy(ref, ref, sem).wait()

    def others(fn):
        def step(d, c):
            fn(d, (b + d) % NB)
            return c
        lax.fori_loop(1, NB, step, 0)

    def all_blk(fn):
        def step(d, c):
            fn((b + d) % NB)
            return c
        lax.fori_loop(0, NB, step, 0)

    def full(ref):
        return jnp.concatenate([ref[c] for c in range(NB)], axis=1)

    def spread(ref, value):
        for c in range(NB):
            ref[c] = value[:, c * 128:(c + 1) * 128].astype(BF16)

    def total(ref, count):
        acc = ref[0].astype(F32)
        for d in range(1, count):
            acc = acc + ref[d].astype(F32)
        return acc

    loads = [
        pltpu.make_async_copy(lr_in.at[0], v.LR.at[b], v.ld.at[0]),
        pltpu.make_async_copy(li_in, v.li, v.ld.at[1]),
        pltpu.make_async_copy(lc_in, v.lc, v.ld.at[2]),
        pltpu.make_async_copy(sr_in, v.SRI, v.ld.at[3]),
        pltpu.make_async_copy(si_in, v.si, v.ld.at[4]),
        pltpu.make_async_copy(sc_in, v.sc, v.ld.at[5]),
    ]
    for load in loads:
        load.start()

    barrier = pltpu.get_barrier_semaphore()

    def greet(leaf, blk):
        pl.semaphore_signal(barrier, inc=1, device_id=(leaf, blk), device_id_type=MESH)

    pair_is_kin = (lev == 2) | ((lev == 1) & (side == 0))
    has_kids = (lev >= 2) & normal
    others(lambda d, t: greet(i, t))

    @pl.when(host | own5)
    def _():
        @pl.when(host)
        def _():
            greet(owner5, b)
            greet(31, b)

        @pl.when(own5)
        def _():
            greet(host_a, b)
            greet(host_b, b)

    @pl.when(own6)
    def _():
        for h in range(4):
            greet(16 * h + 7, b)

    @pl.when(host)
    def _():
        all_blk(lambda t: greet(near, t))
        all_blk(lambda t: greet(far, t))

    @pl.when(~pair_is_kin)
    def _():
        all_blk(lambda t: greet(pair_slot, t))

    @pl.when(lev <= 3)
    def _():
        all_blk(lambda t: greet(parent, t))

    @pl.when(has_kids)
    def _():
        all_blk(lambda t: greet(kid0, t))
        all_blk(lambda t: greet(kid1, t))

    peers = (7 + jnp.where(pair_is_kin, 0, 8) + jnp.where(lev <= 3, 8, 0) + jnp.where(has_kids, 16, 0)
             + jnp.where(host, 18, 0) + jnp.where(own5, 2, 0) + jnp.where(own6, 4, 0))
    pl.semaphore_wait(barrier, peers)

    loads[0].wait()
    others(lambda d, t: send(v.LR.at[b], v.LR.at[b], v.s_lr, v.r_lr, i, t))
    for load in loads[1:]:
        load.wait()

    @pl.when(own5)
    def _():
        send(v.SRI, v.H5, v.s_hs, v.r_h5, host_a, b)
        send(v.SRI, v.H5, v.s_hs, v.r_h5, host_b, b)

    @pl.when(own6)
    def _():
        for h in range(4):
            send(v.SRI, v.H6, v.s_hs, v.r_h6, 16 * h + 7, b)

    drain(v.LR.at[pl.ds(0, 7)], v.r_lr)
    ly = dot_t(full(v.LR), v.li[0])
    v.LA[...] = ly
    lyb = ly.astype(BF16)
    spread(v.T1, dot_t(lyb, v.lc[0, 0]) * pat[0, 0].astype(F32))

    @pl.when(odd == 1)
    def _():
        all_blk(lambda t: send(v.T1.at[t], v.RX.at[NB + b], v.s_t1, v.r_rx, even_slot, t))

    @pl.when(odd == 0)
    def _():
        v.RX[b] = v.T1[b]
        others(lambda d, t: send(v.T1.at[t], v.RX.at[b], v.s_t1, v.r_rx, i, t))

    for a in range(2, LEV + 1):
        n = a - 2
        spread(v.TL.at[n], dot_t(lyb, v.lc[0, a - 1]) * pat[0, a - 1].astype(F32))
        others(lambda d, t, n=n: send(v.TL.at[n, t], v.RSL.at[n, d - 1], v.s_tl.at[n], v.r_tl.at[n], i, t))

    def gather_start(k, src, dst):
        pltpu.make_async_copy(src, dst.at[b], v.l_g.at[k]).start()
        for dy in range(1, 4):
            send(src, dst.at[b], v.s_g.at[k], v.ra_g.at[k], i, (b + 2 * dy) % NB)
        send(src, dst.at[b], v.s_g.at[k], v.rb_g.at[k], i, mate)

    def gather_pass(k, dst):
        drain(dst.at[pl.ds(0, 3)], v.ra_g.at[k])
        for dy in range(1, 4):
            t = (b + 2 * dy) % NB
            send(dst.at[t], dst.at[t], v.s_g.at[k], v.rb_g.at[k], i, mate)

    def gather_end(k, dst):
        drain(dst.at[pl.ds(0, 4)], v.rb_g.at[k])
        drain(dst.at[b], v.l_g.at[k])

    def inverse_columns_start():
        pltpu.make_async_copy(v.si.at[0, :, pl.ds(pl.multiple_of(b * 128, 128), 128)], v.IG.at[b], v.l_ig).start()
        others(lambda d, t: send(v.si.at[0, :, pl.ds(pl.multiple_of(t * 128, 128), 128)], v.IG.at[b],
                                 v.s_ig, v.r_ig, i, t))

    def inverse_columns_end():
        drain(v.IG.at[pl.ds(0, 7)], v.r_ig)
        drain(v.IG.at[b], v.l_ig)

    def form_m(k):
        columns = v.IG[...].reshape(1024, 128)

        def tile(r, c):
            rows = pl.ds(pl.multiple_of(r * 256, 256), 256)
            left = jnp.concatenate([v.CG[k, s, rows, :] for s in range(NB)], axis=1)
            v.M[k, rows, :] = dot(left, columns).astype(BF16)
            return c
        lax.fori_loop(0, 4, tile, 0)

    def form_g():
        columns = v.IG[...].reshape(1024, 128)

        def tile(r, c):
            cols = pl.ds(pl.multiple_of(r * 256, 256), 256)
            right = v.VG[:, :, cols].reshape(1024, 256)
            v.G[:, cols] = lax.dot_general(columns, right, (((0,), (0,)), ((), ())),
                                           preferred_element_type=F32).astype(BF16)
            return c
        lax.fori_loop(0, 4, tile, 0)

    def products_start():
        inverse_columns_start()
        gather_start(0, v.sc.at[0, lev], v.CG.at[0])
        gather_start(1, v.sc.at[0, lev + 1], v.CG.at[1])

    def products_end():
        inverse_columns_end()
        gather_pass(0, v.CG.at[0])
        gather_end(0, v.CG.at[0])
        form_m(0)
        gather_pass(1, v.CG.at[1])
        gather_end(1, v.CG.at[1])
        form_m(1)

    early = (lev == 3) | (lev == 4)

    @pl.when(early)
    def _():
        products_start()

    @pl.when(own5 | own6)
    def _():
        inverse_columns_start()

        @pl.when(own5)
        def _():
            gather_start(0, v.sc.at[0, 5], v.CG.at[0])

        gather_start(2, v.si.at[0], v.VG)

    for a in range(2, LEV + 1):
        n = a - 2
        drain(v.RSL.at[n], v.r_tl.at[n])
        acc = v.TL[n, b].astype(F32) + total(v.RSL.at[n], 7)

        @pl.when(odd == 1)
        def _(n=n, acc=acc):
            v.UO1[n] = acc.astype(BF16)
            send(v.UO1.at[n], v.UX.at[n, 1], v.s_u1.at[n], v.r_ux.at[n], even_slot, b)
            v.U[n] = jnp.zeros((64, 128), F32)

        @pl.when(odd == 0)
        def _(n=n, acc=acc):
            v.U[n] = acc
            v.UX[n, 0] = jnp.zeros((64, 128), BF16)

    @pl.when(early)
    def _():
        products_end()

    @pl.when(own5 | own6)
    def _():
        inverse_columns_end()

        @pl.when(own5)
        def _():
            gather_pass(0, v.CG.at[0])
            gather_end(0, v.CG.at[0])
            form_m(0)
            send(v.M.at[0], v.HM, v.s_hm, v.r_hm, host_a, b)
            send(v.M.at[0], v.HM, v.s_hm, v.r_hm, host_b, b)

        gather_pass(2, v.VG)
        gather_end(2, v.VG)
        form_g()

        @pl.when(own5)
        def _():
            send(v.G, v.HG5, v.s_hm, v.r_hg5, host_a, b)
            send(v.G, v.HG5, v.s_hm, v.r_hg5, host_b, b)

        @pl.when(own6)
        def _():
            for h in range(4):
                send(v.G, v.HG6, v.s_hm, v.r_hg6, 16 * h + 7, b)

    def upward(n):
        @pl.when(lev == 1)
        def _():
            drain(v.UX.at[n, 1], v.r_ux.at[n])

        @pl.when(lev != 1)
        def _():
            drain(v.UX.at[n], v.r_ux.at[n])

        return v.U[n] + v.UX[n, 0].astype(F32) + v.UX[n, 1].astype(F32)

    def to_parent(n):
        others(lambda d, t: send(v.TC.at[t], v.RX.at[side * NB + b], v.s_tc, v.r_rx, parent, t))
        v.TC[b] = (v.TC[b].astype(F32) + upward(n)).astype(BF16)
        send(v.TC.at[b], v.RX.at[side * NB + b], v.s_tc, v.r_rx, parent, b)

    def over_blk(a, value):
        spread(v.TN.at[a - 3], value)
        others(lambda d, t: send(v.TN.at[a - 3, t], v.RSS.at[a - 3, d - 1], v.s_tn.at[a - 3], v.r_tn.at[a - 3], i, t))

    def far_part_start():
        spread(v.PB, dot(v.SA[...].astype(BF16), v.si[0]))
        others(lambda d, t: send(v.PB.at[t], v.RSB.at[d - 1], v.s_pb, v.r_pb, i, t))

    @pl.when(normal)
    def _():
        @pl.when(lev == 1)
        def _():
            drain(v.RX.at[pl.ds(0, 15)], v.r_rx)

        @pl.when(lev != 1)
        def _():
            drain(v.RX, v.r_rx)

        rs = v.SRI[0].astype(F32) - total(v.RX, 16)
        rsb = rs.astype(BF16)
        v.SR[b] = rsb

        @pl.when(early)
        def _():
            spread(v.TC, dot_t(rsb, v.M[0]))

            @pl.when(lev == 3)
            def _():
                to_parent(2)
                over_blk(5, dot_t(rsb, v.M[1]))

            @pl.when(lev == 4)
            def _():
                v.TC[b] = (v.TC[b].astype(F32) + upward(3)).astype(BF16)
                mine = (x % 2) * NB + b
                v.RX5[mine] = v.TC[b]
                all_blk(lambda t: send(v.TC.at[t], v.RX5.at[mine], v.s_tc, v.r_rx5, near, t))
                others(lambda d, t: send(v.TC.at[t], v.RX5.at[mine], v.s_tc, v.r_rx5, i, t))
                over_blk(6, dot_t(rsb, v.M[1]))

        others(lambda d, t: send(v.SR.at[b], v.SR.at[b], v.s_sr, v.r_sr, i, t))
        drain(v.SR.at[pl.ds(0, 7)], v.r_sr)
        sy = dot_t(full(v.SR), v.si[0])
        v.SA[...] = sy
        syb = sy.astype(BF16)

        for a in (2, 3):
            @pl.when(lev == a - 1)
            def _(a=a):
                spread(v.TC, dot_t(syb, v.sc[0, a - 1]))
                to_parent(a - 2)

        for a in range(3, LEV + 1):
            @pl.when((lev < a - 1) & ((lev <= 2) | ((lev == 3) & (a == 6))))
            def _(a=a):
                over_blk(a, dot_t(syb, v.sc[0, a - 1]))

        for a in range(3, LEV + 1):
            n = a - 2

            @pl.when(lev < a - 1)
            def _(a=a, n=n):
                drain(v.RSS.at[a - 3], v.r_tn.at[a - 3])
                acc = v.TN[a - 3, b].astype(F32) + total(v.RSS.at[a - 3], 7) + upward(n)
                v.UO2[n] = acc.astype(BF16)

                @pl.when(lev <= 3)
                def _():
                    send(v.UO2.at[n], v.UX.at[n, side], v.s_u2.at[n], v.r_ux.at[n], parent, b)

                if a == 6:
                    @pl.when(lev == 4)
                    def _():
                        v.HU[x % 2] = v.UO2[n]
                        send(v.UO2.at[n], v.HU.at[x % 2], v.s_u2.at[n], v.r_hu, near, b)

        @pl.when(lev == 4)
        def _():
            far_part_start()

        @pl.when(lev <= 2)
        def _():
            products_start()
            products_end()

    def leaf_part(a):
        v.LA[...] = v.LA[...] - pat[0, a - 1].astype(F32) * dot(full(v.XF.at[a - 1]), v.lc[0, a - 1])

    def to_kids(n, sem):
        all_blk(lambda t: send(v.XF.at[n, b], v.XF.at[n, b], sem, v.r_xf.at[n], kid0, t))
        all_blk(lambda t: send(v.XF.at[n, b], v.XF.at[n, b], sem, v.r_xf.at[n], kid1, t))

    def to_pair(n, sem):
        all_blk(lambda t: send(v.XF.at[n, b], v.XF.at[n, b], sem, v.r_xf.at[n], pair_slot, t))

    def to_blk(n, sem):
        others(lambda d, t: send(v.XF.at[n, b], v.XF.at[n, b], sem, v.r_xf.at[n], i, t))

    def finish():
        drain(v.RSB, v.r_pb)
        sol = v.PB[b].astype(F32) + total(v.RSB, 7) - v.SZ[...]
        own = lev - 1
        v.XF[own, b] = sol.astype(BF16)

        @pl.when(lev >= 2)
        def _():
            to_kids(own, v.s_xo)

        @pl.when(lev == 1)
        def _():
            to_pair(own, v.s_xo)

        to_blk(own, v.s_pb)
        ssol[0] = sol

    @pl.when(host)
    def _():
        drain(v.RX5.at[pl.ds(0, 15)], v.r_rx5)
        drain(v.H5, v.r_h5)
        rs = (v.H5[0].astype(F32) - total(v.RX5, 16)).astype(BF16)
        v.SR5[b] = rs
        drain(v.HM, v.r_hm)
        spread(v.TD, dot_t(rs, v.HM[...]))
        drain(v.HU.at[0], v.r_hu)
        v.TD[b] = (v.TD[b].astype(F32) + v.HU[0].astype(F32) + v.HU[1].astype(F32)).astype(BF16)
        mine = (x // 2) * NB + b
        v.RX6[mine] = v.TD[b]
        all_blk(lambda t: send(v.TD.at[t], v.RX6.at[mine], v.s_td, v.r_rx6, far, t))
        others(lambda d, t: send(v.TD.at[t], v.RX6.at[mine], v.s_td, v.r_rx6, i, t))
        others(lambda d, t: send(v.SR5.at[b], v.SR5.at[b], v.s_r5, v.r_r5, i, t))
        drain(v.SR5.at[pl.ds(0, 7)], v.r_r5)
        drain(v.HG5, v.r_hg5)
        v.Z5[...] = dot_t(full(v.SR5), v.HG5[...])

        drain(v.RX6.at[pl.ds(0, 15)], v.r_rx6)
        drain(v.H6, v.r_h6)
        v.SR6[b] = (v.H6[0].astype(F32) - total(v.RX6, 16)).astype(BF16)
        others(lambda d, t: send(v.SR6.at[b], v.SR6.at[b], v.s_r6, v.r_r6, i, t))
        drain(v.HG6, v.r_hg6)
        drain(v.SR6.at[pl.ds(0, 7)], v.r_r6)
        sol6 = dot_t(full(v.SR6), v.HG6[...])
        v.XF[5, b] = sol6.astype(BF16)
        to_blk(5, v.s_xb.at[1])
        to_kids(5, v.s_xf.at[5])
        drain(v.XF.at[5, pl.ds(0, 7)], v.r_xf.at[5])
        x6 = full(v.XF.at[5])
        sol5 = v.Z5[...] - dot(x6, v.HM[...])
        v.XF[4, b] = sol5.astype(BF16)
        to_blk(4, v.s_xb.at[0])
        to_kids(4, v.s_xf.at[4])
        part = dot(x6, v.M[1])

        @pl.when(x == 1)
        def _():
            v.HX[...] = sol6
            send(v.HX, v.HY, v.s_hx, v.r_hx, 31, b)

        @pl.when(x % 2 == 0)
        def _():
            v.HX[...] = sol5
            send(v.HX, v.HY, v.s_hx, v.r_hx, owner5, b)

        leaf_part(6)
        drain(v.XF.at[4, pl.ds(0, 7)], v.r_xf.at[4])
        v.SZ[...] = part + dot(full(v.XF.at[4]), v.M[0])
        finish()
        leaf_part(5)

    for a in range(LEV, 1, -1):
        @pl.when((lev <= 3) & (lev < a))
        def _(a=a):
            n = a - 1
            drain(v.XF.at[n], v.r_xf.at[n])

            @pl.when(lev >= 2)
            def _():
                to_kids(n, v.s_xf.at[n])

            @pl.when((lev == 1) & (a < lev_next))
            def _():
                to_pair(n, v.s_xf.at[n])

            @pl.when(a >= lev + 3)
            def _():
                v.SA[...] = v.SA[...] - dot(full(v.XF.at[n]), v.sc[0, n])

            @pl.when(a == lev + 3)
            def _():
                far_part_start()

            @pl.when(a == lev + 2)
            def _():
                v.SZ[...] = dot(full(v.XF.at[n]), v.M[1])

            @pl.when(a == lev + 1)
            def _():
                v.SZ[...] = v.SZ[...] + dot(full(v.XF.at[n]), v.M[0])
                finish()

            leaf_part(a)

    @pl.when(normal)
    def _():
        drain(v.XF.at[lev - 1, pl.ds(0, 7)], v.r_xf.at[lev - 1])
        leaf_part(lev)

    @pl.when(own5 | own6)
    def _():
        drain(v.HY, v.r_hx)
        ssol[0] = v.HY[...]

    @pl.when((z == 15) & (x == 3))
    def _():
        ssol[0] = jnp.zeros((64, 128), F32)

    for a in range(LEV, 0, -1):
        @pl.when(a < lev)
        def _(a=a):
            drain(v.XF.at[a - 1], v.r_xf.at[a - 1])
            leaf_part(a)

    spread(v.LB, dot(v.LA[...].astype(BF16), v.li[0]))
    others(lambda d, t: send(v.LB.at[t], v.RLB.at[d - 1], v.s_lb, v.r_lb, i, t))
    drain(v.RLB, v.r_lb)
    lsol[0] = v.LB[b].astype(F32) + total(v.RLB, 7)

    seven = pl.ds(0, 7)
    drain(v.LR.at[seven], v.s_lr)

    @pl.when(odd == 1)
    def _():
        drain(v.T1, v.s_t1)
        for n in range(LEV - 1):
            drain(v.UO1.at[n], v.s_u1.at[n])

    @pl.when(odd == 0)
    def _():
        drain(v.T1.at[seven], v.s_t1)

    for n in range(LEV - 1):
        drain(v.TL.at[n, seven], v.s_tl.at[n])
    drain(v.LB.at[seven], v.s_lb)

    @pl.when(normal)
    def _():
        drain(v.SR.at[seven], v.s_sr)
        drain(v.RX.at[pl.ds(0, 14)], v.s_pb)
        drain(v.IG.at[seven], v.s_ig)
        drain(v.CG.at[0, seven], v.s_g.at[0])
        drain(v.CG.at[1, seven], v.s_g.at[1])

        @pl.when(lev >= 2)
        def _():
            drain(v.RX, v.s_xo)

        @pl.when(lev == 1)
        def _():
            drain(v.PB, v.s_xo)

        @pl.when(lev <= 3)
        def _():
            drain(v.TC, v.s_tc)

        for a in range(3, LEV + 1):
            @pl.when(lev < a - 1)
            def _(a=a):
                drain(v.TN.at[a - 3, seven], v.s_tn.at[a - 3])
                drain(v.UO2.at[a - 2], v.s_u2.at[a - 2])

    @pl.when(host)
    def _():
        drain(v.RX.at[pl.ds(0, 15)], v.s_tc)
        drain(v.RX.at[pl.ds(0, 15)], v.s_td)
        drain(v.SR5.at[seven], v.s_r5)
        drain(v.SR6.at[seven], v.s_r6)
        for n in range(2):
            drain(v.RX, v.s_xf.at[4 + n])
            drain(v.SR5.at[seven], v.s_xb.at[n])

        @pl.when(x < 3)
        def _():
            drain(v.HX, v.s_hx)

    @pl.when(own5 | own6)
    def _():
        drain(v.IG.at[seven], v.s_ig)
        drain(v.VG.at[seven], v.s_g.at[2])
        drain(v.CG.at[0, pl.ds(0, 4)], v.s_hm)

    @pl.when(own5)
    def _():
        drain(v.CG.at[0, seven], v.s_g.at[0])
        drain(v.PB.at[pl.ds(0, 2)], v.s_hs)

    @pl.when(own6)
    def _():
        drain(v.PB.at[pl.ds(0, 4)], v.s_hs)

    for a in range(LEV, 1, -1):
        @pl.when((lev < a) & ((lev == 2) | (lev == 3)))
        def _(a=a):
            drain(v.RX, v.s_xf.at[a - 1])

        @pl.when((lev == 1) & (a < lev_next))
        def _(a=a):
            drain(v.PB, v.s_xf.at[a - 1])


def body(*args):
    vmem = pl.BlockSpec(memory_space=pltpu.VMEM)
    out = jax.ShapeDtypeStruct((1, 64, 128), F32)
    return pl.pallas_call(
        kernel,
        out_shape=(out, out),
        in_specs=[pl.BlockSpec(memory_space=pl.ANY)] * 6 + [pl.BlockSpec(memory_space=pltpu.SMEM)],
        out_specs=(vmem, vmem),
        scratch_shapes=list(SCRATCH.values()),
        compiler_params=pltpu.CompilerParams(collective_id=0, has_side_effects=True, vmem_limit_bytes=56 * 2**20),
        name="solve",
    )(*args)


def solution(mesh):
    in_specs = (
        P("leaf", "blk", None),
        P("leaf", None, None, "blk"),
        P("leaf", "blk", None),
        P("leaf", None, None, "blk"),
        P("leaf", None, "blk"),
        P("leaf", None, "blk"),
        P("leaf", None),
    )
    out_specs = (P("leaf", None, "blk"), P("leaf", None, "blk"))
    return jax.shard_map(body, mesh=mesh, in_specs=in_specs, out_specs=out_specs, check_vma=False)
```

```python
import jax
import jax.numpy as jnp
from jax import lax
from jax.experimental import pallas as pl
from jax.experimental.pallas import tpu as pltpu
from jax.sharding import PartitionSpec as P

MESH = pl.DeviceIdType.MESH
F32 = jnp.float32
BF16 = jnp.bfloat16
NB = 8
LEV = 6


def tree_place(i):
    lev, half, run = 1, 1, 1
    for n in range(3):
        run = run * ((i // 2**n) % 2)
        lev = lev + run
        half = half + run * 2**n
    run = run * ((i // 8) % 2)
    return lev + 3 * run, half


def dot(a, b):
    return jnp.dot(a, b, preferred_element_type=F32)


def dot_t(a, b):
    return lax.dot_general(a, b, (((1,), (1,)), ((), ())), preferred_element_type=F32)


class Names:
    def __init__(self, names, refs):
        for name, ref in zip(names, refs, strict=True):
            setattr(self, name, ref)


def chunks(*lead, dtype=BF16):
    return pltpu.VMEM(lead + (64, 128), dtype)


def sems(*shape):
    return pltpu.SemaphoreType.DMA(shape) if shape else pltpu.SemaphoreType.DMA


def blocks(*shape):
    return pltpu.VMEM(shape, BF16)


SCRATCH = dict(
    li=blocks(1, 128, 1024), lc=blocks(1, 6, 1024, 128), si=blocks(1, 128, 1024), sc=blocks(1, 6, 1024, 128),
    SRI=chunks(1), ld=sems(6),
    LR=chunks(8), LY=chunks(dtype=F32), T1=chunks(8), TL=chunks(5, 8), RSL=chunks(5, 7), U=chunks(5, dtype=F32),
    UO1=chunks(5), UO2=chunks(5), UX=chunks(5, 2),
    s_lr=sems(), r_lr=sems(), s_t1=sems(), s_tl=sems(5), r_tl=sems(5), s_u1=sems(5), s_u2=sems(5), r_ux=sems(5),
    RX=chunks(16), SR=chunks(8), TC=chunks(8), TN=chunks(4, 8), RSS=chunks(4, 7), XF=chunks(6, 8),
    PB=chunks(8), RSB=chunks(7), SA=chunks(dtype=F32), SZ=chunks(dtype=F32), LA=chunks(dtype=F32),
    r_rx=sems(), s_sr=sems(), r_sr=sems(), s_tc=sems(), s_tn=sems(4), r_tn=sems(4),
    s_xf=sems(6), s_xb=sems(2), s_xo=sems(), r_xf=sems(6), s_pb=sems(), r_pb=sems(),
    IG=blocks(8, 128, 128), CG=blocks(2, 8, 1024, 128), VG=blocks(8, 128, 1024), M=blocks(2, 1024, 128), G=blocks(128, 1024),
    CL=blocks(8, 1024, 128), IL=blocks(8, 128, 128), ML=blocks(1024, 128),
    s_ig=sems(2), r_ig=sems(2), l_ig=sems(2), s_g=sems(4), ru_g=sems(4), rd_g=sems(4), rf_g=sems(4), rm_g=sems(4), l_g=sems(4),
    HM=blocks(1024, 128), HG5=blocks(128, 1024), HG6=blocks(128, 1024), H5=chunks(1), H6=chunks(1),
    s_hm=sems(), s_hr=sems(), s_hs=sems(), r_hm=sems(), r_hg5=sems(), r_hg6=sems(), r_h5=sems(), r_h6=sems(),
    RX5=chunks(16), RX6=chunks(16), SR5=chunks(8), SR6=chunks(8), TD=chunks(8), HU=chunks(2), Z5=chunks(dtype=F32),
    r_rx5=sems(), r_rx6=sems(), s_r5=sems(), r_r5=sems(), s_r6=sems(), r_r6=sems(), s_td=sems(), r_hu=sems(),
    HX=chunks(dtype=F32), HY=chunks(dtype=F32), s_hx=sems(), r_hx=sems(),
    LB=chunks(8), RLB=chunks(7), s_lb=sems(), r_lb=sems(),
)


def kernel(li_in, lc_in, si_in, sc_in, lr_in, sr_in, pat, lsol, ssol, *scratch):
    v = Names(SCRATCH, scratch)
    i = lax.axis_index("leaf")
    b = lax.axis_index("blk")
    x, z = i // 16, i % 16
    core = b % 2
    mate = b + 1 - 2 * core
    lev, half = tree_place(i)
    lev_next, _ = tree_place(i + 1)
    odd = i % 2
    even_slot = i - odd
    pair_slot = i + 1 - 2 * odd
    side = (i // (2 * half)) % 2
    parent = i + half - 2 * half * side
    kid0 = i - half // 2
    kid1 = i + half // 2
    gap = half // 4
    normal = lev <= 4
    host = lev == 4
    own5 = (z == 15) & (x % 2 == 0)
    own6 = (z == 15) & (x == 1)
    x_near = x + 1 - 2 * (x % 2)
    x_far = (x + 2) % 4
    near = x_near * 16 + 7
    far = x_far * 16 + 7
    host_a = (x - x % 2) * 16 + 7
    host_b = host_a + 16
    owner5 = (x - x % 2) * 16 + 15

    def send(src, dst, ssem, rsem, leaf, blk):
        pltpu.make_async_remote_copy(src_ref=src, dst_ref=dst, send_sem=ssem, recv_sem=rsem,
                                     device_id=(leaf, blk), device_id_type=MESH).start()

    def drain(ref, sem):
        pltpu.make_async_copy(ref, ref, sem).wait()

    def others(fn):
        def step(d, c):
            fn(d, (b + d) % NB)
            return c
        lax.fori_loop(1, NB, step, 0)

    def all_blk(fn):
        def step(d, c):
            fn((b + d) % NB)
            return c
        lax.fori_loop(0, NB, step, 0)

    def full(ref):
        return jnp.concatenate([ref[c] for c in range(NB)], axis=1)

    def spread(ref, value):
        for c in range(NB):
            ref[c] = value[:, c * 128:(c + 1) * 128].astype(BF16)

    def total(ref, count):
        acc = ref[0].astype(F32)
        for d in range(1, count):
            acc = acc + ref[d].astype(F32)
        return acc

    loads = [
        pltpu.make_async_copy(lr_in.at[0], v.LR.at[b], v.ld.at[0]),
        pltpu.make_async_copy(li_in, v.li, v.ld.at[1]),
        pltpu.make_async_copy(lc_in, v.lc, v.ld.at[2]),
        pltpu.make_async_copy(sr_in, v.SRI, v.ld.at[3]),
        pltpu.make_async_copy(si_in, v.si, v.ld.at[4]),
        pltpu.make_async_copy(sc_in, v.sc, v.ld.at[5]),
    ]
    for load in loads:
        load.start()

    barrier = pltpu.get_barrier_semaphore()

    def greet(leaf, blk):
        pl.semaphore_signal(barrier, inc=1, device_id=(leaf, blk), device_id_type=MESH)

    pair_is_kin = (lev == 2) | (lev == 3) | ((lev == 1) & ((side == 0) | (i % 8 == 2)))
    has_kids = (lev >= 2) & normal
    has_grandkids = (lev == 3) | (lev == 4)
    others(lambda d, t: greet(i, t))

    @pl.when(host)
    def _():
        greet(owner5, b)
        greet(31, b)
        greet(near, b)
        greet(far, b)

    @pl.when(own5)
    def _():
        greet(host_a, b)
        greet(host_b, b)

    @pl.when(own6)
    def _():
        for h in range(4):
            greet(16 * h + 7, b)

    @pl.when(~pair_is_kin)
    def _():
        greet(pair_slot, b)

    @pl.when(lev <= 3)
    def _():
        greet(parent, b)

    @pl.when(lev == 1)
    def _():
        greet(i - i % 8 + 3, b)

    @pl.when(lev == 2)
    def _():
        greet(i - z + 7, b)

    @pl.when(z == 13)
    def _():
        greet(i + 2, b)

    @pl.when(z == 15)
    def _():
        greet(i - 2, b)

    @pl.when(has_kids)
    def _():
        greet(kid0, b)
        greet(kid1, b)

    @pl.when(has_grandkids)
    def _():
        for kid in (kid0, kid1):
            greet(kid - gap, b)
            greet(kid + gap, b)

    peers = (7 + jnp.where(pair_is_kin, 0, 1) + jnp.where(lev <= 3, 1, 0) + jnp.where(lev <= 2, 1, 0)
             + jnp.where((z == 13) | (z == 15), 1, 0)
             + jnp.where(has_kids, 2, 0) + jnp.where(has_grandkids, 4, 0)
             + jnp.where(host, 4, 0) + jnp.where(own5, 2, 0) + jnp.where(own6, 4, 0))
    pl.semaphore_wait(barrier, peers)

    up, down = (b + 2) % NB, (b + 6) % NB
    relay_from, relay_to = (b + 6 + 4 * core) % NB, (b + 2 + 4 * core) % NB

    def gather_start(k, src, dst):
        pltpu.make_async_copy(src, dst.at[b], v.l_g.at[k]).start()
        send(src, dst.at[b], v.s_g.at[k], v.ru_g.at[k], i, up)
        send(src, dst.at[b], v.s_g.at[k], v.rd_g.at[k], i, down)
        send(src, dst.at[b], v.s_g.at[k], v.rm_g.at[k], i, mate)

    def gather_relay(k, dst):
        drain(dst.at[down], v.ru_g.at[k])
        drain(dst.at[up], v.rd_g.at[k])
        send(dst.at[relay_from], dst.at[relay_from], v.s_g.at[k], v.rf_g.at[k], i, relay_to)
        send(dst.at[down], dst.at[down], v.s_g.at[k], v.rm_g.at[k], i, mate)
        send(dst.at[up], dst.at[up], v.s_g.at[k], v.rm_g.at[k], i, mate)

    def gather_end(k, dst):
        opposite = (b + 4) % NB
        drain(dst.at[opposite], v.rf_g.at[k])
        send(dst.at[opposite], dst.at[opposite], v.s_g.at[k], v.rm_g.at[k], i, mate)
        drain(dst.at[pl.ds(0, 4)], v.rm_g.at[k])
        drain(dst.at[b], v.l_g.at[k])

    def columns_start(k, src, dst):
        pltpu.make_async_copy(src.at[0, :, pl.ds(pl.multiple_of(b * 128, 128), 128)], dst.at[b], v.l_ig.at[k]).start()
        others(lambda d, t: send(src.at[0, :, pl.ds(pl.multiple_of(t * 128, 128), 128)], dst.at[b],
                                 v.s_ig.at[k], v.r_ig.at[k], i, t))

    def columns_end(k, dst):
        drain(dst.at[pl.ds(0, 7)], v.r_ig.at[k])
        drain(dst.at[b], v.l_ig.at[k])

    def form_m(out, gathered, inverse):
        columns = inverse[...].reshape(1024, 128)

        def tile(r, c):
            rows = pl.ds(pl.multiple_of(r * 256, 256), 256)
            left = jnp.concatenate([gathered[s, rows, :] for s in range(NB)], axis=1)
            out[rows, :] = dot(left, columns).astype(BF16)
            return c
        lax.fori_loop(0, 4, tile, 0)

    def form_g():
        columns = v.IG[...].reshape(1024, 128)

        def tile(r, c):
            cols = pl.ds(pl.multiple_of(r * 256, 256), 256)
            right = v.VG[:, :, cols].reshape(1024, 256)
            v.G[:, cols] = lax.dot_general(columns, right, (((0,), (0,)), ((), ())),
                                           preferred_element_type=F32).astype(BF16)
            return c
        lax.fori_loop(0, 4, tile, 0)

    early = (lev == 3) | (lev == 4)

    def products_start0():
        columns_start(0, v.si, v.IG)
        gather_start(0, v.sc.at[0, lev], v.CG.at[0])

    def products_start1():
        gather_relay(0, v.CG.at[0])
        gather_start(1, v.sc.at[0, lev + 1], v.CG.at[1])

    def products_end():
        columns_end(0, v.IG)
        gather_end(0, v.CG.at[0])
        gather_relay(1, v.CG.at[1])
        form_m(v.M.at[0], v.CG.at[0], v.IG)
        gather_end(1, v.CG.at[1])
        form_m(v.M.at[1], v.CG.at[1], v.IG)

    def leaf_product():
        columns_start(1, v.li, v.IL)
        gather_start(3, v.lc.at[0, 0], v.CL)
        gather_relay(3, v.CL)
        columns_end(1, v.IL)
        gather_end(3, v.CL)
        form_m(v.ML, v.CL, v.IL)

    loads[0].wait()
    others(lambda d, t: send(v.LR.at[b], v.LR.at[b], v.s_lr, v.r_lr, i, t))
    for load in loads[1:]:
        load.wait()

    @pl.when(own5)
    def _():
        send(v.SRI, v.H5, v.s_hs, v.r_h5, host_a, b)
        send(v.SRI, v.H5, v.s_hs, v.r_h5, host_b, b)

    @pl.when(own6)
    def _():
        for h in range(4):
            send(v.SRI, v.H6, v.s_hs, v.r_h6, 16 * h + 7, b)

    drain(v.LR.at[pl.ds(0, 7)], v.r_lr)
    ly = dot_t(full(v.LR), v.li[0])
    v.LA[...] = ly
    lyb = ly.astype(BF16)
    spread(v.T1, dot_t(lyb, v.lc[0, 0]) * pat[0, 0].astype(F32))

    @pl.when(odd == 1)
    def _():
        all_blk(lambda t: send(v.T1.at[t], v.RX.at[NB + b], v.s_t1, v.r_rx, even_slot, t))

    @pl.when(odd == 0)
    def _():
        v.RX[b] = v.T1[b]
        others(lambda d, t: send(v.T1.at[t], v.RX.at[b], v.s_t1, v.r_rx, i, t))

    for a in range(2, LEV + 1):
        n = a - 2
        spread(v.TL.at[n], dot_t(lyb, v.lc[0, a - 1]) * pat[0, a - 1].astype(F32))
        others(lambda d, t, n=n: send(v.TL.at[n, t], v.RSL.at[n, d - 1], v.s_tl.at[n], v.r_tl.at[n], i, t))

    @pl.when(early)
    def _():
        products_start0()

    @pl.when(own5 | own6)
    def _():
        columns_start(0, v.si, v.IG)

        @pl.when(own5)
        def _():
            gather_start(0, v.sc.at[0, 5], v.CG.at[0])

        @pl.when(own6)
        def _():
            gather_start(2, v.si.at[0], v.VG)

    for a in range(2, LEV + 1):
        n = a - 2
        drain(v.RSL.at[n], v.r_tl.at[n])
        acc = v.TL[n, b].astype(F32) + total(v.RSL.at[n], 7)

        @pl.when(odd == 1)
        def _(n=n, acc=acc):
            v.UO1[n] = acc.astype(BF16)
            send(v.UO1.at[n], v.UX.at[n, 1], v.s_u1.at[n], v.r_ux.at[n], even_slot, b)
            v.U[n] = jnp.zeros((64, 128), F32)

        @pl.when(odd == 0)
        def _(n=n, acc=acc):
            v.U[n] = acc
            v.UX[n, 0] = jnp.zeros((64, 128), BF16)

    @pl.when(early)
    def _():
        products_start1()
        products_end()

        @pl.when(host & (x % 2 == 0))
        def _():
            drain(v.HM, v.r_hm)
            send(v.HM, v.HM, v.s_hr, v.r_hm, near, b)

        @pl.when(host & (x == 1))
        def _():
            drain(v.HG6, v.r_hg6)
            for h in (0, 2, 3):
                send(v.HG6, v.HG6, v.s_hr, v.r_hg6, 16 * h + 7, b)

    @pl.when(own5 | own6)
    def _():
        @pl.when(own5)
        def _():
            gather_relay(0, v.CG.at[0])
            gather_start(2, v.si.at[0], v.VG)

        @pl.when(own6)
        def _():
            gather_relay(2, v.VG)

        columns_end(0, v.IG)

        @pl.when(own5)
        def _():
            gather_end(0, v.CG.at[0])
            form_m(v.M.at[0], v.CG.at[0], v.IG)
            send(v.M.at[0], v.HM, v.s_hm, v.r_hm, host_a, b)
            gather_relay(2, v.VG)

        gather_end(2, v.VG)
        form_g()

        @pl.when(own5)
        def _():
            send(v.G, v.HG5, v.s_hm, v.r_hg5, host_a, b)

        @pl.when(own6)
        def _():
            send(v.G, v.HG6, v.s_hm, v.r_hg6, 23, b)

    @pl.when(z == 15)
    def _():
        leaf_product()

    def upward(n):
        @pl.when(lev == 1)
        def _():
            drain(v.UX.at[n, 1], v.r_ux.at[n])

        @pl.when(lev != 1)
        def _():
            drain(v.UX.at[n], v.r_ux.at[n])

        return v.U[n] + v.UX[n, 0].astype(F32) + v.UX[n, 1].astype(F32)

    def to_parent(n):
        others(lambda d, t: send(v.TC.at[t], v.RX.at[side * NB + b], v.s_tc, v.r_rx, parent, t))
        v.TC[b] = (v.TC[b].astype(F32) + upward(n)).astype(BF16)
        send(v.TC.at[b], v.RX.at[side * NB + b], v.s_tc, v.r_rx, parent, b)

    def over_blk(a, value):
        spread(v.TN.at[a - 3], value)
        others(lambda d, t: send(v.TN.at[a - 3, t], v.RSS.at[a - 3, d - 1], v.s_tn.at[a - 3], v.r_tn.at[a - 3], i, t))

    def far_part_start():
        spread(v.PB, dot(v.SA[...].astype(BF16), v.si[0]))
        others(lambda d, t: send(v.PB.at[t], v.RSB.at[d - 1], v.s_pb, v.r_pb, i, t))

    @pl.when(normal)
    def _():
        @pl.when(lev == 1)
        def _():
            drain(v.RX.at[pl.ds(0, 15)], v.r_rx)

        @pl.when(lev != 1)
        def _():
            drain(v.RX, v.r_rx)

        rs = v.SRI[0].astype(F32) - total(v.RX, 16)
        rsb = rs.astype(BF16)
        v.SR[b] = rsb

        @pl.when(early)
        def _():
            spread(v.TC, dot_t(rsb, v.M[0]))

            @pl.when(lev == 3)
            def _():
                to_parent(2)
                over_blk(5, dot_t(rsb, v.M[1]))

            @pl.when(lev == 4)
            def _():
                v.TC[b] = (v.TC[b].astype(F32) + upward(3)).astype(BF16)
                mine = (x % 2) * NB + b
                v.RX5[mine] = v.TC[b]
                all_blk(lambda t: send(v.TC.at[t], v.RX5.at[mine], v.s_tc, v.r_rx5, near, t))
                others(lambda d, t: send(v.TC.at[t], v.RX5.at[mine], v.s_tc, v.r_rx5, i, t))
                over_blk(6, dot_t(rsb, v.M[1]))

        others(lambda d, t: send(v.SR.at[b], v.SR.at[b], v.s_sr, v.r_sr, i, t))
        drain(v.SR.at[pl.ds(0, 7)], v.r_sr)
        sy = dot_t(full(v.SR), v.si[0])
        v.SA[...] = sy
        syb = sy.astype(BF16)

        for a in (2, 3):
            @pl.when(lev == a - 1)
            def _(a=a):
                spread(v.TC, dot_t(syb, v.sc[0, a - 1]))
                to_parent(a - 2)

        for a in range(3, LEV + 1):
            @pl.when((lev < a - 1) & ((lev <= 2) | ((lev == 3) & (a == 6))))
            def _(a=a):
                over_blk(a, dot_t(syb, v.sc[0, a - 1]))

        for a in range(3, LEV + 1):
            n = a - 2

            @pl.when(lev < a - 1)
            def _(a=a, n=n):
                drain(v.RSS.at[a - 3], v.r_tn.at[a - 3])
                acc = v.TN[a - 3, b].astype(F32) + total(v.RSS.at[a - 3], 7) + upward(n)
                v.UO2[n] = acc.astype(BF16)

                @pl.when(lev <= 3)
                def _():
                    send(v.UO2.at[n], v.UX.at[n, side], v.s_u2.at[n], v.r_ux.at[n], parent, b)

                if a == 6:
                    @pl.when(lev == 4)
                    def _():
                        v.HU[x % 2] = v.UO2[n]
                        send(v.UO2.at[n], v.HU.at[x % 2], v.s_u2.at[n], v.r_hu, near, b)

        @pl.when(lev == 4)
        def _():
            far_part_start()

        @pl.when(lev <= 2)
        def _():
            products_start0()
            products_start1()
            products_end()

        @pl.when(lev <= 3)
        def _():
            leaf_product()

    def leaf_part(a):
        v.LA[...] = v.LA[...] - pat[0, a - 1].astype(F32) * dot(full(v.XF.at[a - 1]), v.lc[0, a - 1])

    def to_slots(n, sem, *slots):
        def each(t):
            for slot in slots:
                send(v.XF.at[n, b], v.XF.at[n, b], sem, v.r_xf.at[n], slot, t)
        all_blk(each)

    def to_blk(n, sem):
        others(lambda d, t: send(v.XF.at[n, b], v.XF.at[n, b], sem, v.r_xf.at[n], i, t))

    def finish():
        drain(v.RSB, v.r_pb)
        sol = v.PB[b].astype(F32) + total(v.RSB, 7) - v.SZ[...]
        own = lev - 1
        v.XF[own, b] = sol.astype(BF16)

        @pl.when(lev >= 2)
        def _():
            to_slots(own, v.s_xo, kid0, kid1)

        @pl.when(lev == 1)
        def _():
            to_slots(own, v.s_xo, pair_slot)

        to_blk(own, v.s_pb)

        @pl.when(lev >= 3)
        def _():
            to_slots(own, v.s_xo, kid0 + gap, kid1 - gap)
            to_slots(own, v.s_xo, kid0 - gap, kid1 + gap)

        @pl.when(lev == 2)
        def _():
            to_slots(own, v.s_xo, i + 2)

        ssol[0] = sol

    @pl.when(host)
    def _():
        drain(v.RX5.at[pl.ds(0, 15)], v.r_rx5)
        drain(v.H5, v.r_h5)
        rs = (v.H5[0].astype(F32) - total(v.RX5, 16)).astype(BF16)
        v.SR5[b] = rs

        @pl.when(x % 2 == 1)
        def _():
            drain(v.HM, v.r_hm)

        spread(v.TD, dot_t(rs, v.HM[...]))
        drain(v.HU.at[0], v.r_hu)
        v.TD[b] = (v.TD[b].astype(F32) + v.HU[0].astype(F32) + v.HU[1].astype(F32)).astype(BF16)
        mine = (x // 2) * NB + b
        v.RX6[mine] = v.TD[b]
        all_blk(lambda t: send(v.TD.at[t], v.RX6.at[mine], v.s_td, v.r_rx6, far, t))
        others(lambda d, t: send(v.TD.at[t], v.RX6.at[mine], v.s_td, v.r_rx6, i, t))
        others(lambda d, t: send(v.SR5.at[b], v.SR5.at[b], v.s_r5, v.r_r5, i, t))
        drain(v.SR5.at[pl.ds(0, 7)], v.r_r5)
        drain(v.HG5, v.r_hg5)

        @pl.when(x % 2 == 0)
        def _():
            send(v.HG5, v.HG5, v.s_hr, v.r_hg5, near, b)

        v.Z5[...] = dot_t(full(v.SR5), v.HG5[...])

        drain(v.RX6.at[pl.ds(0, 15)], v.r_rx6)
        drain(v.H6, v.r_h6)
        v.SR6[b] = (v.H6[0].astype(F32) - total(v.RX6, 16)).astype(BF16)
        others(lambda d, t: send(v.SR6.at[b], v.SR6.at[b], v.s_r6, v.r_r6, i, t))

        @pl.when(x != 1)
        def _():
            drain(v.HG6, v.r_hg6)

        drain(v.SR6.at[pl.ds(0, 7)], v.r_r6)
        sol6 = dot_t(full(v.SR6), v.HG6[...])
        v.XF[5, b] = sol6.astype(BF16)
        to_blk(5, v.s_xb.at[1])
        to_slots(5, v.s_xf.at[5], kid0, kid1)
        drain(v.XF.at[5, pl.ds(0, 7)], v.r_xf.at[5])
        x6 = full(v.XF.at[5])
        sol5 = v.Z5[...] - dot(x6, v.HM[...])
        v.XF[4, b] = sol5.astype(BF16)
        to_blk(4, v.s_xb.at[0])
        to_slots(4, v.s_xf.at[4], kid0, kid1)
        part = dot(x6, v.M[1])

        @pl.when(x == 1)
        def _():
            v.HX[...] = sol6
            send(v.HX, v.HY, v.s_hx, v.r_hx, 31, b)

        @pl.when(x % 2 == 0)
        def _():
            v.HX[...] = sol5
            send(v.HX, v.HY, v.s_hx, v.r_hx, owner5, b)

        leaf_part(6)
        drain(v.XF.at[4, pl.ds(0, 7)], v.r_xf.at[4])
        v.SZ[...] = part + dot(full(v.XF.at[4]), v.M[0])
        finish()
        leaf_part(5)
        leaf_product()

    for a in range(LEV, 1, -1):
        @pl.when((lev <= 3) & (lev < a))
        def _(a=a):
            n = a - 1
            drain(v.XF.at[n], v.r_xf.at[n])

            @pl.when((lev >= 2) & (a >= lev + 2))
            def _():
                to_slots(n, v.s_xf.at[n], kid0, kid1)

            if a >= 3:
                @pl.when((lev == 1) & (a < lev_next))
                def _():
                    to_slots(n, v.s_xf.at[n], pair_slot)

            @pl.when(a >= lev + 3)
            def _():
                v.SA[...] = v.SA[...] - dot(full(v.XF.at[n]), v.sc[0, n])

            @pl.when(a == lev + 3)
            def _():
                far_part_start()

            @pl.when(a == lev + 2)
            def _():
                v.SZ[...] = dot(full(v.XF.at[n]), v.M[1])

            @pl.when(a == lev + 1)
            def _():
                v.SZ[...] = v.SZ[...] + dot(full(v.XF.at[n]), v.M[0])
                finish()

            leaf_part(a)

    @pl.when((lev >= 2) & normal)
    def _():
        drain(v.XF.at[lev - 1, pl.ds(0, 7)], v.r_xf.at[lev - 1])
        leaf_part(lev)

    @pl.when(own5 | own6)
    def _():
        drain(v.HY, v.r_hx)
        ssol[0] = v.HY[...]

    @pl.when((z == 15) & (x == 3))
    def _():
        ssol[0] = jnp.zeros((64, 128), F32)

    for a in range(LEV, 1, -1):
        @pl.when(a < lev)
        def _(a=a):
            drain(v.XF.at[a - 1], v.r_xf.at[a - 1])
            leaf_part(a)

    spread(v.LB, dot(v.LA[...].astype(BF16), v.li[0]))
    others(lambda d, t: send(v.LB.at[t], v.RLB.at[d - 1], v.s_lb, v.r_lb, i, t))

    @pl.when(lev == 1)
    def _():
        drain(v.XF.at[0, pl.ds(0, 7)], v.r_xf.at[0])

    @pl.when(lev != 1)
    def _():
        drain(v.XF.at[0], v.r_xf.at[0])

    last = pat[0, 0].astype(F32) * dot(full(v.XF.at[0]), v.ML[...])
    drain(v.RLB, v.r_lb)
    lsol[0] = v.LB[b].astype(F32) + total(v.RLB, 7) - last

    seven = pl.ds(0, 7)
    drain(v.LR.at[seven], v.s_lr)

    @pl.when(odd == 1)
    def _():
        drain(v.T1, v.s_t1)
        for n in range(LEV - 1):
            drain(v.UO1.at[n], v.s_u1.at[n])

    @pl.when(odd == 0)
    def _():
        drain(v.T1.at[seven], v.s_t1)

    for n in range(LEV - 1):
        drain(v.TL.at[n, seven], v.s_tl.at[n])
    drain(v.LB.at[seven], v.s_lb)
    drain(v.IL.at[seven], v.s_ig.at[1])
    drain(v.CL.at[seven], v.s_g.at[3])

    @pl.when(normal)
    def _():
        drain(v.SR.at[seven], v.s_sr)
        drain(v.RX.at[pl.ds(0, 14)], v.s_pb)
        drain(v.IG.at[seven], v.s_ig.at[0])
        drain(v.CG.at[0, seven], v.s_g.at[0])
        drain(v.CG.at[1, seven], v.s_g.at[1])

        @pl.when(lev >= 3)
        def _():
            drain(v.XF, v.s_xo)

        @pl.when(lev == 2)
        def _():
            drain(v.XF.at[pl.ds(0, 3)], v.s_xo)

        @pl.when(lev == 1)
        def _():
            drain(v.PB, v.s_xo)

        @pl.when(lev <= 3)
        def _():
            drain(v.TC, v.s_tc)

        for a in range(3, LEV + 1):
            @pl.when(lev < a - 1)
            def _(a=a):
                drain(v.TN.at[a - 3, seven], v.s_tn.at[a - 3])
                drain(v.UO2.at[a - 2], v.s_u2.at[a - 2])

    @pl.when(host)
    def _():
        drain(v.RX.at[pl.ds(0, 15)], v.s_tc)
        drain(v.RX.at[pl.ds(0, 15)], v.s_td)
        drain(v.SR5.at[seven], v.s_r5)
        drain(v.SR6.at[seven], v.s_r6)
        for n in range(2):
            drain(v.RX, v.s_xf.at[4 + n])
            drain(v.SR5.at[seven], v.s_xb.at[n])

        @pl.when(x < 3)
        def _():
            drain(v.HX, v.s_hx)

    @pl.when(own5 | own6)
    def _():
        drain(v.IG.at[seven], v.s_ig.at[0])
        drain(v.VG.at[seven], v.s_g.at[2])

    @pl.when(own5)
    def _():
        drain(v.CG.at[0, pl.ds(0, 2)], v.s_hm)
        drain(v.CG.at[0, seven], v.s_g.at[0])
        drain(v.PB.at[pl.ds(0, 2)], v.s_hs)

    @pl.when(own6)
    def _():
        drain(v.CG.at[0, 0], v.s_hm)
        drain(v.PB.at[pl.ds(0, 4)], v.s_hs)

    @pl.when(host & (x % 2 == 0))
    def _():
        drain(v.CG.at[0, pl.ds(0, 2)], v.s_hr)

    @pl.when(host & (x == 1))
    def _():
        drain(v.CG.at[0, pl.ds(0, 3)], v.s_hr)

    for a in range(LEV, 2, -1):
        @pl.when((lev + 2 <= a) & ((lev == 2) | (lev == 3)))
        def _(a=a):
            drain(v.RX, v.s_xf.at[a - 1])

        @pl.when((lev == 1) & (a < lev_next))
        def _(a=a):
            drain(v.PB, v.s_xf.at[a - 1])


def body(*args):
    vmem = pl.BlockSpec(memory_space=pltpu.VMEM)
    out = jax.ShapeDtypeStruct((1, 64, 128), F32)
    return pl.pallas_call(
        kernel,
        out_shape=(out, out),
        in_specs=[pl.BlockSpec(memory_space=pl.ANY)] * 6 + [pl.BlockSpec(memory_space=pltpu.SMEM)],
        out_specs=(vmem, vmem),
        scratch_shapes=list(SCRATCH.values()),
        compiler_params=pltpu.CompilerParams(collective_id=0, has_side_effects=True, vmem_limit_bytes=56 * 2**20),
        name="solve",
    )(*args)


def solution(mesh):
    in_specs = (
        P("leaf", "blk", None),
        P("leaf", None, None, "blk"),
        P("leaf", "blk", None),
        P("leaf", None, None, "blk"),
        P("leaf", None, "blk"),
        P("leaf", None, "blk"),
        P("leaf", None),
    )
    out_specs = (P("leaf", None, "blk"), P("leaf", None, "blk"))
    return jax.shard_map(body, mesh=mesh, in_specs=in_specs, out_specs=out_specs, check_vma=False)
```

```python
import jax
import jax.numpy as jnp
from jax import lax
from jax.experimental import pallas as pl
from jax.experimental.pallas import tpu as pltpu
from jax.sharding import PartitionSpec as P

MESH = pl.DeviceIdType.MESH
F32 = jnp.float32
BF16 = jnp.bfloat16
NB = 8
LEV = 6


def tree_place(i):
    lev, half, run = 1, 1, 1
    for n in range(3):
        run = run * ((i // 2**n) % 2)
        lev = lev + run
        half = half + run * 2**n
    run = run * ((i // 8) % 2)
    return lev + 3 * run, half


def dot(a, b):
    return jnp.dot(a, b, preferred_element_type=F32)


def dot_t(a, b):
    return lax.dot_general(a, b, (((1,), (1,)), ((), ())), preferred_element_type=F32)


class Names:
    def __init__(self, names, refs):
        for name, ref in zip(names, refs, strict=True):
            setattr(self, name, ref)


def chunks(*lead, dtype=BF16):
    return pltpu.VMEM(lead + (64, 128), dtype)


def sems(*shape):
    return pltpu.SemaphoreType.DMA(shape) if shape else pltpu.SemaphoreType.DMA


def blocks(*shape):
    return pltpu.VMEM(shape, BF16)


SCRATCH = dict(
    li=blocks(1, 128, 1024), lc=blocks(1, 6, 1024, 128), si=blocks(1, 128, 1024), sc=blocks(1, 6, 1024, 128),
    SRI=chunks(1), ld=sems(6),
    LR=chunks(8), LY=chunks(dtype=F32), T1=chunks(8), TL=chunks(5, 8), RSL=chunks(5, 7), U=chunks(5, dtype=F32),
    UO1=chunks(5), UO2=chunks(5), UX=chunks(5, 2),
    s_lr=sems(), r_lr=sems(), s_t1=sems(), s_tl=sems(5), r_tl=sems(5), s_u1=sems(5), s_u2=sems(5), r_ux=sems(5),
    RX=chunks(16), SR=chunks(8), TC=chunks(8), TN=chunks(4, 8), RSS=chunks(4, 7), XF=chunks(6, 8),
    PB=chunks(8), RSB=chunks(7), SA=chunks(dtype=F32), SZ=chunks(dtype=F32), LA=chunks(dtype=F32),
    r_rx=sems(), s_sr=sems(), r_sr=sems(), s_tc=sems(), s_tn=sems(4), r_tn=sems(4),
    s_xf=sems(6), s_xb=sems(2), s_xo=sems(), r_xf=sems(6), s_pb=sems(), r_pb=sems(),
    IG=blocks(8, 128, 128), CG=blocks(2, 8, 1024, 128), VG=blocks(8, 128, 1024), M=blocks(2, 1024, 128), G=blocks(128, 1024),
    CL=blocks(8, 1024, 128), IL=blocks(8, 128, 128), ML=blocks(1024, 128),
    s_ig=sems(2), r_ig=sems(2), l_ig=sems(2), s_g=sems(4), ru_g=sems(4), rd_g=sems(4), rf_g=sems(4), rm_g=sems(4), l_g=sems(4),
    HM=blocks(1024, 128), HI5=blocks(1, 128, 1024), HG6=blocks(128, 1024), H5=chunks(1), H6=chunks(1),
    s_hm=sems(), s_hr=sems(), s_hs=sems(), r_hm=sems(), r_hi5=sems(), r_hg6=sems(), r_h5=sems(), r_h6=sems(),
    RX5=chunks(16), RX6=chunks(16), SR5=chunks(8), SR6=chunks(8), TD=chunks(8), HU=chunks(2), PB5=chunks(8), RSB5=chunks(7), s_p5=sems(), r_p5=sems(),
    r_rx5=sems(), r_rx6=sems(), s_r5=sems(), r_r5=sems(), s_r6=sems(), r_r6=sems(), s_td=sems(), r_hu=sems(),
    HX=chunks(dtype=F32), HY=chunks(dtype=F32), s_hx=sems(), r_hx=sems(),
    LB=chunks(8), RLB=chunks(7), s_lb=sems(), r_lb=sems(),
)


def kernel(li_in, lc_in, si_in, sc_in, lr_in, sr_in, pat, lsol, ssol, *scratch):
    v = Names(SCRATCH, scratch)
    i = lax.axis_index("leaf")
    b = lax.axis_index("blk")
    x, z = i // 16, i % 16
    core = b % 2
    mate = b + 1 - 2 * core
    lev, half = tree_place(i)
    lev_next, _ = tree_place(i + 1)
    odd = i % 2
    even_slot = i - odd
    pair_slot = i + 1 - 2 * odd
    side = (i // (2 * half)) % 2
    parent = i + half - 2 * half * side
    kid0 = i - half // 2
    kid1 = i + half // 2
    gap = half // 4
    normal = lev <= 4
    host = lev == 4
    own5 = (z == 15) & (x % 2 == 0)
    own6 = (z == 15) & (x == 1)
    x_near = x + 1 - 2 * (x % 2)
    x_far = (x + 2) % 4
    near = x_near * 16 + 7
    far = x_far * 16 + 7
    host_a = (x - x % 2) * 16 + 7
    host_b = host_a + 16
    owner5 = (x - x % 2) * 16 + 15

    def send(src, dst, ssem, rsem, leaf, blk):
        pltpu.make_async_remote_copy(src_ref=src, dst_ref=dst, send_sem=ssem, recv_sem=rsem,
                                     device_id=(leaf, blk), device_id_type=MESH).start()

    def drain(ref, sem):
        pltpu.make_async_copy(ref, ref, sem).wait()

    def offset(k):
        return 4 + ((k + 1) // 2) * (2 * (k % 2) - 1)

    def others(fn):
        def step(k, c):
            d = offset(k)
            fn(d, (b + d) % NB)
            return c
        lax.fori_loop(0, NB - 1, step, 0)

    def all_blk(fn):
        def step(k, c):
            fn((b + offset(k)) % NB)
            return c
        lax.fori_loop(0, NB, step, 0)

    def full(ref):
        return jnp.concatenate([ref[c] for c in range(NB)], axis=1)

    def spread(ref, value):
        for c in range(NB):
            ref[c] = value[:, c * 128:(c + 1) * 128].astype(BF16)

    def total(ref, count):
        acc = ref[0].astype(F32)
        for d in range(1, count):
            acc = acc + ref[d].astype(F32)
        return acc

    loads = [
        pltpu.make_async_copy(lr_in.at[0], v.LR.at[b], v.ld.at[0]),
        pltpu.make_async_copy(li_in, v.li, v.ld.at[1]),
        pltpu.make_async_copy(lc_in, v.lc, v.ld.at[2]),
        pltpu.make_async_copy(sr_in, v.SRI, v.ld.at[3]),
        pltpu.make_async_copy(si_in, v.si, v.ld.at[4]),
        pltpu.make_async_copy(sc_in, v.sc, v.ld.at[5]),
    ]
    for load in loads:
        load.start()

    barrier = pltpu.get_barrier_semaphore()

    def greet(leaf, blk):
        pl.semaphore_signal(barrier, inc=1, device_id=(leaf, blk), device_id_type=MESH)

    pair_is_kin = (lev == 2) | (lev == 3) | ((lev == 1) & ((side == 0) | (i % 8 == 2)))
    has_kids = (lev >= 2) & normal
    has_grandkids = (lev == 3) | (lev == 4)
    others(lambda d, t: greet(i, t))

    @pl.when(host)
    def _():
        greet(owner5, b)
        greet(31, b)
        greet(near, b)
        greet(far, b)

    @pl.when(own5)
    def _():
        greet(host_a, b)
        greet(host_b, b)

    @pl.when(own6)
    def _():
        for h in range(4):
            greet(16 * h + 7, b)

    @pl.when(~pair_is_kin)
    def _():
        greet(pair_slot, b)

    @pl.when(lev <= 3)
    def _():
        greet(parent, b)

    @pl.when(lev == 1)
    def _():
        greet(i - i % 8 + 3, b)

    @pl.when(lev == 2)
    def _():
        greet(i - z + 7, b)

    @pl.when(z == 13)
    def _():
        greet(i + 2, b)

    @pl.when(z == 15)
    def _():
        greet(i - 2, b)

    @pl.when(has_kids)
    def _():
        greet(kid0, b)
        greet(kid1, b)

    @pl.when(has_grandkids)
    def _():
        for kid in (kid0, kid1):
            greet(kid - gap, b)
            greet(kid + gap, b)

    peers = (7 + jnp.where(pair_is_kin, 0, 1) + jnp.where(lev <= 3, 1, 0) + jnp.where(lev <= 2, 1, 0)
             + jnp.where((z == 13) | (z == 15), 1, 0)
             + jnp.where(has_kids, 2, 0) + jnp.where(has_grandkids, 4, 0)
             + jnp.where(host, 4, 0) + jnp.where(own5, 2, 0) + jnp.where(own6, 4, 0))
    pl.semaphore_wait(barrier, peers)

    up, down = (b + 2) % NB, (b + 6) % NB
    relay_from, relay_to = (b + 6 + 4 * core) % NB, (b + 2 + 4 * core) % NB

    def gather_start(k, src, dst):
        pltpu.make_async_copy(src, dst.at[b], v.l_g.at[k]).start()
        send(src, dst.at[b], v.s_g.at[k], v.ru_g.at[k], i, up)
        send(src, dst.at[b], v.s_g.at[k], v.rd_g.at[k], i, down)
        send(src, dst.at[b], v.s_g.at[k], v.rm_g.at[k], i, mate)

    def gather_relay(k, dst):
        drain(dst.at[down], v.ru_g.at[k])
        drain(dst.at[up], v.rd_g.at[k])
        send(dst.at[relay_from], dst.at[relay_from], v.s_g.at[k], v.rf_g.at[k], i, relay_to)
        send(dst.at[down], dst.at[down], v.s_g.at[k], v.rm_g.at[k], i, mate)
        send(dst.at[up], dst.at[up], v.s_g.at[k], v.rm_g.at[k], i, mate)

    def gather_end(k, dst):
        opposite = (b + 4) % NB
        drain(dst.at[opposite], v.rf_g.at[k])
        send(dst.at[opposite], dst.at[opposite], v.s_g.at[k], v.rm_g.at[k], i, mate)
        drain(dst.at[pl.ds(0, 4)], v.rm_g.at[k])
        drain(dst.at[b], v.l_g.at[k])

    def columns_start(k, src, dst):
        pltpu.make_async_copy(src.at[0, :, pl.ds(pl.multiple_of(b * 128, 128), 128)], dst.at[b], v.l_ig.at[k]).start()
        others(lambda d, t: send(src.at[0, :, pl.ds(pl.multiple_of(t * 128, 128), 128)], dst.at[b],
                                 v.s_ig.at[k], v.r_ig.at[k], i, t))

    def columns_end(k, dst):
        drain(dst.at[pl.ds(0, 7)], v.r_ig.at[k])
        drain(dst.at[b], v.l_ig.at[k])

    def form_m(out, gathered, inverse):
        columns = inverse[...].reshape(1024, 128)

        def tile(r, c):
            rows = pl.ds(pl.multiple_of(r * 256, 256), 256)
            left = jnp.concatenate([gathered[s, rows, :] for s in range(NB)], axis=1)
            out[rows, :] = dot(left, columns).astype(BF16)
            return c
        lax.fori_loop(0, 4, tile, 0)

    def form_g():
        columns = v.IG[...].reshape(1024, 128)

        def tile(r, c):
            cols = pl.ds(pl.multiple_of(r * 256, 256), 256)
            right = v.VG[:, :, cols].reshape(1024, 256)
            v.G[:, cols] = lax.dot_general(columns, right, (((0,), (0,)), ((), ())),
                                           preferred_element_type=F32).astype(BF16)
            return c
        lax.fori_loop(0, 4, tile, 0)

    early = (lev == 3) | (lev == 4)

    def products_start0():
        columns_start(0, v.si, v.IG)
        gather_start(0, v.sc.at[0, lev], v.CG.at[0])

    def products_start1():
        gather_relay(0, v.CG.at[0])
        gather_start(1, v.sc.at[0, lev + 1], v.CG.at[1])

    def products_end():
        columns_end(0, v.IG)
        gather_end(0, v.CG.at[0])
        gather_relay(1, v.CG.at[1])
        form_m(v.M.at[0], v.CG.at[0], v.IG)
        gather_end(1, v.CG.at[1])
        form_m(v.M.at[1], v.CG.at[1], v.IG)

    def leaf_product():
        columns_start(1, v.li, v.IL)
        gather_start(3, v.lc.at[0, 0], v.CL)
        gather_relay(3, v.CL)
        columns_end(1, v.IL)
        gather_end(3, v.CL)
        form_m(v.ML, v.CL, v.IL)

    loads[0].wait()
    others(lambda d, t: send(v.LR.at[b], v.LR.at[b], v.s_lr, v.r_lr, i, t))
    for load in loads[1:]:
        load.wait()

    @pl.when(own5)
    def _():
        send(v.SRI, v.H5, v.s_hs, v.r_h5, host_a, b)
        send(v.SRI, v.H5, v.s_hs, v.r_h5, host_b, b)

    @pl.when(own6)
    def _():
        for h in range(4):
            send(v.SRI, v.H6, v.s_hs, v.r_h6, 16 * h + 7, b)

    drain(v.LR.at[pl.ds(0, 7)], v.r_lr)
    ly = dot_t(full(v.LR), v.li[0])
    v.LA[...] = ly
    lyb = ly.astype(BF16)
    spread(v.T1, dot_t(lyb, v.lc[0, 0]) * pat[0, 0].astype(F32))

    @pl.when(odd == 1)
    def _():
        all_blk(lambda t: send(v.T1.at[t], v.RX.at[NB + b], v.s_t1, v.r_rx, even_slot, t))

    @pl.when(odd == 0)
    def _():
        v.RX[b] = v.T1[b]
        others(lambda d, t: send(v.T1.at[t], v.RX.at[b], v.s_t1, v.r_rx, i, t))

    for a in range(2, LEV + 1):
        n = a - 2
        spread(v.TL.at[n], dot_t(lyb, v.lc[0, a - 1]) * pat[0, a - 1].astype(F32))
        others(lambda d, t, n=n: send(v.TL.at[n, t], v.RSL.at[n, d - 1], v.s_tl.at[n], v.r_tl.at[n], i, t))

    @pl.when(early)
    def _():
        products_start0()

    @pl.when(own5 | own6)
    def _():
        columns_start(0, v.si, v.IG)

        @pl.when(own5)
        def _():
            gather_start(0, v.sc.at[0, 5], v.CG.at[0])
            send(v.si, v.HI5, v.s_hm, v.r_hi5, host_a, b)

        @pl.when(own6)
        def _():
            gather_start(2, v.si.at[0], v.VG)

    for a in range(2, LEV + 1):
        n = a - 2
        drain(v.RSL.at[n], v.r_tl.at[n])
        acc = v.TL[n, b].astype(F32) + total(v.RSL.at[n], 7)

        @pl.when(odd == 1)
        def _(n=n, acc=acc):
            v.UO1[n] = acc.astype(BF16)
            send(v.UO1.at[n], v.UX.at[n, 1], v.s_u1.at[n], v.r_ux.at[n], even_slot, b)
            v.U[n] = jnp.zeros((64, 128), F32)

        @pl.when(odd == 0)
        def _(n=n, acc=acc):
            v.U[n] = acc
            v.UX[n, 0] = jnp.zeros((64, 128), BF16)

    @pl.when(early)
    def _():
        products_start1()
        products_end()

        @pl.when(host & (x % 2 == 0))
        def _():
            drain(v.HI5, v.r_hi5)
            send(v.HI5, v.HI5, v.s_hr, v.r_hi5, near, b)
            drain(v.HM, v.r_hm)
            send(v.HM, v.HM, v.s_hr, v.r_hm, near, b)

        @pl.when(host & (x == 1))
        def _():
            drain(v.HG6, v.r_hg6)
            for h in (0, 2, 3):
                send(v.HG6, v.HG6, v.s_hr, v.r_hg6, 16 * h + 7, b)

    @pl.when(own5 | own6)
    def _():
        @pl.when(own5)
        def _():
            gather_relay(0, v.CG.at[0])

        @pl.when(own6)
        def _():
            gather_relay(2, v.VG)

        columns_end(0, v.IG)

        @pl.when(own5)
        def _():
            gather_end(0, v.CG.at[0])
            form_m(v.M.at[0], v.CG.at[0], v.IG)
            send(v.M.at[0], v.HM, v.s_hm, v.r_hm, host_a, b)

        @pl.when(own6)
        def _():
            gather_end(2, v.VG)
            form_g()
            send(v.G, v.HG6, v.s_hm, v.r_hg6, 23, b)

    @pl.when(z == 15)
    def _():
        leaf_product()

    def upward(n):
        @pl.when(lev == 1)
        def _():
            drain(v.UX.at[n, 1], v.r_ux.at[n])

        @pl.when(lev != 1)
        def _():
            drain(v.UX.at[n], v.r_ux.at[n])

        return v.U[n] + v.UX[n, 0].astype(F32) + v.UX[n, 1].astype(F32)

    def to_parent(n):
        others(lambda d, t: send(v.TC.at[t], v.RX.at[side * NB + b], v.s_tc, v.r_rx, parent, t))
        v.TC[b] = (v.TC[b].astype(F32) + upward(n)).astype(BF16)
        send(v.TC.at[b], v.RX.at[side * NB + b], v.s_tc, v.r_rx, parent, b)

    def over_blk(a, value):
        spread(v.TN.at[a - 3], value)
        others(lambda d, t: send(v.TN.at[a - 3, t], v.RSS.at[a - 3, d - 1], v.s_tn.at[a - 3], v.r_tn.at[a - 3], i, t))

    def far_part_start():
        spread(v.PB, dot(v.SA[...].astype(BF16), v.si[0]))
        others(lambda d, t: send(v.PB.at[t], v.RSB.at[d - 1], v.s_pb, v.r_pb, i, t))

    @pl.when(normal)
    def _():
        @pl.when(lev == 1)
        def _():
            drain(v.RX.at[pl.ds(0, 15)], v.r_rx)

        @pl.when(lev != 1)
        def _():
            drain(v.RX, v.r_rx)

        rs = v.SRI[0].astype(F32) - total(v.RX, 16)
        rsb = rs.astype(BF16)
        v.SR[b] = rsb

        @pl.when(early)
        def _():
            spread(v.TC, dot_t(rsb, v.M[0]))

            @pl.when(lev == 3)
            def _():
                to_parent(2)
                over_blk(5, dot_t(rsb, v.M[1]))

            @pl.when(lev == 4)
            def _():
                v.TC[b] = (v.TC[b].astype(F32) + upward(3)).astype(BF16)
                mine = (x % 2) * NB + b
                v.RX5[mine] = v.TC[b]
                all_blk(lambda t: send(v.TC.at[t], v.RX5.at[mine], v.s_tc, v.r_rx5, near, t))
                others(lambda d, t: send(v.TC.at[t], v.RX5.at[mine], v.s_tc, v.r_rx5, i, t))
                over_blk(6, dot_t(rsb, v.M[1]))

        others(lambda d, t: send(v.SR.at[b], v.SR.at[b], v.s_sr, v.r_sr, i, t))
        drain(v.SR.at[pl.ds(0, 7)], v.r_sr)
        sy = dot_t(full(v.SR), v.si[0])
        v.SA[...] = sy
        syb = sy.astype(BF16)

        for a in (2, 3):
            @pl.when(lev == a - 1)
            def _(a=a):
                spread(v.TC, dot_t(syb, v.sc[0, a - 1]))
                to_parent(a - 2)

        for a in range(3, LEV + 1):
            @pl.when((lev < a - 1) & ((lev <= 2) | ((lev == 3) & (a == 6))))
            def _(a=a):
                over_blk(a, dot_t(syb, v.sc[0, a - 1]))

        for a in range(3, LEV + 1):
            n = a - 2

            @pl.when(lev < a - 1)
            def _(a=a, n=n):
                drain(v.RSS.at[a - 3], v.r_tn.at[a - 3])
                acc = v.TN[a - 3, b].astype(F32) + total(v.RSS.at[a - 3], 7) + upward(n)
                v.UO2[n] = acc.astype(BF16)

                @pl.when(lev <= 3)
                def _():
                    send(v.UO2.at[n], v.UX.at[n, side], v.s_u2.at[n], v.r_ux.at[n], parent, b)

                if a == 6:
                    @pl.when(lev == 4)
                    def _():
                        v.HU[x % 2] = v.UO2[n]
                        send(v.UO2.at[n], v.HU.at[x % 2], v.s_u2.at[n], v.r_hu, near, b)

        @pl.when(lev == 4)
        def _():
            far_part_start()

        @pl.when(lev <= 2)
        def _():
            products_start0()
            products_start1()
            products_end()

        @pl.when(lev <= 3)
        def _():
            leaf_product()

    def leaf_part(a):
        v.LA[...] = v.LA[...] - pat[0, a - 1].astype(F32) * dot(full(v.XF.at[a - 1]), v.lc[0, a - 1])

    def to_slots(n, sem, *slots):
        def each(t):
            for slot in slots:
                send(v.XF.at[n, b], v.XF.at[n, b], sem, v.r_xf.at[n], slot, t)
        all_blk(each)

    def to_blk(n, sem):
        others(lambda d, t: send(v.XF.at[n, b], v.XF.at[n, b], sem, v.r_xf.at[n], i, t))

    def finish():
        drain(v.RSB, v.r_pb)
        sol = v.PB[b].astype(F32) + total(v.RSB, 7) - v.SZ[...]
        own = lev - 1
        v.XF[own, b] = sol.astype(BF16)

        @pl.when(lev >= 2)
        def _():
            to_slots(own, v.s_xo, kid0, kid1)

        @pl.when(lev == 1)
        def _():
            to_slots(own, v.s_xo, pair_slot)

        to_blk(own, v.s_pb)

        @pl.when(lev >= 3)
        def _():
            to_slots(own, v.s_xo, kid0 + gap, kid1 - gap)
            to_slots(own, v.s_xo, kid0 - gap, kid1 + gap)

        @pl.when(lev == 2)
        def _():
            to_slots(own, v.s_xo, i + 2)

        ssol[0] = sol

    @pl.when(host)
    def _():
        drain(v.RX5.at[pl.ds(0, 15)], v.r_rx5)
        drain(v.H5, v.r_h5)
        rs = (v.H5[0].astype(F32) - total(v.RX5, 16)).astype(BF16)
        v.SR5[b] = rs

        @pl.when(x % 2 == 1)
        def _():
            drain(v.HM, v.r_hm)

        spread(v.TD, dot_t(rs, v.HM[...]))
        drain(v.HU.at[0], v.r_hu)
        v.TD[b] = (v.TD[b].astype(F32) + v.HU[0].astype(F32) + v.HU[1].astype(F32)).astype(BF16)
        mine = (x // 2) * NB + b
        v.RX6[mine] = v.TD[b]
        all_blk(lambda t: send(v.TD.at[t], v.RX6.at[mine], v.s_td, v.r_rx6, far, t))
        others(lambda d, t: send(v.TD.at[t], v.RX6.at[mine], v.s_td, v.r_rx6, i, t))
        others(lambda d, t: send(v.SR5.at[b], v.SR5.at[b], v.s_r5, v.r_r5, i, t))
        drain(v.SR5.at[pl.ds(0, 7)], v.r_r5)

        @pl.when(x % 2 == 1)
        def _():
            drain(v.HI5, v.r_hi5)

        sy5 = dot_t(full(v.SR5), v.HI5[0])
        spread(v.PB5, dot(sy5.astype(BF16), v.HI5[0]))
        others(lambda d, t: send(v.PB5.at[t], v.RSB5.at[d - 1], v.s_p5, v.r_p5, i, t))

        drain(v.RX6.at[pl.ds(0, 15)], v.r_rx6)
        drain(v.H6, v.r_h6)
        v.SR6[b] = (v.H6[0].astype(F32) - total(v.RX6, 16)).astype(BF16)
        others(lambda d, t: send(v.SR6.at[b], v.SR6.at[b], v.s_r6, v.r_r6, i, t))

        @pl.when(x != 1)
        def _():
            drain(v.HG6, v.r_hg6)

        drain(v.SR6.at[pl.ds(0, 7)], v.r_r6)
        sol6 = dot_t(full(v.SR6), v.HG6[...])
        v.XF[5, b] = sol6.astype(BF16)
        to_blk(5, v.s_xb.at[1])
        to_slots(5, v.s_xf.at[5], kid0, kid1)
        drain(v.XF.at[5, pl.ds(0, 7)], v.r_xf.at[5])
        x6 = full(v.XF.at[5])
        drain(v.RSB5, v.r_p5)
        sol5 = v.PB5[b].astype(F32) + total(v.RSB5, 7) - dot(x6, v.HM[...])
        v.XF[4, b] = sol5.astype(BF16)
        to_blk(4, v.s_xb.at[0])
        to_slots(4, v.s_xf.at[4], kid0, kid1)
        part = dot(x6, v.M[1])

        @pl.when(x == 1)
        def _():
            v.HX[...] = sol6
            send(v.HX, v.HY, v.s_hx, v.r_hx, 31, b)

        @pl.when(x % 2 == 0)
        def _():
            v.HX[...] = sol5
            send(v.HX, v.HY, v.s_hx, v.r_hx, owner5, b)

        leaf_part(6)
        drain(v.XF.at[4, pl.ds(0, 7)], v.r_xf.at[4])
        v.SZ[...] = part + dot(full(v.XF.at[4]), v.M[0])
        finish()
        leaf_part(5)
        leaf_product()

    for a in range(LEV, 1, -1):
        @pl.when((lev <= 3) & (lev < a))
        def _(a=a):
            n = a - 1
            drain(v.XF.at[n], v.r_xf.at[n])

            @pl.when((lev >= 2) & (a >= lev + 2))
            def _():
                to_slots(n, v.s_xf.at[n], kid0, kid1)

            if a >= 3:
                @pl.when((lev == 1) & (a < lev_next))
                def _():
                    to_slots(n, v.s_xf.at[n], pair_slot)

            @pl.when(a >= lev + 3)
            def _():
                v.SA[...] = v.SA[...] - dot(full(v.XF.at[n]), v.sc[0, n])

            @pl.when(a == lev + 3)
            def _():
                far_part_start()

            @pl.when(a == lev + 2)
            def _():
                v.SZ[...] = dot(full(v.XF.at[n]), v.M[1])

            @pl.when(a == lev + 1)
            def _():
                v.SZ[...] = v.SZ[...] + dot(full(v.XF.at[n]), v.M[0])
                finish()

            leaf_part(a)

    @pl.when((lev >= 2) & normal)
    def _():
        drain(v.XF.at[lev - 1, pl.ds(0, 7)], v.r_xf.at[lev - 1])
        leaf_part(lev)

    @pl.when(own5 | own6)
    def _():
        drain(v.HY, v.r_hx)
        ssol[0] = v.HY[...]

    @pl.when((z == 15) & (x == 3))
    def _():
        ssol[0] = jnp.zeros((64, 128), F32)

    for a in range(LEV, 1, -1):
        @pl.when(a < lev)
        def _(a=a):
            drain(v.XF.at[a - 1], v.r_xf.at[a - 1])
            leaf_part(a)

    spread(v.LB, dot(v.LA[...].astype(BF16), v.li[0]))
    others(lambda d, t: send(v.LB.at[t], v.RLB.at[d - 1], v.s_lb, v.r_lb, i, t))

    @pl.when(lev == 1)
    def _():
        drain(v.XF.at[0, pl.ds(0, 7)], v.r_xf.at[0])

    @pl.when(lev != 1)
    def _():
        drain(v.XF.at[0], v.r_xf.at[0])

    last = pat[0, 0].astype(F32) * dot(full(v.XF.at[0]), v.ML[...])
    drain(v.RLB, v.r_lb)
    lsol[0] = v.LB[b].astype(F32) + total(v.RLB, 7) - last

    seven = pl.ds(0, 7)
    drain(v.LR.at[seven], v.s_lr)

    @pl.when(odd == 1)
    def _():
        drain(v.T1, v.s_t1)
        for n in range(LEV - 1):
            drain(v.UO1.at[n], v.s_u1.at[n])

    @pl.when(odd == 0)
    def _():
        drain(v.T1.at[seven], v.s_t1)

    for n in range(LEV - 1):
        drain(v.TL.at[n, seven], v.s_tl.at[n])
    drain(v.LB.at[seven], v.s_lb)
    drain(v.IL.at[seven], v.s_ig.at[1])
    drain(v.CL.at[seven], v.s_g.at[3])

    @pl.when(normal)
    def _():
        drain(v.SR.at[seven], v.s_sr)
        drain(v.RX.at[pl.ds(0, 14)], v.s_pb)
        drain(v.IG.at[seven], v.s_ig.at[0])
        drain(v.CG.at[0, seven], v.s_g.at[0])
        drain(v.CG.at[1, seven], v.s_g.at[1])

        @pl.when(lev >= 3)
        def _():
            drain(v.XF, v.s_xo)

        @pl.when(lev == 2)
        def _():
            drain(v.XF.at[pl.ds(0, 3)], v.s_xo)

        @pl.when(lev == 1)
        def _():
            drain(v.PB, v.s_xo)

        @pl.when(lev <= 3)
        def _():
            drain(v.TC, v.s_tc)

        for a in range(3, LEV + 1):
            @pl.when(lev < a - 1)
            def _(a=a):
                drain(v.TN.at[a - 3, seven], v.s_tn.at[a - 3])
                drain(v.UO2.at[a - 2], v.s_u2.at[a - 2])

    @pl.when(host)
    def _():
        drain(v.RX.at[pl.ds(0, 15)], v.s_tc)
        drain(v.RX.at[pl.ds(0, 15)], v.s_td)
        drain(v.SR5.at[seven], v.s_r5)
        drain(v.SR6.at[seven], v.s_r6)
        for n in range(2):
            drain(v.RX, v.s_xf.at[4 + n])
            drain(v.SR5.at[seven], v.s_xb.at[n])

        @pl.when(x < 3)
        def _():
            drain(v.HX, v.s_hx)

    @pl.when(host)
    def _():
        drain(v.PB5.at[seven], v.s_p5)

    @pl.when(own5 | own6)
    def _():
        drain(v.IG.at[seven], v.s_ig.at[0])

    @pl.when(own5)
    def _():
        drain(v.CG.at[0, pl.ds(0, 2)], v.s_hm)
        drain(v.CG.at[0, seven], v.s_g.at[0])
        drain(v.PB.at[pl.ds(0, 2)], v.s_hs)

    @pl.when(own6)
    def _():
        drain(v.CG.at[0, 0], v.s_hm)
        drain(v.VG.at[seven], v.s_g.at[2])
        drain(v.PB.at[pl.ds(0, 4)], v.s_hs)

    @pl.when(host & (x % 2 == 0))
    def _():
        drain(v.CG.at[0, pl.ds(0, 2)], v.s_hr)

    @pl.when(host & (x == 1))
    def _():
        drain(v.CG.at[0, pl.ds(0, 3)], v.s_hr)

    for a in range(LEV, 2, -1):
        @pl.when((lev + 2 <= a) & ((lev == 2) | (lev == 3)))
        def _(a=a):
            drain(v.RX, v.s_xf.at[a - 1])

        @pl.when((lev == 1) & (a < lev_next))
        def _(a=a):
            drain(v.PB, v.s_xf.at[a - 1])


def body(*args):
    vmem = pl.BlockSpec(memory_space=pltpu.VMEM)
    out = jax.ShapeDtypeStruct((1, 64, 128), F32)
    return pl.pallas_call(
        kernel,
        out_shape=(out, out),
        in_specs=[pl.BlockSpec(memory_space=pl.ANY)] * 6 + [pl.BlockSpec(memory_space=pltpu.SMEM)],
        out_specs=(vmem, vmem),
        scratch_shapes=list(SCRATCH.values()),
        compiler_params=pltpu.CompilerParams(collective_id=0, has_side_effects=True, vmem_limit_bytes=56 * 2**20),
        name="solve",
    )(*args)


def solution(mesh):
    in_specs = (
        P("leaf", "blk", None),
        P("leaf", None, None, "blk"),
        P("leaf", "blk", None),
        P("leaf", None, None, "blk"),
        P("leaf", None, "blk"),
        P("leaf", None, "blk"),
        P("leaf", None),
    )
    out_specs = (P("leaf", None, "blk"), P("leaf", None, "blk"))
    return jax.shard_map(body, mesh=mesh, in_specs=in_specs, out_specs=out_specs, check_vma=False)
```

```python
import jax
import jax.numpy as jnp
from jax import lax
from jax.experimental import pallas as pl
from jax.experimental.pallas import tpu as pltpu
from jax.sharding import PartitionSpec as P

MESH = pl.DeviceIdType.MESH
F32 = jnp.float32
BF16 = jnp.bfloat16
NB = 8
LEV = 6


def tree_place(i):
    lev, half, run = 1, 1, 1
    for n in range(3):
        run = run * ((i // 2**n) % 2)
        lev = lev + run
        half = half + run * 2**n
    run = run * ((i // 8) % 2)
    return lev + 3 * run, half


def dot(a, b):
    return jnp.dot(a, b, preferred_element_type=F32)


def dot_t(a, b):
    return lax.dot_general(a, b, (((1,), (1,)), ((), ())), preferred_element_type=F32)


class Names:
    def __init__(self, names, refs):
        for name, ref in zip(names, refs, strict=True):
            setattr(self, name, ref)


def chunks(*lead, dtype=BF16):
    return pltpu.VMEM(lead + (64, 128), dtype)


def sems(*shape):
    return pltpu.SemaphoreType.DMA(shape) if shape else pltpu.SemaphoreType.DMA


def blocks(*shape):
    return pltpu.VMEM(shape, BF16)


SCRATCH = dict(
    li=blocks(1, 128, 1024), lc=blocks(1, 6, 1024, 128), si=blocks(1, 128, 1024), sc=blocks(1, 6, 1024, 128),
    SRI=chunks(1), ld=sems(6),
    LR=chunks(8), LY=chunks(dtype=F32), T1=chunks(8), TL=chunks(5, 8), RSL=chunks(5, 7), U=chunks(5, dtype=F32),
    UO1=chunks(5), UO2=chunks(5), UX=chunks(5, 2),
    s_lr=sems(), r_lr=sems(), s_t1=sems(), s_tl=sems(5), r_tl=sems(5), s_u1=sems(5), s_u2=sems(5), r_ux=sems(5),
    RX=chunks(16), SR=chunks(8), TC=chunks(8), TN=chunks(4, 8), RSS=chunks(4, 7), XF=chunks(6, 8),
    PB=chunks(8), RSB=chunks(7), SA=chunks(dtype=F32), SZ=chunks(dtype=F32), LA=chunks(dtype=F32),
    r_rx=sems(), s_sr=sems(), r_sr=sems(), s_tc=sems(), s_tn=sems(4), r_tn=sems(4),
    s_xf=sems(6), s_xb=sems(2), s_xo=sems(), r_xf=sems(6), s_pb=sems(), r_pb=sems(),
    IG=blocks(8, 128, 128), CG=blocks(2, 8, 1024, 128), VG=blocks(8, 128, 1024), M=blocks(2, 1024, 128), G=blocks(128, 1024),
    CL=blocks(8, 1024, 128), IL=blocks(8, 128, 128), ML=blocks(1024, 128),
    s_ig=sems(2), r_ig=sems(2), l_ig=sems(2), s_g=sems(4), ru_g=sems(4), rd_g=sems(4), rf_g=sems(4), rm_g=sems(4), l_g=sems(4),
    HM=blocks(1024, 128), HI5=blocks(1, 128, 1024), HG6=blocks(128, 1024), H5=chunks(1), H6=chunks(1),
    s_hm=sems(), s_hr=sems(), s_hs=sems(), r_hm=sems(), r_hi5=sems(), r_hg6=sems(), r_h5=sems(), r_h6=sems(),
    RX5=chunks(16), RX6=chunks(16), SR5=chunks(8), SR6=chunks(8), TD=chunks(8), HU=chunks(2), PB5=chunks(8), RSB5=chunks(7), s_p5=sems(), r_p5=sems(),
    r_rx5=sems(), r_rx6=sems(), s_r5=sems(), r_r5=sems(), s_r6=sems(), r_r6=sems(), s_td=sems(), r_hu=sems(),
    HX=chunks(dtype=F32), HY=chunks(dtype=F32), s_hx=sems(), r_hx=sems(),
    LB=chunks(8), RLB=chunks(7), s_lb=sems(), r_lb=sems(),
)


def kernel(li_in, lc_in, si_in, sc_in, lr_in, sr_in, pat, lsol, ssol, *scratch):
    v = Names(SCRATCH, scratch)
    i = lax.axis_index("leaf")
    b = lax.axis_index("blk")
    x, z = i // 16, i % 16
    core = b % 2
    mate = b + 1 - 2 * core
    lev, half = tree_place(i)
    lev_next, _ = tree_place(i + 1)
    odd = i % 2
    even_slot = i - odd
    pair_slot = i + 1 - 2 * odd
    side = (i // (2 * half)) % 2
    parent = i + half - 2 * half * side
    kid0 = i - half // 2
    kid1 = i + half // 2
    gap = half // 4
    normal = lev <= 4
    host = lev == 4
    own5 = (z == 15) & (x % 2 == 0)
    own6 = (z == 15) & (x == 1)
    x_near = x + 1 - 2 * (x % 2)
    x_far = (x + 2) % 4
    near = x_near * 16 + 7
    far = x_far * 16 + 7
    host_a = (x - x % 2) * 16 + 7
    host_b = host_a + 16
    owner5 = (x - x % 2) * 16 + 15

    def send(src, dst, ssem, rsem, leaf, blk):
        pltpu.make_async_remote_copy(src_ref=src, dst_ref=dst, send_sem=ssem, recv_sem=rsem,
                                     device_id=(leaf, blk), device_id_type=MESH).start()

    def drain(ref, sem):
        pltpu.make_async_copy(ref, ref, sem).wait()

    def offset(k):
        return 4 + ((k + 1) // 2) * (2 * (k % 2) - 1)

    def others(fn):
        def step(k, c):
            d = offset(k)
            fn(d, (b + d) % NB)
            return c
        lax.fori_loop(0, NB - 1, step, 0)

    def all_blk(fn):
        def step(k, c):
            fn((b + offset(k)) % NB)
            return c
        lax.fori_loop(0, NB, step, 0)

    def full(ref):
        return jnp.concatenate([ref[c] for c in range(NB)], axis=1)

    def spread(ref, value):
        for c in range(NB):
            ref[c] = value[:, c * 128:(c + 1) * 128].astype(BF16)

    def total(ref, count):
        acc = ref[0].astype(F32)
        for d in range(1, count):
            acc = acc + ref[d].astype(F32)
        return acc

    loads = [
        pltpu.make_async_copy(lr_in.at[0], v.LR.at[b], v.ld.at[0]),
        pltpu.make_async_copy(li_in, v.li, v.ld.at[1]),
        pltpu.make_async_copy(lc_in, v.lc, v.ld.at[2]),
        pltpu.make_async_copy(sr_in, v.SRI, v.ld.at[3]),
        pltpu.make_async_copy(si_in, v.si, v.ld.at[4]),
        pltpu.make_async_copy(sc_in, v.sc, v.ld.at[5]),
    ]
    for load in loads:
        load.start()

    barrier = pltpu.get_barrier_semaphore()

    def greet(leaf, blk):
        pl.semaphore_signal(barrier, inc=1, device_id=(leaf, blk), device_id_type=MESH)

    pair_is_kin = (lev == 2) | (lev == 3) | ((lev == 1) & ((side == 0) | (i % 8 == 2)))
    has_kids = (lev >= 2) & normal
    has_grandkids = (lev == 3) | (lev == 4)
    others(lambda d, t: greet(i, t))

    @pl.when(host)
    def _():
        greet(owner5, b)
        greet(31, b)
        greet(near, b)
        greet(far, b)

    @pl.when(own5)
    def _():
        greet(host_a, b)
        greet(host_b, b)

    @pl.when(own6)
    def _():
        for h in range(4):
            greet(16 * h + 7, b)

    @pl.when(~pair_is_kin)
    def _():
        greet(pair_slot, b)

    @pl.when(lev <= 3)
    def _():
        greet(parent, b)

    @pl.when(lev == 1)
    def _():
        greet(i - i % 8 + 3, b)

    @pl.when(lev == 2)
    def _():
        greet(i - z + 7, b)

    @pl.when(z == 13)
    def _():
        greet(i + 2, b)

    @pl.when(z == 15)
    def _():
        greet(i - 2, b)

    @pl.when(has_kids)
    def _():
        greet(kid0, b)
        greet(kid1, b)

    @pl.when(has_grandkids)
    def _():
        for kid in (kid0, kid1):
            greet(kid - gap, b)
            greet(kid + gap, b)

    peers = (7 + jnp.where(pair_is_kin, 0, 1) + jnp.where(lev <= 3, 1, 0) + jnp.where(lev <= 2, 1, 0)
             + jnp.where((z == 13) | (z == 15), 1, 0)
             + jnp.where(has_kids, 2, 0) + jnp.where(has_grandkids, 4, 0)
             + jnp.where(host, 4, 0) + jnp.where(own5, 2, 0) + jnp.where(own6, 4, 0))
    pl.semaphore_wait(barrier, peers)

    up, down = (b + 2) % NB, (b + 6) % NB
    relay_from, relay_to = (b + 6 + 4 * core) % NB, (b + 2 + 4 * core) % NB

    def gather_start(k, src, dst):
        pltpu.make_async_copy(src, dst.at[b], v.l_g.at[k]).start()
        send(src, dst.at[b], v.s_g.at[k], v.ru_g.at[k], i, up)
        send(src, dst.at[b], v.s_g.at[k], v.rd_g.at[k], i, down)
        send(src, dst.at[b], v.s_g.at[k], v.rm_g.at[k], i, mate)

    def gather_relay(k, dst):
        drain(dst.at[down], v.ru_g.at[k])
        drain(dst.at[up], v.rd_g.at[k])
        send(dst.at[relay_from], dst.at[relay_from], v.s_g.at[k], v.rf_g.at[k], i, relay_to)
        send(dst.at[down], dst.at[down], v.s_g.at[k], v.rm_g.at[k], i, mate)
        send(dst.at[up], dst.at[up], v.s_g.at[k], v.rm_g.at[k], i, mate)

    def gather_end(k, dst):
        opposite = (b + 4) % NB
        drain(dst.at[opposite], v.rf_g.at[k])
        send(dst.at[opposite], dst.at[opposite], v.s_g.at[k], v.rm_g.at[k], i, mate)
        drain(dst.at[pl.ds(0, 4)], v.rm_g.at[k])
        drain(dst.at[b], v.l_g.at[k])

    def columns_start(k, src, dst):
        pltpu.make_async_copy(src.at[0, :, pl.ds(pl.multiple_of(b * 128, 128), 128)], dst.at[b], v.l_ig.at[k]).start()
        others(lambda d, t: send(src.at[0, :, pl.ds(pl.multiple_of(t * 128, 128), 128)], dst.at[b],
                                 v.s_ig.at[k], v.r_ig.at[k], i, t))

    def columns_end(k, dst):
        drain(dst.at[pl.ds(0, 7)], v.r_ig.at[k])
        drain(dst.at[b], v.l_ig.at[k])

    def form_m(out, gathered, inverse):
        columns = inverse[...].reshape(1024, 128)

        def tile(r, c):
            rows = pl.ds(pl.multiple_of(r * 256, 256), 256)
            left = jnp.concatenate([gathered[s, rows, :] for s in range(NB)], axis=1)
            out[rows, :] = dot(left, columns).astype(BF16)
            return c
        lax.fori_loop(0, 4, tile, 0)

    def form_g():
        columns = v.IG[...].reshape(1024, 128)

        def tile(r, c):
            cols = pl.ds(pl.multiple_of(r * 256, 256), 256)
            right = v.VG[:, :, cols].reshape(1024, 256)
            v.G[:, cols] = lax.dot_general(columns, right, (((0,), (0,)), ((), ())),
                                           preferred_element_type=F32).astype(BF16)
            return c
        lax.fori_loop(0, 4, tile, 0)

    early = (lev == 3) | (lev == 4)

    def products_start0():
        columns_start(0, v.si, v.IG)
        gather_start(0, v.sc.at[0, lev], v.CG.at[0])

    def products_start1():
        gather_relay(0, v.CG.at[0])
        gather_start(1, v.sc.at[0, lev + 1], v.CG.at[1])

    def products_end():
        columns_end(0, v.IG)
        gather_end(0, v.CG.at[0])
        gather_relay(1, v.CG.at[1])
        form_m(v.M.at[0], v.CG.at[0], v.IG)
        gather_end(1, v.CG.at[1])
        form_m(v.M.at[1], v.CG.at[1], v.IG)

    def leaf_product():
        columns_start(1, v.li, v.IL)
        gather_start(3, v.lc.at[0, 0], v.CL)
        gather_relay(3, v.CL)
        columns_end(1, v.IL)
        gather_end(3, v.CL)
        form_m(v.ML, v.CL, v.IL)

    loads[0].wait()
    others(lambda d, t: send(v.LR.at[b], v.LR.at[b], v.s_lr, v.r_lr, i, t))
    for load in loads[1:]:
        load.wait()

    @pl.when(own5)
    def _():
        send(v.SRI, v.H5, v.s_hs, v.r_h5, host_a, b)
        send(v.SRI, v.H5, v.s_hs, v.r_h5, host_b, b)

    @pl.when(own6)
    def _():
        for h in range(4):
            send(v.SRI, v.H6, v.s_hs, v.r_h6, 16 * h + 7, b)

    drain(v.LR.at[pl.ds(0, 7)], v.r_lr)
    ly = dot_t(full(v.LR), v.li[0])
    v.LA[...] = ly
    lyb = ly.astype(BF16)
    spread(v.T1, dot_t(lyb, v.lc[0, 0]) * pat[0, 0].astype(F32))

    @pl.when(odd == 1)
    def _():
        all_blk(lambda t: send(v.T1.at[t], v.RX.at[NB + b], v.s_t1, v.r_rx, even_slot, t))

    @pl.when(odd == 0)
    def _():
        v.RX[b] = v.T1[b]
        others(lambda d, t: send(v.T1.at[t], v.RX.at[b], v.s_t1, v.r_rx, i, t))

    for a in range(2, LEV + 1):
        n = a - 2
        spread(v.TL.at[n], dot_t(lyb, v.lc[0, a - 1]) * pat[0, a - 1].astype(F32))
        others(lambda d, t, n=n: send(v.TL.at[n, t], v.RSL.at[n, d - 1], v.s_tl.at[n], v.r_tl.at[n], i, t))

    @pl.when(early)
    def _():
        products_start0()

    @pl.when(own5 | own6)
    def _():
        columns_start(0, v.si, v.IG)

        @pl.when(own5)
        def _():
            gather_start(0, v.sc.at[0, 5], v.CG.at[0])
            send(v.si, v.HI5, v.s_hm, v.r_hi5, host_a, b)

        @pl.when(own6)
        def _():
            gather_start(2, v.si.at[0], v.VG)

    for a in range(2, LEV + 1):
        n = a - 2
        drain(v.RSL.at[n], v.r_tl.at[n])
        acc = v.TL[n, b].astype(F32) + total(v.RSL.at[n], 7)

        @pl.when(odd == 1)
        def _(n=n, acc=acc):
            v.UO1[n] = acc.astype(BF16)
            send(v.UO1.at[n], v.UX.at[n, 1], v.s_u1.at[n], v.r_ux.at[n], even_slot, b)
            v.U[n] = jnp.zeros((64, 128), F32)

        @pl.when(odd == 0)
        def _(n=n, acc=acc):
            v.U[n] = acc
            v.UX[n, 0] = jnp.zeros((64, 128), BF16)

    @pl.when(early)
    def _():
        products_start1()
        products_end()

        @pl.when(host & (x % 2 == 0))
        def _():
            drain(v.HI5, v.r_hi5)
            send(v.HI5, v.HI5, v.s_hr, v.r_hi5, near, b)
            drain(v.HM, v.r_hm)
            send(v.HM, v.HM, v.s_hr, v.r_hm, near, b)

        @pl.when(host & (x == 1))
        def _():
            drain(v.HG6, v.r_hg6)
            for h in (0, 2, 3):
                send(v.HG6, v.HG6, v.s_hr, v.r_hg6, 16 * h + 7, b)

    @pl.when(own5 | own6)
    def _():
        @pl.when(own5)
        def _():
            gather_relay(0, v.CG.at[0])

        @pl.when(own6)
        def _():
            gather_relay(2, v.VG)

        columns_end(0, v.IG)

        @pl.when(own5)
        def _():
            gather_end(0, v.CG.at[0])
            form_m(v.M.at[0], v.CG.at[0], v.IG)
            send(v.M.at[0], v.HM, v.s_hm, v.r_hm, host_a, b)

        @pl.when(own6)
        def _():
            gather_end(2, v.VG)
            form_g()
            send(v.G, v.HG6, v.s_hm, v.r_hg6, 23, b)

    @pl.when(z == 15)
    def _():
        leaf_product()

    def upward(n):
        @pl.when(lev == 1)
        def _():
            drain(v.UX.at[n, 1], v.r_ux.at[n])

        @pl.when(lev != 1)
        def _():
            drain(v.UX.at[n], v.r_ux.at[n])

        return v.U[n] + v.UX[n, 0].astype(F32) + v.UX[n, 1].astype(F32)

    def to_parent_start(value):
        spread(v.TC, value)
        others(lambda d, t: send(v.TC.at[t], v.RX.at[side * NB + b], v.s_tc, v.r_rx, parent, t))

    def to_parent_end(n):
        v.TC[b] = (v.TC[b].astype(F32) + upward(n)).astype(BF16)
        send(v.TC.at[b], v.RX.at[side * NB + b], v.s_tc, v.r_rx, parent, b)

    def over_blk(a, value):
        spread(v.TN.at[a - 3], value)
        others(lambda d, t: send(v.TN.at[a - 3, t], v.RSS.at[a - 3, d - 1], v.s_tn.at[a - 3], v.r_tn.at[a - 3], i, t))

    def far_part_start():
        spread(v.PB, dot(v.SA[...].astype(BF16), v.si[0]))
        others(lambda d, t: send(v.PB.at[t], v.RSB.at[d - 1], v.s_pb, v.r_pb, i, t))

    @pl.when(normal)
    def _():
        @pl.when(lev == 1)
        def _():
            drain(v.RX.at[pl.ds(0, 15)], v.r_rx)

        @pl.when(lev != 1)
        def _():
            drain(v.RX, v.r_rx)

        rs = v.SRI[0].astype(F32) - total(v.RX, 16)
        rsb = rs.astype(BF16)
        v.SR[b] = rsb

        @pl.when(early)
        def _():
            @pl.when(lev == 3)
            def _():
                to_parent_start(dot_t(rsb, v.M[0]))
                over_blk(5, dot_t(rsb, v.M[1]))

            @pl.when(lev == 4)
            def _():
                spread(v.TC, dot_t(rsb, v.M[0]))
                mine = (x % 2) * NB + b
                others(lambda d, t: send(v.TC.at[t], v.RX5.at[mine], v.s_tc, v.r_rx5, near, t))
                others(lambda d, t: send(v.TC.at[t], v.RX5.at[mine], v.s_tc, v.r_rx5, i, t))
                over_blk(6, dot_t(rsb, v.M[1]))

        others(lambda d, t: send(v.SR.at[b], v.SR.at[b], v.s_sr, v.r_sr, i, t))

        @pl.when(lev == 3)
        def _():
            to_parent_end(2)

        @pl.when(lev == 4)
        def _():
            v.TC[b] = (v.TC[b].astype(F32) + upward(3)).astype(BF16)
            mine = (x % 2) * NB + b
            v.RX5[mine] = v.TC[b]
            send(v.TC.at[b], v.RX5.at[mine], v.s_tc, v.r_rx5, near, b)

        drain(v.SR.at[pl.ds(0, 7)], v.r_sr)
        sy = dot_t(full(v.SR), v.si[0])
        v.SA[...] = sy
        syb = sy.astype(BF16)

        for a in (2, 3):
            @pl.when(lev == a - 1)
            def _(a=a):
                to_parent_start(dot_t(syb, v.sc[0, a - 1]))

        for a in range(3, LEV + 1):
            @pl.when((lev < a - 1) & ((lev <= 2) | ((lev == 3) & (a == 6))))
            def _(a=a):
                over_blk(a, dot_t(syb, v.sc[0, a - 1]))

            if a == 3:
                @pl.when(lev == 1)
                def _():
                    to_parent_end(0)

            if a == 4:
                @pl.when(lev == 2)
                def _():
                    to_parent_end(1)

        for a in range(3, LEV + 1):
            n = a - 2

            @pl.when(lev < a - 1)
            def _(a=a, n=n):
                drain(v.RSS.at[a - 3], v.r_tn.at[a - 3])
                acc = v.TN[a - 3, b].astype(F32) + total(v.RSS.at[a - 3], 7) + upward(n)
                v.UO2[n] = acc.astype(BF16)

                @pl.when(lev <= 3)
                def _():
                    send(v.UO2.at[n], v.UX.at[n, side], v.s_u2.at[n], v.r_ux.at[n], parent, b)

                if a == 6:
                    @pl.when(lev == 4)
                    def _():
                        v.HU[x % 2] = v.UO2[n]
                        send(v.UO2.at[n], v.HU.at[x % 2], v.s_u2.at[n], v.r_hu, near, b)

        @pl.when(lev == 4)
        def _():
            far_part_start()

        @pl.when(lev <= 2)
        def _():
            products_start0()
            products_start1()
            products_end()

        @pl.when(lev <= 3)
        def _():
            leaf_product()

    def leaf_part(a):
        v.LA[...] = v.LA[...] - pat[0, a - 1].astype(F32) * dot(full(v.XF.at[a - 1]), v.lc[0, a - 1])

    def to_slots(n, sem, *slots):
        def each(t):
            for slot in slots:
                send(v.XF.at[n, b], v.XF.at[n, b], sem, v.r_xf.at[n], slot, t)
        all_blk(each)

    def to_blk(n, sem):
        others(lambda d, t: send(v.XF.at[n, b], v.XF.at[n, b], sem, v.r_xf.at[n], i, t))

    def finish():
        drain(v.RSB, v.r_pb)
        sol = v.PB[b].astype(F32) + total(v.RSB, 7) - v.SZ[...]
        own = lev - 1
        v.XF[own, b] = sol.astype(BF16)

        @pl.when(lev >= 2)
        def _():
            to_slots(own, v.s_xo, kid0, kid1)

        @pl.when(lev == 1)
        def _():
            to_slots(own, v.s_xo, pair_slot)

        to_blk(own, v.s_pb)

        @pl.when(lev >= 3)
        def _():
            to_slots(own, v.s_xo, kid0 + gap, kid1 - gap)
            to_slots(own, v.s_xo, kid0 - gap, kid1 + gap)

        @pl.when(lev == 2)
        def _():
            to_slots(own, v.s_xo, i + 2)

        ssol[0] = sol

    @pl.when(host)
    def _():
        drain(v.RX5.at[pl.ds(0, 15)], v.r_rx5)
        drain(v.H5, v.r_h5)
        rs = (v.H5[0].astype(F32) - total(v.RX5, 16)).astype(BF16)
        v.SR5[b] = rs

        @pl.when(x % 2 == 1)
        def _():
            drain(v.HM, v.r_hm)

        spread(v.TD, dot_t(rs, v.HM[...]))
        drain(v.HU.at[0], v.r_hu)
        v.TD[b] = (v.TD[b].astype(F32) + v.HU[0].astype(F32) + v.HU[1].astype(F32)).astype(BF16)
        mine = (x // 2) * NB + b
        v.RX6[mine] = v.TD[b]
        all_blk(lambda t: send(v.TD.at[t], v.RX6.at[mine], v.s_td, v.r_rx6, far, t))
        others(lambda d, t: send(v.TD.at[t], v.RX6.at[mine], v.s_td, v.r_rx6, i, t))
        others(lambda d, t: send(v.SR5.at[b], v.SR5.at[b], v.s_r5, v.r_r5, i, t))
        drain(v.SR5.at[pl.ds(0, 7)], v.r_r5)

        @pl.when(x % 2 == 1)
        def _():
            drain(v.HI5, v.r_hi5)

        sy5 = dot_t(full(v.SR5), v.HI5[0])
        spread(v.PB5, dot(sy5.astype(BF16), v.HI5[0]))
        others(lambda d, t: send(v.PB5.at[t], v.RSB5.at[d - 1], v.s_p5, v.r_p5, i, t))

        drain(v.RX6.at[pl.ds(0, 15)], v.r_rx6)
        drain(v.H6, v.r_h6)
        v.SR6[b] = (v.H6[0].astype(F32) - total(v.RX6, 16)).astype(BF16)
        others(lambda d, t: send(v.SR6.at[b], v.SR6.at[b], v.s_r6, v.r_r6, i, t))

        @pl.when(x != 1)
        def _():
            drain(v.HG6, v.r_hg6)

        drain(v.SR6.at[pl.ds(0, 7)], v.r_r6)
        sol6 = dot_t(full(v.SR6), v.HG6[...])
        v.XF[5, b] = sol6.astype(BF16)
        to_blk(5, v.s_xb.at[1])
        to_slots(5, v.s_xf.at[5], kid0, kid1)
        drain(v.XF.at[5, pl.ds(0, 7)], v.r_xf.at[5])
        x6 = full(v.XF.at[5])
        drain(v.RSB5, v.r_p5)
        sol5 = v.PB5[b].astype(F32) + total(v.RSB5, 7) - dot(x6, v.HM[...])
        v.XF[4, b] = sol5.astype(BF16)
        to_blk(4, v.s_xb.at[0])
        to_slots(4, v.s_xf.at[4], kid0, kid1)
        part = dot(x6, v.M[1])

        @pl.when(x == 1)
        def _():
            v.HX[...] = sol6
            send(v.HX, v.HY, v.s_hx, v.r_hx, 31, b)

        @pl.when(x % 2 == 0)
        def _():
            v.HX[...] = sol5
            send(v.HX, v.HY, v.s_hx, v.r_hx, owner5, b)

        leaf_part(6)
        drain(v.XF.at[4, pl.ds(0, 7)], v.r_xf.at[4])
        v.SZ[...] = part + dot(full(v.XF.at[4]), v.M[0])
        finish()
        leaf_part(5)
        leaf_product()

    for a in range(LEV, 1, -1):
        @pl.when((lev <= 3) & (lev < a))
        def _(a=a):
            n = a - 1
            drain(v.XF.at[n], v.r_xf.at[n])

            @pl.when((lev >= 2) & (a >= lev + 2))
            def _():
                to_slots(n, v.s_xf.at[n], kid0, kid1)

            if a >= 3:
                @pl.when((lev == 1) & (a < lev_next))
                def _():
                    to_slots(n, v.s_xf.at[n], pair_slot)

            @pl.when(a >= lev + 3)
            def _():
                v.SA[...] = v.SA[...] - dot(full(v.XF.at[n]), v.sc[0, n])

            @pl.when(a == lev + 3)
            def _():
                far_part_start()

            @pl.when(a == lev + 2)
            def _():
                v.SZ[...] = dot(full(v.XF.at[n]), v.M[1])

            @pl.when(a == lev + 1)
            def _():
                v.SZ[...] = v.SZ[...] + dot(full(v.XF.at[n]), v.M[0])
                finish()

            leaf_part(a)

    @pl.when((lev >= 2) & normal)
    def _():
        drain(v.XF.at[lev - 1, pl.ds(0, 7)], v.r_xf.at[lev - 1])
        leaf_part(lev)

    @pl.when(own5 | own6)
    def _():
        drain(v.HY, v.r_hx)
        ssol[0] = v.HY[...]

    @pl.when((z == 15) & (x == 3))
    def _():
        ssol[0] = jnp.zeros((64, 128), F32)

    for a in range(LEV, 1, -1):
        @pl.when(a < lev)
        def _(a=a):
            drain(v.XF.at[a - 1], v.r_xf.at[a - 1])
            leaf_part(a)

    spread(v.LB, dot(v.LA[...].astype(BF16), v.li[0]))
    others(lambda d, t: send(v.LB.at[t], v.RLB.at[d - 1], v.s_lb, v.r_lb, i, t))

    @pl.when(lev == 1)
    def _():
        drain(v.XF.at[0, pl.ds(0, 7)], v.r_xf.at[0])

    @pl.when(lev != 1)
    def _():
        drain(v.XF.at[0], v.r_xf.at[0])

    last = pat[0, 0].astype(F32) * dot(full(v.XF.at[0]), v.ML[...])
    drain(v.RLB, v.r_lb)
    lsol[0] = v.LB[b].astype(F32) + total(v.RLB, 7) - last

    seven = pl.ds(0, 7)
    drain(v.LR.at[seven], v.s_lr)

    @pl.when(odd == 1)
    def _():
        drain(v.T1, v.s_t1)
        for n in range(LEV - 1):
            drain(v.UO1.at[n], v.s_u1.at[n])

    @pl.when(odd == 0)
    def _():
        drain(v.T1.at[seven], v.s_t1)

    for n in range(LEV - 1):
        drain(v.TL.at[n, seven], v.s_tl.at[n])
    drain(v.LB.at[seven], v.s_lb)
    drain(v.IL.at[seven], v.s_ig.at[1])
    drain(v.CL.at[seven], v.s_g.at[3])

    @pl.when(normal)
    def _():
        drain(v.SR.at[seven], v.s_sr)
        drain(v.RX.at[pl.ds(0, 14)], v.s_pb)
        drain(v.IG.at[seven], v.s_ig.at[0])
        drain(v.CG.at[0, seven], v.s_g.at[0])
        drain(v.CG.at[1, seven], v.s_g.at[1])

        @pl.when(lev >= 3)
        def _():
            drain(v.XF, v.s_xo)

        @pl.when(lev == 2)
        def _():
            drain(v.XF.at[pl.ds(0, 3)], v.s_xo)

        @pl.when(lev == 1)
        def _():
            drain(v.PB, v.s_xo)

        @pl.when(lev <= 3)
        def _():
            drain(v.TC, v.s_tc)

        for a in range(3, LEV + 1):
            @pl.when(lev < a - 1)
            def _(a=a):
                drain(v.TN.at[a - 3, seven], v.s_tn.at[a - 3])
                drain(v.UO2.at[a - 2], v.s_u2.at[a - 2])

    @pl.when(host)
    def _():
        drain(v.RX.at[pl.ds(0, 15)], v.s_tc)
        drain(v.RX.at[pl.ds(0, 15)], v.s_td)
        drain(v.SR5.at[seven], v.s_r5)
        drain(v.SR6.at[seven], v.s_r6)
        for n in range(2):
            drain(v.RX, v.s_xf.at[4 + n])
            drain(v.SR5.at[seven], v.s_xb.at[n])

        @pl.when(x < 3)
        def _():
            drain(v.HX, v.s_hx)

    @pl.when(host)
    def _():
        drain(v.PB5.at[seven], v.s_p5)

    @pl.when(own5 | own6)
    def _():
        drain(v.IG.at[seven], v.s_ig.at[0])

    @pl.when(own5)
    def _():
        drain(v.CG.at[0, pl.ds(0, 2)], v.s_hm)
        drain(v.CG.at[0, seven], v.s_g.at[0])
        drain(v.PB.at[pl.ds(0, 2)], v.s_hs)

    @pl.when(own6)
    def _():
        drain(v.CG.at[0, 0], v.s_hm)
        drain(v.VG.at[seven], v.s_g.at[2])
        drain(v.PB.at[pl.ds(0, 4)], v.s_hs)

    @pl.when(host & (x % 2 == 0))
    def _():
        drain(v.CG.at[0, pl.ds(0, 2)], v.s_hr)

    @pl.when(host & (x == 1))
    def _():
        drain(v.CG.at[0, pl.ds(0, 3)], v.s_hr)

    for a in range(LEV, 2, -1):
        @pl.when((lev + 2 <= a) & ((lev == 2) | (lev == 3)))
        def _(a=a):
            drain(v.RX, v.s_xf.at[a - 1])

        @pl.when((lev == 1) & (a < lev_next))
        def _(a=a):
            drain(v.PB, v.s_xf.at[a - 1])


def body(*args):
    vmem = pl.BlockSpec(memory_space=pltpu.VMEM)
    out = jax.ShapeDtypeStruct((1, 64, 128), F32)
    return pl.pallas_call(
        kernel,
        out_shape=(out, out),
        in_specs=[pl.BlockSpec(memory_space=pl.ANY)] * 6 + [pl.BlockSpec(memory_space=pltpu.SMEM)],
        out_specs=(vmem, vmem),
        scratch_shapes=list(SCRATCH.values()),
        compiler_params=pltpu.CompilerParams(collective_id=0, has_side_effects=True, vmem_limit_bytes=56 * 2**20),
        name="solve",
    )(*args)


def solution(mesh):
    in_specs = (
        P("leaf", "blk", None),
        P("leaf", None, None, "blk"),
        P("leaf", "blk", None),
        P("leaf", None, None, "blk"),
        P("leaf", None, "blk"),
        P("leaf", None, "blk"),
        P("leaf", None),
    )
    out_specs = (P("leaf", None, "blk"), P("leaf", None, "blk"))
    return jax.shard_map(body, mesh=mesh, in_specs=in_specs, out_specs=out_specs, check_vma=False)
```

```python
import jax
import jax.numpy as jnp
from jax import lax
from jax.experimental import pallas as pl
from jax.experimental.pallas import tpu as pltpu
from jax.sharding import PartitionSpec as P

MESH = pl.DeviceIdType.MESH
F32 = jnp.float32
BF16 = jnp.bfloat16
NB = 8
LEV = 6


def tree_place(i):
    lev, half, run = 1, 1, 1
    for n in range(3):
        run = run * ((i // 2**n) % 2)
        lev = lev + run
        half = half + run * 2**n
    run = run * ((i // 8) % 2)
    return lev + 3 * run, half


def dot(a, b):
    return jnp.dot(a, b, preferred_element_type=F32)


def dot_t(a, b):
    return lax.dot_general(a, b, (((1,), (1,)), ((), ())), preferred_element_type=F32)


class Names:
    def __init__(self, names, refs):
        for name, ref in zip(names, refs, strict=True):
            setattr(self, name, ref)


def chunks(*lead, dtype=BF16):
    return pltpu.VMEM(lead + (64, 128), dtype)


def sems(*shape):
    return pltpu.SemaphoreType.DMA(shape) if shape else pltpu.SemaphoreType.DMA


def blocks(*shape):
    return pltpu.VMEM(shape, BF16)


SCRATCH = dict(
    li=blocks(1, 128, 1024), lc=blocks(1, 6, 1024, 128), si=blocks(1, 128, 1024), sc=blocks(1, 6, 1024, 128),
    SRI=chunks(1), ld=sems(6),
    LR=chunks(8), LY=chunks(dtype=F32), T1=chunks(8), TL=chunks(5, 8), RSL=chunks(5, 7), U=chunks(5, dtype=F32),
    UO1=chunks(5), UO2=chunks(5), UX=chunks(5, 2),
    s_lr=sems(), r_lr=sems(), s_t1=sems(), s_tl=sems(5), r_tl=sems(5), s_u1=sems(5), s_u2=sems(5), r_ux=sems(5),
    RX=chunks(16), SR=chunks(8), TC=chunks(8), TN=chunks(4, 8), RSS=chunks(4, 7), XF=chunks(6, 8),
    PB=chunks(8), RSB=chunks(7), SA=chunks(dtype=F32), SZ=chunks(dtype=F32), LA=chunks(dtype=F32),
    r_rx=sems(), s_sr=sems(), r_sr=sems(), s_tc=sems(), s_tn=sems(4), r_tn=sems(4),
    s_xf=sems(6), s_xb=sems(2), s_xo=sems(), r_xf=sems(6), s_pb=sems(), r_pb=sems(),
    IG=blocks(8, 128, 128), CG=blocks(2, 8, 1024, 128), VG=blocks(8, 128, 1024), M=blocks(2, 1024, 128), G=blocks(128, 1024),
    CL=blocks(8, 1024, 128), IL=blocks(8, 128, 128), ML=blocks(1024, 128),
    s_ig=sems(2), r_ig=sems(2), l_ig=sems(2), s_g=sems(4), ru_g=sems(4), rd_g=sems(4), rf_g=sems(4), rm_g=sems(4), l_g=sems(4),
    HM=blocks(1024, 128), HI5=blocks(1, 128, 1024), HG6=blocks(128, 1024), H5=chunks(1), H6=chunks(1),
    s_hm=sems(), s_hr=sems(), s_hs=sems(), r_hm=sems(), r_hi5=sems(), r_hg6=sems(), r_h5=sems(), r_h6=sems(),
    RX5=chunks(16), RX6=chunks(16), SR5=chunks(8), SR6=chunks(8), TD=chunks(8), HU=chunks(4), PB5=chunks(8), RSB5=chunks(7), s_p5=sems(), r_p5=sems(),
    r_rx5=sems(), r_rx6=sems(), s_r5=sems(), r_r5=sems(), s_r6=sems(), r_r6=sems(), s_td=sems(), r_hu=sems(),
    HX=chunks(dtype=F32), HY=chunks(dtype=F32), s_hx=sems(), r_hx=sems(),
    LB=chunks(8), RLB=chunks(7), s_lb=sems(), r_lb=sems(),
)


def kernel(li_in, lc_in, si_in, sc_in, lr_in, sr_in, pat, lsol, ssol, *scratch):
    v = Names(SCRATCH, scratch)
    i = lax.axis_index("leaf")
    b = lax.axis_index("blk")
    x, z = i // 16, i % 16
    core = b % 2
    mate = b + 1 - 2 * core
    lev, half = tree_place(i)
    lev_next, _ = tree_place(i + 1)
    odd = i % 2
    even_slot = i - odd
    pair_slot = i + 1 - 2 * odd
    side = (i // (2 * half)) % 2
    parent = i + half - 2 * half * side
    kid0 = i - half // 2
    kid1 = i + half // 2
    gap = half // 4
    normal = lev <= 4
    host = lev == 4
    own5 = (z == 15) & (x % 2 == 0)
    own6 = (z == 15) & (x == 1)
    x_near = x + 1 - 2 * (x % 2)
    x_far = (x + 2) % 4
    near = x_near * 16 + 7
    far = x_far * 16 + 7
    cross = (3 - x) * 16 + 7
    host_a = (x - x % 2) * 16 + 7
    host_b = host_a + 16
    owner5 = (x - x % 2) * 16 + 15

    def send(src, dst, ssem, rsem, leaf, blk):
        pltpu.make_async_remote_copy(src_ref=src, dst_ref=dst, send_sem=ssem, recv_sem=rsem,
                                     device_id=(leaf, blk), device_id_type=MESH).start()

    def drain(ref, sem):
        pltpu.make_async_copy(ref, ref, sem).wait()

    def offset(k):
        return 4 + ((k + 1) // 2) * (2 * (k % 2) - 1)

    def others(fn):
        def step(k, c):
            d = offset(k)
            fn(d, (b + d) % NB)
            return c
        lax.fori_loop(0, NB - 1, step, 0)

    def all_blk(fn):
        def step(k, c):
            fn((b + offset(k)) % NB)
            return c
        lax.fori_loop(0, NB, step, 0)

    def full(ref):
        return jnp.concatenate([ref[c] for c in range(NB)], axis=1)

    def spread(ref, value):
        for c in range(NB):
            ref[c] = value[:, c * 128:(c + 1) * 128].astype(BF16)

    def total(ref, count):
        acc = ref[0].astype(F32)
        for d in range(1, count):
            acc = acc + ref[d].astype(F32)
        return acc

    loads = [
        pltpu.make_async_copy(lr_in.at[0], v.LR.at[b], v.ld.at[0]),
        pltpu.make_async_copy(li_in, v.li, v.ld.at[1]),
        pltpu.make_async_copy(lc_in, v.lc, v.ld.at[2]),
        pltpu.make_async_copy(sr_in, v.SRI, v.ld.at[3]),
        pltpu.make_async_copy(si_in, v.si, v.ld.at[4]),
        pltpu.make_async_copy(sc_in, v.sc, v.ld.at[5]),
    ]
    for load in loads:
        load.start()

    barrier = pltpu.get_barrier_semaphore()

    def greet(leaf, blk):
        pl.semaphore_signal(barrier, inc=1, device_id=(leaf, blk), device_id_type=MESH)

    pair_is_kin = (lev == 2) | (lev == 3) | ((lev == 1) & ((side == 0) | (i % 8 == 2)))
    has_kids = (lev >= 2) & normal
    has_grandkids = (lev == 3) | (lev == 4)
    others(lambda d, t: greet(i, t))

    @pl.when(host)
    def _():
        greet(owner5, b)
        greet(31, b)
        greet(near, b)
        greet(far, b)
        greet(cross, b)

    @pl.when(own5)
    def _():
        greet(host_a, b)
        greet(host_b, b)

    @pl.when(own6)
    def _():
        for h in range(4):
            greet(16 * h + 7, b)

    @pl.when(~pair_is_kin)
    def _():
        greet(pair_slot, b)

    @pl.when(lev <= 3)
    def _():
        greet(parent, b)

    @pl.when(lev == 1)
    def _():
        greet(i - i % 8 + 3, b)

    @pl.when(lev == 2)
    def _():
        greet(i - z + 7, b)

    @pl.when(z == 13)
    def _():
        greet(i + 2, b)

    @pl.when(z == 15)
    def _():
        greet(i - 2, b)

    @pl.when(has_kids)
    def _():
        greet(kid0, b)
        greet(kid1, b)

    @pl.when(has_grandkids)
    def _():
        for kid in (kid0, kid1):
            greet(kid - gap, b)
            greet(kid + gap, b)

    peers = (7 + jnp.where(pair_is_kin, 0, 1) + jnp.where(lev <= 3, 1, 0) + jnp.where(lev <= 2, 1, 0)
             + jnp.where((z == 13) | (z == 15), 1, 0)
             + jnp.where(has_kids, 2, 0) + jnp.where(has_grandkids, 4, 0)
             + jnp.where(host, 5, 0) + jnp.where(own5, 2, 0) + jnp.where(own6, 4, 0))
    pl.semaphore_wait(barrier, peers)

    up, down = (b + 2) % NB, (b + 6) % NB
    relay_from, relay_to = (b + 6 + 4 * core) % NB, (b + 2 + 4 * core) % NB

    def gather_start(k, src, dst):
        pltpu.make_async_copy(src, dst.at[b], v.l_g.at[k]).start()
        send(src, dst.at[b], v.s_g.at[k], v.ru_g.at[k], i, up)
        send(src, dst.at[b], v.s_g.at[k], v.rd_g.at[k], i, down)
        send(src, dst.at[b], v.s_g.at[k], v.rm_g.at[k], i, mate)

    def gather_relay(k, dst):
        drain(dst.at[down], v.ru_g.at[k])
        drain(dst.at[up], v.rd_g.at[k])
        send(dst.at[relay_from], dst.at[relay_from], v.s_g.at[k], v.rf_g.at[k], i, relay_to)
        send(dst.at[down], dst.at[down], v.s_g.at[k], v.rm_g.at[k], i, mate)
        send(dst.at[up], dst.at[up], v.s_g.at[k], v.rm_g.at[k], i, mate)

    def gather_end(k, dst):
        opposite = (b + 4) % NB
        drain(dst.at[opposite], v.rf_g.at[k])
        send(dst.at[opposite], dst.at[opposite], v.s_g.at[k], v.rm_g.at[k], i, mate)
        drain(dst.at[pl.ds(0, 4)], v.rm_g.at[k])
        drain(dst.at[b], v.l_g.at[k])

    def columns_start(k, src, dst):
        pltpu.make_async_copy(src.at[0, :, pl.ds(pl.multiple_of(b * 128, 128), 128)], dst.at[b], v.l_ig.at[k]).start()
        others(lambda d, t: send(src.at[0, :, pl.ds(pl.multiple_of(t * 128, 128), 128)], dst.at[b],
                                 v.s_ig.at[k], v.r_ig.at[k], i, t))

    def columns_end(k, dst):
        drain(dst.at[pl.ds(0, 7)], v.r_ig.at[k])
        drain(dst.at[b], v.l_ig.at[k])

    def form_m(out, gathered, inverse):
        columns = inverse[...].reshape(1024, 128)

        def tile(r, c):
            rows = pl.ds(pl.multiple_of(r * 256, 256), 256)
            left = jnp.concatenate([gathered[s, rows, :] for s in range(NB)], axis=1)
            out[rows, :] = dot(left, columns).astype(BF16)
            return c
        lax.fori_loop(0, 4, tile, 0)

    def form_g():
        columns = v.IG[...].reshape(1024, 128)

        def tile(r, c):
            cols = pl.ds(pl.multiple_of(r * 256, 256), 256)
            right = v.VG[:, :, cols].reshape(1024, 256)
            v.G[:, cols] = lax.dot_general(columns, right, (((0,), (0,)), ((), ())),
                                           preferred_element_type=F32).astype(BF16)
            return c
        lax.fori_loop(0, 4, tile, 0)

    early = (lev == 3) | (lev == 4)

    def products_start0():
        columns_start(0, v.si, v.IG)
        gather_start(0, v.sc.at[0, lev], v.CG.at[0])

    def products_start1():
        gather_relay(0, v.CG.at[0])
        gather_start(1, v.sc.at[0, lev + 1], v.CG.at[1])

    def products_end():
        columns_end(0, v.IG)
        gather_end(0, v.CG.at[0])
        gather_relay(1, v.CG.at[1])
        form_m(v.M.at[0], v.CG.at[0], v.IG)
        gather_end(1, v.CG.at[1])
        form_m(v.M.at[1], v.CG.at[1], v.IG)

    def leaf_product():
        columns_start(1, v.li, v.IL)
        gather_start(3, v.lc.at[0, 0], v.CL)
        gather_relay(3, v.CL)
        columns_end(1, v.IL)
        gather_end(3, v.CL)
        form_m(v.ML, v.CL, v.IL)

    loads[0].wait()
    others(lambda d, t: send(v.LR.at[b], v.LR.at[b], v.s_lr, v.r_lr, i, t))
    for load in loads[1:]:
        load.wait()

    @pl.when(own5)
    def _():
        send(v.SRI, v.H5, v.s_hs, v.r_h5, host_a, b)
        send(v.SRI, v.H5, v.s_hs, v.r_h5, host_b, b)

    @pl.when(own6)
    def _():
        for h in range(4):
            send(v.SRI, v.H6, v.s_hs, v.r_h6, 16 * h + 7, b)

    @pl.when(own5 | own6)
    def _():
        columns_start(0, v.si, v.IG)

        @pl.when(own5)
        def _():
            gather_start(0, v.sc.at[0, 5], v.CG.at[0])
            send(v.si, v.HI5, v.s_hm, v.r_hi5, host_a, b)

        @pl.when(own6)
        def _():
            gather_start(2, v.si.at[0], v.VG)

    @pl.when(early)
    def _():
        products_start0()

    drain(v.LR.at[pl.ds(0, 7)], v.r_lr)
    ly = dot_t(full(v.LR), v.li[0])
    v.LA[...] = ly
    lyb = ly.astype(BF16)
    spread(v.T1, dot_t(lyb, v.lc[0, 0]) * pat[0, 0].astype(F32))

    @pl.when(odd == 1)
    def _():
        all_blk(lambda t: send(v.T1.at[t], v.RX.at[NB + b], v.s_t1, v.r_rx, even_slot, t))

    @pl.when(odd == 0)
    def _():
        v.RX[b] = v.T1[b]
        others(lambda d, t: send(v.T1.at[t], v.RX.at[b], v.s_t1, v.r_rx, i, t))

    for a in range(2, LEV + 1):
        n = a - 2
        spread(v.TL.at[n], dot_t(lyb, v.lc[0, a - 1]) * pat[0, a - 1].astype(F32))
        others(lambda d, t, n=n: send(v.TL.at[n, t], v.RSL.at[n, d - 1], v.s_tl.at[n], v.r_tl.at[n], i, t))

    @pl.when(own5)
    def _():
        gather_relay(0, v.CG.at[0])

    @pl.when(own6)
    def _():
        gather_relay(2, v.VG)

    @pl.when(early)
    def _():
        products_start1()

    for a in range(2, LEV + 1):
        n = a - 2
        drain(v.RSL.at[n], v.r_tl.at[n])
        acc = v.TL[n, b].astype(F32) + total(v.RSL.at[n], 7)

        @pl.when(odd == 1)
        def _(n=n, acc=acc):
            v.UO1[n] = acc.astype(BF16)
            send(v.UO1.at[n], v.UX.at[n, 1], v.s_u1.at[n], v.r_ux.at[n], even_slot, b)
            v.U[n] = jnp.zeros((64, 128), F32)

        @pl.when(odd == 0)
        def _(n=n, acc=acc):
            v.U[n] = acc
            v.UX[n, 0] = jnp.zeros((64, 128), BF16)

    @pl.when(early)
    def _():
        products_end()

        @pl.when(host & (x % 2 == 0))
        def _():
            drain(v.HI5, v.r_hi5)
            send(v.HI5, v.HI5, v.s_hr, v.r_hi5, near, b)
            drain(v.HM, v.r_hm)
            send(v.HM, v.HM, v.s_hr, v.r_hm, near, b)

        @pl.when(host & (x == 1))
        def _():
            drain(v.HG6, v.r_hg6)
            for h in (0, 2, 3):
                send(v.HG6, v.HG6, v.s_hr, v.r_hg6, 16 * h + 7, b)

    @pl.when(own5 | own6)
    def _():
        columns_end(0, v.IG)

        @pl.when(own5)
        def _():
            gather_end(0, v.CG.at[0])
            form_m(v.M.at[0], v.CG.at[0], v.IG)
            send(v.M.at[0], v.HM, v.s_hm, v.r_hm, host_a, b)

        @pl.when(own6)
        def _():
            gather_end(2, v.VG)
            form_g()
            send(v.G, v.HG6, v.s_hm, v.r_hg6, 23, b)

    @pl.when(z == 15)
    def _():
        leaf_product()

    def upward(n):
        @pl.when(lev == 1)
        def _():
            drain(v.UX.at[n, 1], v.r_ux.at[n])

        @pl.when(lev != 1)
        def _():
            drain(v.UX.at[n], v.r_ux.at[n])

        return v.U[n] + v.UX[n, 0].astype(F32) + v.UX[n, 1].astype(F32)

    def to_parent_start(value):
        spread(v.TC, value)
        others(lambda d, t: send(v.TC.at[t], v.RX.at[side * NB + b], v.s_tc, v.r_rx, parent, t))

    def to_parent_end(n):
        v.TC[b] = (v.TC[b].astype(F32) + upward(n)).astype(BF16)
        send(v.TC.at[b], v.RX.at[side * NB + b], v.s_tc, v.r_rx, parent, b)

    def over_blk(a, value):
        spread(v.TN.at[a - 3], value)
        others(lambda d, t: send(v.TN.at[a - 3, t], v.RSS.at[a - 3, d - 1], v.s_tn.at[a - 3], v.r_tn.at[a - 3], i, t))

    def far_part_start():
        spread(v.PB, dot(v.SA[...].astype(BF16), v.si[0]))
        others(lambda d, t: send(v.PB.at[t], v.RSB.at[d - 1], v.s_pb, v.r_pb, i, t))

    @pl.when(normal)
    def _():
        @pl.when(lev == 1)
        def _():
            drain(v.RX.at[pl.ds(0, 15)], v.r_rx)

        @pl.when(lev != 1)
        def _():
            drain(v.RX, v.r_rx)

        rs = v.SRI[0].astype(F32) - total(v.RX, 16)
        rsb = rs.astype(BF16)
        v.SR[b] = rsb

        @pl.when(early)
        def _():
            @pl.when(lev == 3)
            def _():
                to_parent_start(dot_t(rsb, v.M[0]))
                over_blk(5, dot_t(rsb, v.M[1]))

            @pl.when(lev == 4)
            def _():
                spread(v.TC, dot_t(rsb, v.M[0]))
                mine = (x % 2) * NB + b
                others(lambda d, t: send(v.TC.at[t], v.RX5.at[mine], v.s_tc, v.r_rx5, near, t))
                others(lambda d, t: send(v.TC.at[t], v.RX5.at[mine], v.s_tc, v.r_rx5, i, t))
                over_blk(6, dot_t(rsb, v.M[1]))

        others(lambda d, t: send(v.SR.at[b], v.SR.at[b], v.s_sr, v.r_sr, i, t))

        @pl.when(lev == 3)
        def _():
            to_parent_end(2)

        @pl.when(lev == 4)
        def _():
            v.TC[b] = (v.TC[b].astype(F32) + upward(3)).astype(BF16)
            mine = (x % 2) * NB + b
            v.RX5[mine] = v.TC[b]
            send(v.TC.at[b], v.RX5.at[mine], v.s_tc, v.r_rx5, near, b)

        drain(v.SR.at[pl.ds(0, 7)], v.r_sr)
        sy = dot_t(full(v.SR), v.si[0])
        v.SA[...] = sy
        syb = sy.astype(BF16)

        for a in (2, 3):
            @pl.when(lev == a - 1)
            def _(a=a):
                to_parent_start(dot_t(syb, v.sc[0, a - 1]))

        for a in range(3, LEV + 1):
            @pl.when((lev < a - 1) & ((lev <= 2) | ((lev == 3) & (a == 6))))
            def _(a=a):
                over_blk(a, dot_t(syb, v.sc[0, a - 1]))

            if a == 3:
                @pl.when(lev == 1)
                def _():
                    to_parent_end(0)

            if a == 4:
                @pl.when(lev == 2)
                def _():
                    to_parent_end(1)

        for a in range(3, LEV + 1):
            n = a - 2

            @pl.when((lev < a - 1) & (lev <= 3))
            def _(a=a, n=n):
                drain(v.RSS.at[a - 3], v.r_tn.at[a - 3])
                acc = v.TN[a - 3, b].astype(F32) + total(v.RSS.at[a - 3], 7) + upward(n)
                v.UO2[n] = acc.astype(BF16)
                send(v.UO2.at[n], v.UX.at[n, side], v.s_u2.at[n], v.r_ux.at[n], parent, b)

        @pl.when(lev == 4)
        def _():
            far_part_start()

        @pl.when(lev <= 2)
        def _():
            products_start0()
            products_start1()
            products_end()

        @pl.when(lev <= 3)
        def _():
            leaf_product()

    def leaf_part(a):
        v.LA[...] = v.LA[...] - pat[0, a - 1].astype(F32) * dot(full(v.XF.at[a - 1]), v.lc[0, a - 1])

    def to_slots(n, sem, *slots):
        def each(t):
            for slot in slots:
                send(v.XF.at[n, b], v.XF.at[n, b], sem, v.r_xf.at[n], slot, t)
        all_blk(each)

    def to_blk(n, sem):
        others(lambda d, t: send(v.XF.at[n, b], v.XF.at[n, b], sem, v.r_xf.at[n], i, t))

    def finish():
        drain(v.RSB, v.r_pb)
        sol = v.PB[b].astype(F32) + total(v.RSB, 7) - v.SZ[...]
        own = lev - 1
        v.XF[own, b] = sol.astype(BF16)

        @pl.when(lev >= 2)
        def _():
            to_slots(own, v.s_xo, kid0, kid1)

        @pl.when(lev == 1)
        def _():
            to_slots(own, v.s_xo, pair_slot)

        to_blk(own, v.s_pb)

        @pl.when(lev >= 3)
        def _():
            to_slots(own, v.s_xo, kid0 + gap, kid1 - gap)
            to_slots(own, v.s_xo, kid0 - gap, kid1 + gap)

        @pl.when(lev == 2)
        def _():
            to_slots(own, v.s_xo, i + 2)

        ssol[0] = sol

    @pl.when(host)
    def _():
        drain(v.RX5.at[pl.ds(0, 15)], v.r_rx5)
        drain(v.H5, v.r_h5)
        rs = (v.H5[0].astype(F32) - total(v.RX5, 16)).astype(BF16)
        v.SR5[b] = rs

        @pl.when(x % 2 == 1)
        def _():
            drain(v.HM, v.r_hm)

        spread(v.TD, dot_t(rs, v.HM[...]))
        mine = (x // 2) * NB + b
        v.RX6[mine] = v.TD[b]
        all_blk(lambda t: send(v.TD.at[t], v.RX6.at[mine], v.s_td, v.r_rx6, far, t))
        others(lambda d, t: send(v.TD.at[t], v.RX6.at[mine], v.s_td, v.r_rx6, i, t))
        others(lambda d, t: send(v.SR5.at[b], v.SR5.at[b], v.s_r5, v.r_r5, i, t))

        drain(v.RSS.at[3], v.r_tn.at[3])
        acc = v.TN[3, b].astype(F32) + total(v.RSS.at[3], 7) + upward(4)
        v.UO2[4] = acc.astype(BF16)
        v.HU[x] = v.UO2[4]
        for slot in (near, far, cross):
            send(v.UO2.at[4], v.HU.at[x], v.s_u2.at[4], v.r_hu, slot, b)

        drain(v.SR5.at[pl.ds(0, 7)], v.r_r5)

        @pl.when(x % 2 == 1)
        def _():
            drain(v.HI5, v.r_hi5)

        sy5 = dot_t(full(v.SR5), v.HI5[0])
        spread(v.PB5, dot(sy5.astype(BF16), v.HI5[0]))
        others(lambda d, t: send(v.PB5.at[t], v.RSB5.at[d - 1], v.s_p5, v.r_p5, i, t))

        drain(v.RX6.at[pl.ds(0, 15)], v.r_rx6)
        drain(v.H6, v.r_h6)
        drain(v.HU.at[pl.ds(0, 3)], v.r_hu)
        v.SR6[b] = (v.H6[0].astype(F32) - total(v.RX6, 16) - total(v.HU, 4)).astype(BF16)
        others(lambda d, t: send(v.SR6.at[b], v.SR6.at[b], v.s_r6, v.r_r6, i, t))

        @pl.when(x != 1)
        def _():
            drain(v.HG6, v.r_hg6)

        drain(v.SR6.at[pl.ds(0, 7)], v.r_r6)
        sol6 = dot_t(full(v.SR6), v.HG6[...])
        v.XF[5, b] = sol6.astype(BF16)
        to_blk(5, v.s_xb.at[1])
        to_slots(5, v.s_xf.at[5], kid0, kid1)
        drain(v.XF.at[5, pl.ds(0, 7)], v.r_xf.at[5])
        x6 = full(v.XF.at[5])
        drain(v.RSB5, v.r_p5)
        sol5 = v.PB5[b].astype(F32) + total(v.RSB5, 7) - dot(x6, v.HM[...])
        v.XF[4, b] = sol5.astype(BF16)
        to_blk(4, v.s_xb.at[0])
        to_slots(4, v.s_xf.at[4], kid0, kid1)
        part = dot(x6, v.M[1])

        @pl.when(x == 1)
        def _():
            v.HX[...] = sol6
            send(v.HX, v.HY, v.s_hx, v.r_hx, 31, b)

        @pl.when(x % 2 == 0)
        def _():
            v.HX[...] = sol5
            send(v.HX, v.HY, v.s_hx, v.r_hx, owner5, b)

        leaf_part(6)
        drain(v.XF.at[4, pl.ds(0, 7)], v.r_xf.at[4])
        v.SZ[...] = part + dot(full(v.XF.at[4]), v.M[0])
        finish()
        leaf_part(5)
        leaf_product()

    for a in range(LEV, 1, -1):
        @pl.when((lev <= 3) & (lev < a))
        def _(a=a):
            n = a - 1
            drain(v.XF.at[n], v.r_xf.at[n])

            @pl.when((lev >= 2) & (a >= lev + 2))
            def _():
                to_slots(n, v.s_xf.at[n], kid0, kid1)

            if a >= 3:
                @pl.when((lev == 1) & (a < lev_next))
                def _():
                    to_slots(n, v.s_xf.at[n], pair_slot)

            @pl.when(a >= lev + 3)
            def _():
                v.SA[...] = v.SA[...] - dot(full(v.XF.at[n]), v.sc[0, n])

            @pl.when(a == lev + 3)
            def _():
                far_part_start()

            @pl.when(a == lev + 2)
            def _():
                v.SZ[...] = dot(full(v.XF.at[n]), v.M[1])

            @pl.when(a == lev + 1)
            def _():
                v.SZ[...] = v.SZ[...] + dot(full(v.XF.at[n]), v.M[0])
                finish()

            leaf_part(a)

    @pl.when((lev >= 2) & normal)
    def _():
        drain(v.XF.at[lev - 1, pl.ds(0, 7)], v.r_xf.at[lev - 1])
        leaf_part(lev)

    @pl.when(own5 | own6)
    def _():
        drain(v.HY, v.r_hx)
        ssol[0] = v.HY[...]

    @pl.when((z == 15) & (x == 3))
    def _():
        ssol[0] = jnp.zeros((64, 128), F32)

    for a in range(LEV, 1, -1):
        @pl.when(a < lev)
        def _(a=a):
            drain(v.XF.at[a - 1], v.r_xf.at[a - 1])
            leaf_part(a)

    spread(v.LB, dot(v.LA[...].astype(BF16), v.li[0]))
    others(lambda d, t: send(v.LB.at[t], v.RLB.at[d - 1], v.s_lb, v.r_lb, i, t))

    @pl.when(lev == 1)
    def _():
        drain(v.XF.at[0, pl.ds(0, 7)], v.r_xf.at[0])

    @pl.when(lev != 1)
    def _():
        drain(v.XF.at[0], v.r_xf.at[0])

    last = pat[0, 0].astype(F32) * dot(full(v.XF.at[0]), v.ML[...])
    drain(v.RLB, v.r_lb)
    lsol[0] = v.LB[b].astype(F32) + total(v.RLB, 7) - last

    seven = pl.ds(0, 7)
    drain(v.LR.at[seven], v.s_lr)

    @pl.when(odd == 1)
    def _():
        drain(v.T1, v.s_t1)
        for n in range(LEV - 1):
            drain(v.UO1.at[n], v.s_u1.at[n])

    @pl.when(odd == 0)
    def _():
        drain(v.T1.at[seven], v.s_t1)

    for n in range(LEV - 1):
        drain(v.TL.at[n, seven], v.s_tl.at[n])
    drain(v.LB.at[seven], v.s_lb)
    drain(v.IL.at[seven], v.s_ig.at[1])
    drain(v.CL.at[seven], v.s_g.at[3])

    @pl.when(normal)
    def _():
        drain(v.SR.at[seven], v.s_sr)
        drain(v.RX.at[pl.ds(0, 14)], v.s_pb)
        drain(v.IG.at[seven], v.s_ig.at[0])
        drain(v.CG.at[0, seven], v.s_g.at[0])
        drain(v.CG.at[1, seven], v.s_g.at[1])

        @pl.when(lev >= 3)
        def _():
            drain(v.XF, v.s_xo)

        @pl.when(lev == 2)
        def _():
            drain(v.XF.at[pl.ds(0, 3)], v.s_xo)

        @pl.when(lev == 1)
        def _():
            drain(v.PB, v.s_xo)

        @pl.when(lev <= 3)
        def _():
            drain(v.TC, v.s_tc)

        for a in range(3, LEV + 1):
            @pl.when(lev < a - 1)
            def _(a=a):
                drain(v.TN.at[a - 3, seven], v.s_tn.at[a - 3])

            @pl.when((lev < a - 1) & (lev <= 3))
            def _(a=a):
                drain(v.UO2.at[a - 2], v.s_u2.at[a - 2])

    @pl.when(host)
    def _():
        drain(v.UO2.at[pl.ds(0, 3)], v.s_u2.at[4])
        drain(v.RX.at[pl.ds(0, 15)], v.s_tc)
        drain(v.RX.at[pl.ds(0, 15)], v.s_td)
        drain(v.SR5.at[seven], v.s_r5)
        drain(v.SR6.at[seven], v.s_r6)
        for n in range(2):
            drain(v.RX, v.s_xf.at[4 + n])
            drain(v.SR5.at[seven], v.s_xb.at[n])

        @pl.when(x < 3)
        def _():
            drain(v.HX, v.s_hx)

    @pl.when(host)
    def _():
        drain(v.PB5.at[seven], v.s_p5)

    @pl.when(own5 | own6)
    def _():
        drain(v.IG.at[seven], v.s_ig.at[0])

    @pl.when(own5)
    def _():
        drain(v.CG.at[0, pl.ds(0, 2)], v.s_hm)
        drain(v.CG.at[0, seven], v.s_g.at[0])
        drain(v.PB.at[pl.ds(0, 2)], v.s_hs)

    @pl.when(own6)
    def _():
        drain(v.CG.at[0, 0], v.s_hm)
        drain(v.VG.at[seven], v.s_g.at[2])
        drain(v.PB.at[pl.ds(0, 4)], v.s_hs)

    @pl.when(host & (x % 2 == 0))
    def _():
        drain(v.CG.at[0, pl.ds(0, 2)], v.s_hr)

    @pl.when(host & (x == 1))
    def _():
        drain(v.CG.at[0, pl.ds(0, 3)], v.s_hr)

    for a in range(LEV, 2, -1):
        @pl.when((lev + 2 <= a) & ((lev == 2) | (lev == 3)))
        def _(a=a):
            drain(v.RX, v.s_xf.at[a - 1])

        @pl.when((lev == 1) & (a < lev_next))
        def _(a=a):
            drain(v.PB, v.s_xf.at[a - 1])


def body(*args):
    vmem = pl.BlockSpec(memory_space=pltpu.VMEM)
    out = jax.ShapeDtypeStruct((1, 64, 128), F32)
    return pl.pallas_call(
        kernel,
        out_shape=(out, out),
        in_specs=[pl.BlockSpec(memory_space=pl.ANY)] * 6 + [pl.BlockSpec(memory_space=pltpu.SMEM)],
        out_specs=(vmem, vmem),
        scratch_shapes=list(SCRATCH.values()),
        compiler_params=pltpu.CompilerParams(collective_id=0, has_side_effects=True, vmem_limit_bytes=56 * 2**20),
        name="solve",
    )(*args)


def solution(mesh):
    in_specs = (
        P("leaf", "blk", None),
        P("leaf", None, None, "blk"),
        P("leaf", "blk", None),
        P("leaf", None, None, "blk"),
        P("leaf", None, "blk"),
        P("leaf", None, "blk"),
        P("leaf", None),
    )
    out_specs = (P("leaf", None, "blk"), P("leaf", None, "blk"))
    return jax.shard_map(body, mesh=mesh, in_specs=in_specs, out_specs=out_specs, check_vma=False)
```

```python
import jax
import jax.numpy as jnp
from jax import lax
from jax.experimental import pallas as pl
from jax.experimental.pallas import tpu as pltpu
from jax.sharding import PartitionSpec as P

MESH = pl.DeviceIdType.MESH
F32 = jnp.float32
BF16 = jnp.bfloat16
NB = 8
LEV = 6


def tree_place(i):
    lev, half, run = 1, 1, 1
    for n in range(3):
        run = run * ((i // 2**n) % 2)
        lev = lev + run
        half = half + run * 2**n
    run = run * ((i // 8) % 2)
    return lev + 3 * run, half


def dot(a, b):
    return jnp.dot(a, b, preferred_element_type=F32)


def dot_t(a, b):
    return lax.dot_general(a, b, (((1,), (1,)), ((), ())), preferred_element_type=F32)


class Names:
    def __init__(self, names, refs):
        for name, ref in zip(names, refs, strict=True):
            setattr(self, name, ref)


def chunks(*lead, dtype=BF16):
    return pltpu.VMEM(lead + (64, 128), dtype)


def sems(*shape):
    return pltpu.SemaphoreType.DMA(shape) if shape else pltpu.SemaphoreType.DMA


def blocks(*shape):
    return pltpu.VMEM(shape, BF16)


SCRATCH = dict(
    li=blocks(1, 128, 1024), lc=blocks(1, 6, 1024, 128), si=blocks(1, 128, 1024), sc=blocks(1, 6, 1024, 128),
    SRI=chunks(1), ld=sems(6),
    LR=chunks(8), LY=chunks(dtype=F32), T1=chunks(8), TL=chunks(5, 8), RSL=chunks(5, 7), U=chunks(5, dtype=F32),
    UO1=chunks(5), UO2=chunks(5), UX=chunks(5, 2),
    s_lr=sems(), r_lr=sems(), s_t1=sems(), s_tl=sems(5), r_tl=sems(5), s_u1=sems(5), s_u2=sems(5), r_ux=sems(5),
    RX=chunks(16), SR=chunks(8), TC=chunks(8), TN=chunks(4, 8), RSS=chunks(4, 7), XF=chunks(6, 8),
    PB=chunks(8), RSB=chunks(7), SA=chunks(dtype=F32), SZ=chunks(dtype=F32), LA=chunks(dtype=F32),
    r_rx=sems(), s_sr=sems(), r_sr=sems(), s_tc=sems(), s_tn=sems(4), r_tn=sems(4),
    s_xf=sems(6), s_xb=sems(2), s_xo=sems(), r_xf=sems(6), s_pb=sems(), r_pb=sems(),
    IG=blocks(8, 128, 128), CG=blocks(2, 8, 1024, 128), VG=blocks(8, 128, 1024), M=blocks(2, 1024, 128), G=blocks(128, 1024),
    CL=blocks(8, 1024, 128), IL=blocks(8, 128, 128), ML=blocks(1024, 128),
    s_ig=sems(2), r_ig=sems(2), l_ig=sems(2), s_g=sems(4), ru_g=sems(4), rd_g=sems(4), rf_g=sems(4), rm_g=sems(4), l_g=sems(4),
    HM=blocks(1024, 128), HI5=blocks(1, 128, 1024), HG6=blocks(128, 1024), H5=chunks(1), H6=chunks(1),
    s_hm=sems(), s_hr=sems(), s_hs=sems(), r_hm=sems(), r_hi5=sems(), r_hg6=sems(), r_h5=sems(), r_h6=sems(),
    RX5=chunks(16), RX6=chunks(16), SR5=chunks(8), SR6=chunks(8), TD=chunks(8), HU=chunks(4), PB5=chunks(8), RSB5=chunks(7), s_p5=sems(), r_p5=sems(),
    r_rx5=sems(), r_rx6=sems(), s_r5=sems(), r_r5=sems(), s_r6=sems(), r_r6=sems(), s_td=sems(), r_hu=sems(),
    HX=chunks(dtype=F32), HY=chunks(dtype=F32), s_hx=sems(), r_hx=sems(),
    LB=chunks(8), RLB=chunks(7), s_lb=sems(), r_lb=sems(),
)


def kernel(li_in, lc_in, si_in, sc_in, lr_in, sr_in, pat, lsol, ssol, *scratch):
    v = Names(SCRATCH, scratch)
    i = lax.axis_index("leaf")
    b = lax.axis_index("blk")
    x, z = i // 16, i % 16
    core = b % 2
    mate = b + 1 - 2 * core
    lev, half = tree_place(i)
    lev_next, _ = tree_place(i + 1)
    odd = i % 2
    even_slot = i - odd
    pair_slot = i + 1 - 2 * odd
    side = (i // (2 * half)) % 2
    parent = i + half - 2 * half * side
    kid0 = i - half // 2
    kid1 = i + half // 2
    gap = half // 4
    normal = lev <= 4
    host = lev == 4
    own5 = (z == 15) & (x % 2 == 0)
    own6 = (z == 15) & (x == 1)
    x_near = x + 1 - 2 * (x % 2)
    x_far = (x + 2) % 4
    near = x_near * 16 + 7
    far = x_far * 16 + 7
    cross = (3 - x) * 16 + 7
    host_a = (x - x % 2) * 16 + 7
    host_b = host_a + 16
    owner5 = (x - x % 2) * 16 + 15

    def send(src, dst, ssem, rsem, leaf, blk):
        pltpu.make_async_remote_copy(src_ref=src, dst_ref=dst, send_sem=ssem, recv_sem=rsem,
                                     device_id=(leaf, blk), device_id_type=MESH).start()

    def drain(ref, sem):
        pltpu.make_async_copy(ref, ref, sem).wait()

    def offset(k):
        return 4 + ((k + 1) // 2) * (2 * (k % 2) - 1)

    def others(fn):
        for k in range(NB - 1):
            fn(offset(k), (b + offset(k)) % NB)

    def all_blk(fn):
        for k in range(NB):
            fn((b + offset(k)) % NB)

    def full(ref):
        return jnp.concatenate([ref[c] for c in range(NB)], axis=1)

    def spread(ref, value):
        for c in range(NB):
            ref[c] = value[:, c * 128:(c + 1) * 128].astype(BF16)

    def total(ref, count):
        acc = ref[0].astype(F32)
        for d in range(1, count):
            acc = acc + ref[d].astype(F32)
        return acc

    loads = [
        pltpu.make_async_copy(lr_in.at[0], v.LR.at[b], v.ld.at[0]),
        pltpu.make_async_copy(li_in, v.li, v.ld.at[1]),
        pltpu.make_async_copy(lc_in, v.lc, v.ld.at[2]),
        pltpu.make_async_copy(sr_in, v.SRI, v.ld.at[3]),
        pltpu.make_async_copy(si_in, v.si, v.ld.at[4]),
        pltpu.make_async_copy(sc_in, v.sc, v.ld.at[5]),
    ]
    for load in loads:
        load.start()

    barrier = pltpu.get_barrier_semaphore()

    def greet(leaf, blk):
        pl.semaphore_signal(barrier, inc=1, device_id=(leaf, blk), device_id_type=MESH)

    pair_is_kin = (lev == 2) | (lev == 3) | ((lev == 1) & ((side == 0) | (i % 8 == 2)))
    has_kids = (lev >= 2) & normal
    has_grandkids = (lev == 3) | (lev == 4)
    others(lambda d, t: greet(i, t))

    @pl.when(host)
    def _():
        greet(owner5, b)
        greet(31, b)
        greet(near, b)
        greet(far, b)
        greet(cross, b)

    @pl.when(own5)
    def _():
        greet(host_a, b)
        greet(host_b, b)

    @pl.when(own6)
    def _():
        for h in range(4):
            greet(16 * h + 7, b)

    @pl.when(~pair_is_kin)
    def _():
        greet(pair_slot, b)

    @pl.when(lev <= 3)
    def _():
        greet(parent, b)

    @pl.when(lev == 1)
    def _():
        greet(i - i % 8 + 3, b)

    @pl.when(lev == 2)
    def _():
        greet(i - z + 7, b)

    @pl.when(z == 13)
    def _():
        greet(i + 2, b)

    @pl.when(z == 15)
    def _():
        greet(i - 2, b)

    @pl.when(has_kids)
    def _():
        greet(kid0, b)
        greet(kid1, b)

    @pl.when(has_grandkids)
    def _():
        for kid in (kid0, kid1):
            greet(kid - gap, b)
            greet(kid + gap, b)

    peers = (7 + jnp.where(pair_is_kin, 0, 1) + jnp.where(lev <= 3, 1, 0) + jnp.where(lev <= 2, 1, 0)
             + jnp.where((z == 13) | (z == 15), 1, 0)
             + jnp.where(has_kids, 2, 0) + jnp.where(has_grandkids, 4, 0)
             + jnp.where(host, 5, 0) + jnp.where(own5, 2, 0) + jnp.where(own6, 4, 0))
    pl.semaphore_wait(barrier, peers)

    up, down = (b + 2) % NB, (b + 6) % NB
    relay_from, relay_to = (b + 6 + 4 * core) % NB, (b + 2 + 4 * core) % NB

    def gather_start(k, src, dst):
        pltpu.make_async_copy(src, dst.at[b], v.l_g.at[k]).start()
        send(src, dst.at[b], v.s_g.at[k], v.ru_g.at[k], i, up)
        send(src, dst.at[b], v.s_g.at[k], v.rd_g.at[k], i, down)
        send(src, dst.at[b], v.s_g.at[k], v.rm_g.at[k], i, mate)

    def gather_relay(k, dst):
        drain(dst.at[down], v.ru_g.at[k])
        drain(dst.at[up], v.rd_g.at[k])
        send(dst.at[relay_from], dst.at[relay_from], v.s_g.at[k], v.rf_g.at[k], i, relay_to)
        send(dst.at[down], dst.at[down], v.s_g.at[k], v.rm_g.at[k], i, mate)
        send(dst.at[up], dst.at[up], v.s_g.at[k], v.rm_g.at[k], i, mate)

    def gather_end(k, dst):
        opposite = (b + 4) % NB
        drain(dst.at[opposite], v.rf_g.at[k])
        send(dst.at[opposite], dst.at[opposite], v.s_g.at[k], v.rm_g.at[k], i, mate)
        drain(dst.at[pl.ds(0, 4)], v.rm_g.at[k])
        drain(dst.at[b], v.l_g.at[k])

    def columns_start(k, src, dst):
        pltpu.make_async_copy(src.at[0, :, pl.ds(pl.multiple_of(b * 128, 128), 128)], dst.at[b], v.l_ig.at[k]).start()
        others(lambda d, t: send(src.at[0, :, pl.ds(pl.multiple_of(t * 128, 128), 128)], dst.at[b],
                                 v.s_ig.at[k], v.r_ig.at[k], i, t))

    def columns_end(k, dst):
        drain(dst.at[pl.ds(0, 7)], v.r_ig.at[k])
        drain(dst.at[b], v.l_ig.at[k])

    def form_m(out, gathered, inverse):
        columns = inverse[...].reshape(1024, 128)

        def tile(r, c):
            rows = pl.ds(pl.multiple_of(r * 256, 256), 256)
            left = jnp.concatenate([gathered[s, rows, :] for s in range(NB)], axis=1)
            out[rows, :] = dot(left, columns).astype(BF16)
            return c
        lax.fori_loop(0, 4, tile, 0)

    def form_g():
        columns = v.IG[...].reshape(1024, 128)

        def tile(r, c):
            cols = pl.ds(pl.multiple_of(r * 256, 256), 256)
            right = v.VG[:, :, cols].reshape(1024, 256)
            v.G[:, cols] = lax.dot_general(columns, right, (((0,), (0,)), ((), ())),
                                           preferred_element_type=F32).astype(BF16)
            return c
        lax.fori_loop(0, 4, tile, 0)

    early = (lev == 3) | (lev == 4)

    def products_start0():
        columns_start(0, v.si, v.IG)
        gather_start(0, v.sc.at[0, lev], v.CG.at[0])

    def products_start1():
        gather_relay(0, v.CG.at[0])
        gather_start(1, v.sc.at[0, lev + 1], v.CG.at[1])

    def products_end():
        columns_end(0, v.IG)
        gather_end(0, v.CG.at[0])
        gather_relay(1, v.CG.at[1])
        form_m(v.M.at[0], v.CG.at[0], v.IG)
        gather_end(1, v.CG.at[1])
        form_m(v.M.at[1], v.CG.at[1], v.IG)

    def leaf_product():
        columns_start(1, v.li, v.IL)
        gather_start(3, v.lc.at[0, 0], v.CL)
        gather_relay(3, v.CL)
        columns_end(1, v.IL)
        gather_end(3, v.CL)
        form_m(v.ML, v.CL, v.IL)

    loads[0].wait()
    others(lambda d, t: send(v.LR.at[b], v.LR.at[b], v.s_lr, v.r_lr, i, t))
    for load in loads[1:]:
        load.wait()

    @pl.when(own5)
    def _():
        send(v.SRI, v.H5, v.s_hs, v.r_h5, host_a, b)
        send(v.SRI, v.H5, v.s_hs, v.r_h5, host_b, b)

    @pl.when(own6)
    def _():
        for h in range(4):
            send(v.SRI, v.H6, v.s_hs, v.r_h6, 16 * h + 7, b)

    @pl.when(own5 | own6)
    def _():
        columns_start(0, v.si, v.IG)

        @pl.when(own5)
        def _():
            gather_start(0, v.sc.at[0, 5], v.CG.at[0])
            send(v.si, v.HI5, v.s_hm, v.r_hi5, host_a, b)

        @pl.when(own6)
        def _():
            gather_start(2, v.si.at[0], v.VG)

    @pl.when(early)
    def _():
        products_start0()

    drain(v.LR.at[pl.ds(0, 7)], v.r_lr)
    ly = dot_t(full(v.LR), v.li[0])
    v.LA[...] = ly
    lyb = ly.astype(BF16)
    spread(v.T1, dot_t(lyb, v.lc[0, 0]) * pat[0, 0].astype(F32))

    @pl.when(odd == 1)
    def _():
        all_blk(lambda t: send(v.T1.at[t], v.RX.at[NB + b], v.s_t1, v.r_rx, even_slot, t))

    @pl.when(odd == 0)
    def _():
        v.RX[b] = v.T1[b]
        others(lambda d, t: send(v.T1.at[t], v.RX.at[b], v.s_t1, v.r_rx, i, t))

    for a in range(2, LEV + 1):
        n = a - 2
        spread(v.TL.at[n], dot_t(lyb, v.lc[0, a - 1]) * pat[0, a - 1].astype(F32))
        others(lambda d, t, n=n: send(v.TL.at[n, t], v.RSL.at[n, d - 1], v.s_tl.at[n], v.r_tl.at[n], i, t))

    @pl.when(own5)
    def _():
        gather_relay(0, v.CG.at[0])

    @pl.when(own6)
    def _():
        gather_relay(2, v.VG)

    @pl.when(early)
    def _():
        products_start1()

    for a in range(2, LEV + 1):
        n = a - 2
        drain(v.RSL.at[n], v.r_tl.at[n])
        acc = v.TL[n, b].astype(F32) + total(v.RSL.at[n], 7)

        @pl.when(odd == 1)
        def _(n=n, acc=acc):
            v.UO1[n] = acc.astype(BF16)
            send(v.UO1.at[n], v.UX.at[n, 1], v.s_u1.at[n], v.r_ux.at[n], even_slot, b)
            v.U[n] = jnp.zeros((64, 128), F32)

        @pl.when(odd == 0)
        def _(n=n, acc=acc):
            v.U[n] = acc
            v.UX[n, 0] = jnp.zeros((64, 128), BF16)

    @pl.when(early)
    def _():
        products_end()

        @pl.when(host & (x % 2 == 0))
        def _():
            drain(v.HI5, v.r_hi5)
            send(v.HI5, v.HI5, v.s_hr, v.r_hi5, near, b)
            drain(v.HM, v.r_hm)
            send(v.HM, v.HM, v.s_hr, v.r_hm, near, b)

        @pl.when(host & (x == 1))
        def _():
            drain(v.HG6, v.r_hg6)
            for h in (0, 2, 3):
                send(v.HG6, v.HG6, v.s_hr, v.r_hg6, 16 * h + 7, b)

    @pl.when(own5 | own6)
    def _():
        columns_end(0, v.IG)

        @pl.when(own5)
        def _():
            gather_end(0, v.CG.at[0])
            form_m(v.M.at[0], v.CG.at[0], v.IG)
            send(v.M.at[0], v.HM, v.s_hm, v.r_hm, host_a, b)

        @pl.when(own6)
        def _():
            gather_end(2, v.VG)
            form_g()
            send(v.G, v.HG6, v.s_hm, v.r_hg6, 23, b)

    @pl.when(z == 15)
    def _():
        leaf_product()

    def upward(n):
        @pl.when(lev == 1)
        def _():
            drain(v.UX.at[n, 1], v.r_ux.at[n])

        @pl.when(lev != 1)
        def _():
            drain(v.UX.at[n], v.r_ux.at[n])

        return v.U[n] + v.UX[n, 0].astype(F32) + v.UX[n, 1].astype(F32)

    def to_parent_start(value):
        spread(v.TC, value)
        others(lambda d, t: send(v.TC.at[t], v.RX.at[side * NB + b], v.s_tc, v.r_rx, parent, t))

    def to_parent_end(n):
        v.TC[b] = (v.TC[b].astype(F32) + upward(n)).astype(BF16)
        send(v.TC.at[b], v.RX.at[side * NB + b], v.s_tc, v.r_rx, parent, b)

    def over_blk(a, value):
        spread(v.TN.at[a - 3], value)
        others(lambda d, t: send(v.TN.at[a - 3, t], v.RSS.at[a - 3, d - 1], v.s_tn.at[a - 3], v.r_tn.at[a - 3], i, t))

    def far_part_start():
        spread(v.PB, dot(v.SA[...].astype(BF16), v.si[0]))
        others(lambda d, t: send(v.PB.at[t], v.RSB.at[d - 1], v.s_pb, v.r_pb, i, t))

    @pl.when(normal)
    def _():
        @pl.when(lev == 1)
        def _():
            drain(v.RX.at[pl.ds(0, 15)], v.r_rx)

        @pl.when(lev != 1)
        def _():
            drain(v.RX, v.r_rx)

        rs = v.SRI[0].astype(F32) - total(v.RX, 16)
        rsb = rs.astype(BF16)
        v.SR[b] = rsb

        @pl.when(early)
        def _():
            @pl.when(lev == 3)
            def _():
                to_parent_start(dot_t(rsb, v.M[0]))
                over_blk(5, dot_t(rsb, v.M[1]))

            @pl.when(lev == 4)
            def _():
                spread(v.TC, dot_t(rsb, v.M[0]))
                mine = (x % 2) * NB + b
                others(lambda d, t: send(v.TC.at[t], v.RX5.at[mine], v.s_tc, v.r_rx5, near, t))
                others(lambda d, t: send(v.TC.at[t], v.RX5.at[mine], v.s_tc, v.r_rx5, i, t))
                over_blk(6, dot_t(rsb, v.M[1]))

        others(lambda d, t: send(v.SR.at[b], v.SR.at[b], v.s_sr, v.r_sr, i, t))

        @pl.when(lev == 3)
        def _():
            to_parent_end(2)

        @pl.when(lev == 4)
        def _():
            v.TC[b] = (v.TC[b].astype(F32) + upward(3)).astype(BF16)
            mine = (x % 2) * NB + b
            v.RX5[mine] = v.TC[b]
            send(v.TC.at[b], v.RX5.at[mine], v.s_tc, v.r_rx5, near, b)

        drain(v.SR.at[pl.ds(0, 7)], v.r_sr)
        sy = dot_t(full(v.SR), v.si[0])
        v.SA[...] = sy
        syb = sy.astype(BF16)

        for a in (2, 3):
            @pl.when(lev == a - 1)
            def _(a=a):
                to_parent_start(dot_t(syb, v.sc[0, a - 1]))

        for a in range(3, LEV + 1):
            @pl.when((lev < a - 1) & ((lev <= 2) | ((lev == 3) & (a == 6))))
            def _(a=a):
                over_blk(a, dot_t(syb, v.sc[0, a - 1]))

            if a == 3:
                @pl.when(lev == 1)
                def _():
                    to_parent_end(0)

            if a == 4:
                @pl.when(lev == 2)
                def _():
                    to_parent_end(1)

        for a in range(3, LEV + 1):
            n = a - 2

            @pl.when((lev < a - 1) & (lev <= 3))
            def _(a=a, n=n):
                drain(v.RSS.at[a - 3], v.r_tn.at[a - 3])
                acc = v.TN[a - 3, b].astype(F32) + total(v.RSS.at[a - 3], 7) + upward(n)
                v.UO2[n] = acc.astype(BF16)
                send(v.UO2.at[n], v.UX.at[n, side], v.s_u2.at[n], v.r_ux.at[n], parent, b)

        @pl.when(lev == 4)
        def _():
            far_part_start()

        @pl.when(lev <= 2)
        def _():
            products_start0()
            products_start1()
            products_end()

        @pl.when(lev <= 3)
        def _():
            leaf_product()

    def leaf_part(a):
        v.LA[...] = v.LA[...] - pat[0, a - 1].astype(F32) * dot(full(v.XF.at[a - 1]), v.lc[0, a - 1])

    def to_slots(n, sem, *slots):
        def each(t):
            for slot in slots:
                send(v.XF.at[n, b], v.XF.at[n, b], sem, v.r_xf.at[n], slot, t)
        all_blk(each)

    def to_blk(n, sem):
        others(lambda d, t: send(v.XF.at[n, b], v.XF.at[n, b], sem, v.r_xf.at[n], i, t))

    def finish():
        drain(v.RSB, v.r_pb)
        sol = v.PB[b].astype(F32) + total(v.RSB, 7) - v.SZ[...]
        own = lev - 1
        v.XF[own, b] = sol.astype(BF16)

        @pl.when(lev >= 2)
        def _():
            to_slots(own, v.s_xo, kid0, kid1)

        @pl.when(lev == 1)
        def _():
            to_slots(own, v.s_xo, pair_slot)

        to_blk(own, v.s_pb)

        @pl.when(lev >= 3)
        def _():
            to_slots(own, v.s_xo, kid0 + gap, kid1 - gap)
            to_slots(own, v.s_xo, kid0 - gap, kid1 + gap)

        @pl.when(lev == 2)
        def _():
            to_slots(own, v.s_xo, i + 2)

        ssol[0] = sol

    @pl.when(host)
    def _():
        drain(v.RX5.at[pl.ds(0, 15)], v.r_rx5)
        drain(v.H5, v.r_h5)
        rs = (v.H5[0].astype(F32) - total(v.RX5, 16)).astype(BF16)
        v.SR5[b] = rs

        @pl.when(x % 2 == 1)
        def _():
            drain(v.HM, v.r_hm)

        spread(v.TD, dot_t(rs, v.HM[...]))
        mine = (x // 2) * NB + b
        v.RX6[mine] = v.TD[b]
        all_blk(lambda t: send(v.TD.at[t], v.RX6.at[mine], v.s_td, v.r_rx6, far, t))
        others(lambda d, t: send(v.TD.at[t], v.RX6.at[mine], v.s_td, v.r_rx6, i, t))
        others(lambda d, t: send(v.SR5.at[b], v.SR5.at[b], v.s_r5, v.r_r5, i, t))

        drain(v.RSS.at[3], v.r_tn.at[3])
        acc = v.TN[3, b].astype(F32) + total(v.RSS.at[3], 7) + upward(4)
        v.UO2[4] = acc.astype(BF16)
        v.HU[x] = v.UO2[4]
        for slot in (near, far, cross):
            send(v.UO2.at[4], v.HU.at[x], v.s_u2.at[4], v.r_hu, slot, b)

        drain(v.SR5.at[pl.ds(0, 7)], v.r_r5)

        @pl.when(x % 2 == 1)
        def _():
            drain(v.HI5, v.r_hi5)

        sy5 = dot_t(full(v.SR5), v.HI5[0])
        spread(v.PB5, dot(sy5.astype(BF16), v.HI5[0]))
        others(lambda d, t: send(v.PB5.at[t], v.RSB5.at[d - 1], v.s_p5, v.r_p5, i, t))

        drain(v.RX6.at[pl.ds(0, 15)], v.r_rx6)
        drain(v.H6, v.r_h6)
        drain(v.HU.at[pl.ds(0, 3)], v.r_hu)
        v.SR6[b] = (v.H6[0].astype(F32) - total(v.RX6, 16) - total(v.HU, 4)).astype(BF16)
        others(lambda d, t: send(v.SR6.at[b], v.SR6.at[b], v.s_r6, v.r_r6, i, t))

        @pl.when(x != 1)
        def _():
            drain(v.HG6, v.r_hg6)

        drain(v.SR6.at[pl.ds(0, 7)], v.r_r6)
        sol6 = dot_t(full(v.SR6), v.HG6[...])
        v.XF[5, b] = sol6.astype(BF16)
        to_blk(5, v.s_xb.at[1])
        to_slots(5, v.s_xf.at[5], kid0, kid1)
        drain(v.XF.at[5, pl.ds(0, 7)], v.r_xf.at[5])
        x6 = full(v.XF.at[5])
        drain(v.RSB5, v.r_p5)
        sol5 = v.PB5[b].astype(F32) + total(v.RSB5, 7) - dot(x6, v.HM[...])
        v.XF[4, b] = sol5.astype(BF16)
        to_blk(4, v.s_xb.at[0])
        to_slots(4, v.s_xf.at[4], kid0, kid1)
        part = dot(x6, v.M[1])

        @pl.when(x == 1)
        def _():
            v.HX[...] = sol6
            send(v.HX, v.HY, v.s_hx, v.r_hx, 31, b)

        @pl.when(x % 2 == 0)
        def _():
            v.HX[...] = sol5
            send(v.HX, v.HY, v.s_hx, v.r_hx, owner5, b)

        leaf_part(6)
        drain(v.XF.at[4, pl.ds(0, 7)], v.r_xf.at[4])
        v.SZ[...] = part + dot(full(v.XF.at[4]), v.M[0])
        finish()
        leaf_part(5)
        leaf_product()

    for a in range(LEV, 1, -1):
        @pl.when((lev <= 3) & (lev < a))
        def _(a=a):
            n = a - 1
            drain(v.XF.at[n], v.r_xf.at[n])

            @pl.when((lev >= 2) & (a >= lev + 2))
            def _():
                to_slots(n, v.s_xf.at[n], kid0, kid1)

            if a >= 3:
                @pl.when((lev == 1) & (a < lev_next))
                def _():
                    to_slots(n, v.s_xf.at[n], pair_slot)

            @pl.when(a >= lev + 3)
            def _():
                v.SA[...] = v.SA[...] - dot(full(v.XF.at[n]), v.sc[0, n])

            @pl.when(a == lev + 3)
            def _():
                far_part_start()

            @pl.when(a == lev + 2)
            def _():
                v.SZ[...] = dot(full(v.XF.at[n]), v.M[1])

            @pl.when(a == lev + 1)
            def _():
                v.SZ[...] = v.SZ[...] + dot(full(v.XF.at[n]), v.M[0])
                finish()

            leaf_part(a)

    @pl.when((lev >= 2) & normal)
    def _():
        drain(v.XF.at[lev - 1, pl.ds(0, 7)], v.r_xf.at[lev - 1])
        leaf_part(lev)

    @pl.when(own5 | own6)
    def _():
        drain(v.HY, v.r_hx)
        ssol[0] = v.HY[...]

    @pl.when((z == 15) & (x == 3))
    def _():
        ssol[0] = jnp.zeros((64, 128), F32)

    for a in range(LEV, 1, -1):
        @pl.when(a < lev)
        def _(a=a):
            drain(v.XF.at[a - 1], v.r_xf.at[a - 1])
            leaf_part(a)

    spread(v.LB, dot(v.LA[...].astype(BF16), v.li[0]))
    others(lambda d, t: send(v.LB.at[t], v.RLB.at[d - 1], v.s_lb, v.r_lb, i, t))

    @pl.when(lev == 1)
    def _():
        drain(v.XF.at[0, pl.ds(0, 7)], v.r_xf.at[0])

    @pl.when(lev != 1)
    def _():
        drain(v.XF.at[0], v.r_xf.at[0])

    last = pat[0, 0].astype(F32) * dot(full(v.XF.at[0]), v.ML[...])
    drain(v.RLB, v.r_lb)
    lsol[0] = v.LB[b].astype(F32) + total(v.RLB, 7) - last

    seven = pl.ds(0, 7)
    drain(v.LR.at[seven], v.s_lr)

    @pl.when(odd == 1)
    def _():
        drain(v.T1, v.s_t1)
        for n in range(LEV - 1):
            drain(v.UO1.at[n], v.s_u1.at[n])

    @pl.when(odd == 0)
    def _():
        drain(v.T1.at[seven], v.s_t1)

    for n in range(LEV - 1):
        drain(v.TL.at[n, seven], v.s_tl.at[n])
    drain(v.LB.at[seven], v.s_lb)
    drain(v.IL.at[seven], v.s_ig.at[1])
    drain(v.CL.at[seven], v.s_g.at[3])

    @pl.when(normal)
    def _():
        drain(v.SR.at[seven], v.s_sr)
        drain(v.RX.at[pl.ds(0, 14)], v.s_pb)
        drain(v.IG.at[seven], v.s_ig.at[0])
        drain(v.CG.at[0, seven], v.s_g.at[0])
        drain(v.CG.at[1, seven], v.s_g.at[1])

        @pl.when(lev >= 3)
        def _():
            drain(v.XF, v.s_xo)

        @pl.when(lev == 2)
        def _():
            drain(v.XF.at[pl.ds(0, 3)], v.s_xo)

        @pl.when(lev == 1)
        def _():
            drain(v.PB, v.s_xo)

        @pl.when(lev <= 3)
        def _():
            drain(v.TC, v.s_tc)

        for a in range(3, LEV + 1):
            @pl.when(lev < a - 1)
            def _(a=a):
                drain(v.TN.at[a - 3, seven], v.s_tn.at[a - 3])

            @pl.when((lev < a - 1) & (lev <= 3))
            def _(a=a):
                drain(v.UO2.at[a - 2], v.s_u2.at[a - 2])

    @pl.when(host)
    def _():
        drain(v.UO2.at[pl.ds(0, 3)], v.s_u2.at[4])
        drain(v.RX.at[pl.ds(0, 15)], v.s_tc)
        drain(v.RX.at[pl.ds(0, 15)], v.s_td)
        drain(v.SR5.at[seven], v.s_r5)
        drain(v.SR6.at[seven], v.s_r6)
        for n in range(2):
            drain(v.RX, v.s_xf.at[4 + n])
            drain(v.SR5.at[seven], v.s_xb.at[n])

        @pl.when(x < 3)
        def _():
            drain(v.HX, v.s_hx)

    @pl.when(host)
    def _():
        drain(v.PB5.at[seven], v.s_p5)

    @pl.when(own5 | own6)
    def _():
        drain(v.IG.at[seven], v.s_ig.at[0])

    @pl.when(own5)
    def _():
        drain(v.CG.at[0, pl.ds(0, 2)], v.s_hm)
        drain(v.CG.at[0, seven], v.s_g.at[0])
        drain(v.PB.at[pl.ds(0, 2)], v.s_hs)

    @pl.when(own6)
    def _():
        drain(v.CG.at[0, 0], v.s_hm)
        drain(v.VG.at[seven], v.s_g.at[2])
        drain(v.PB.at[pl.ds(0, 4)], v.s_hs)

    @pl.when(host & (x % 2 == 0))
    def _():
        drain(v.CG.at[0, pl.ds(0, 2)], v.s_hr)

    @pl.when(host & (x == 1))
    def _():
        drain(v.CG.at[0, pl.ds(0, 3)], v.s_hr)

    for a in range(LEV, 2, -1):
        @pl.when((lev + 2 <= a) & ((lev == 2) | (lev == 3)))
        def _(a=a):
            drain(v.RX, v.s_xf.at[a - 1])

        @pl.when((lev == 1) & (a < lev_next))
        def _(a=a):
            drain(v.PB, v.s_xf.at[a - 1])


def body(*args):
    vmem = pl.BlockSpec(memory_space=pltpu.VMEM)
    out = jax.ShapeDtypeStruct((1, 64, 128), F32)
    return pl.pallas_call(
        kernel,
        out_shape=(out, out),
        in_specs=[pl.BlockSpec(memory_space=pl.ANY)] * 6 + [pl.BlockSpec(memory_space=pltpu.SMEM)],
        out_specs=(vmem, vmem),
        scratch_shapes=list(SCRATCH.values()),
        compiler_params=pltpu.CompilerParams(collective_id=0, has_side_effects=True, vmem_limit_bytes=56 * 2**20),
        name="solve",
    )(*args)


def solution(mesh):
    in_specs = (
        P("leaf", "blk", None),
        P("leaf", None, None, "blk"),
        P("leaf", "blk", None),
        P("leaf", None, None, "blk"),
        P("leaf", None, "blk"),
        P("leaf", None, "blk"),
        P("leaf", None),
    )
    out_specs = (P("leaf", None, "blk"), P("leaf", None, "blk"))
    return jax.shard_map(body, mesh=mesh, in_specs=in_specs, out_specs=out_specs, check_vma=False)
```
